32 devices in a mesh: section: 2 (over x), dp: 4 (over z), tensor: 4 (over y, core).
Axes of the slice: x: 2, y: 2, z: 4, core: 2. Of those that a mesh axis runs over, the one named last changes fastest.
Arguments:
- tokens: bfloat16 [4, 8, 256, 1152], P(None, 'dp', 'tensor'), may hold values from -110 to 110
- velocity_grad: bfloat16 [4, 8, 256, 1152], P(None, 'dp', 'tensor'), may hold values from -6 to 6
- bins: int32 [4, 8], P(None, 'dp'), may hold values from 0 to 999
- labels: int32 [4, 8], P(None, 'dp'), may hold values from 0 to 999
- places: int32 [4, 8, 256], P(None, 'dp'), may hold values from 0 to 255, each once within a row
- class_table: bfloat16 [1000, 1152], replicated, may hold values from -6 to 6
- mod_weight: bfloat16 [2, 1152, 6, 1152], P('section', None, None, 'tensor'), may hold values from -0.1875 to 0.1875
- qkv_weight: bfloat16 [2, 3, 1152, 1152], P('section', None, None, 'tensor'), may hold values from -0.1875 to 0.1875
- out_weight: bfloat16 [2, 1152, 1152], P('section', 'tensor'), may hold values from -0.75 to 0.75
- gate_up_weight: bfloat16 [2, 2, 1152, 3072], P('section', None, None, 'tensor'), may hold values from -0.1875 to 0.1875
- down_weight: bfloat16 [2, 3072, 1152], P('section', 'tensor'), may hold values from -0.109375 to 0.109375
- q_gain: bfloat16 [2, 1152], P('section', 'tensor'), may hold values from 1 to 2
- k_gain: bfloat16 [2, 1152], P('section', 'tensor'), may hold values from 1 to 2
Outputs:
- block_outputs: bfloat16 [2, 4, 8, 256, 1152], P('section', None, 'dp', 'tensor')
- input_grads: float32 [2, 4, 8, 256, 1152], P('section', None, 'dp', 'tensor')
- mod_grad: float32 [2, 1152, 6, 1152], P('section', None, None, 'tensor')
- qkv_grad: float32 [2, 3, 1152, 1152], P('section', None, None, 'tensor')
- out_grad: float32 [2, 1152, 1152], P('section', 'tensor')
- gate_up_grad: float32 [2, 2, 1152, 3072], P('section', None, None, 'tensor')
- down_grad: float32 [2, 3072, 1152], P('section', 'tensor')
- q_gain_grad: float32 [2, 1152], P('section', 'tensor')
- k_gain_grad: float32 [2, 1152], P('section', 'tensor')
- class_grad: float32 [1000, 1152], replicated
- stats: float32 [2, 3], P('section')
The draws below stay inside these ranges and needn't reach their ends.
Inputs may be any that keep to these rules, and one draw needn't show every extreme that they name: Each image's row holds each of its 256 patch places once.
All inputs are finite; a program needn't handle non-finite values.
Results may differ from the reference program's by a relative error of at most 0.028.
Values may be sent and summed in bfloat16 or wider, within the bound.
A program may use at most 320 MiB of HBM per device.

```python
import math
import jax
import jax.numpy as jnp
from jax import lax

D = 1152
HEADS = 16
HEAD_DIM = 72
FF = 3072
NCLASS = 1000
NBINS = 1000
GRID = 16
PATCHES = 256
MICRO = 4
IMAGES_MB = 8


def draw_tokens(key, part):
    key = jax.random.fold_in(key, 11)
    value_key, feature_key = jax.random.split(key)
    image_pos = jnp.arange(IMAGES_MB, dtype=jnp.float32)[:, None]
    patch_pos = jnp.arange(PATCHES, dtype=jnp.float32)[None, :]
    placing = (image_pos * PATCHES + patch_pos) / (IMAGES_MB * PATCHES - 1)
    layout = (MICRO, IMAGES_MB, PATCHES, D)
    feature_rank = jax.random.permutation(feature_key, D)
    feature_boost = jnp.where(feature_rank < 8, 6.0, 1.0).astype(jnp.float32)
    values = jnp.clip(jax.random.normal(value_key, layout, jnp.float32), -6.0, 6.0)
    rising = 3.0 ** placing
    return (values * rising[None, :, :, None] * feature_boost[None, None, None, :]).astype(jnp.bfloat16)


def set_ends(values, own_key, least, largest):
    place = [jax.random.randint(jax.random.fold_in(own_key, axis), (), 0, length) for axis, length in enumerate(values.shape)]
    widest = values.shape.index(max(values.shape))
    next_to = place[:widest] + [(place[widest] + 1) % values.shape[widest]] + place[widest + 1:]
    return values.at[tuple(place)].set(least).at[tuple(next_to)].set(largest)


def levels(rng, extent, cuts, low, high):
    gain = 1.0
    for dim, shards_of in cuts:
        heights = jax.random.uniform(jax.random.fold_in(jax.random.fold_in(rng, 6), dim), (shards_of,), jnp.float32, low / len(cuts), high / len(cuts))
        gain = gain * jnp.repeat(jnp.exp(heights), extent[dim] // shards_of).reshape((-1,) + (1,) * (len(extent) - 1 - dim))
    return gain


def centred(own_key, shape, scale, limit, cuts=(), kind=jnp.bfloat16):
    values = scale * jax.random.normal(own_key, shape, jnp.float32)
    if cuts:
        values = values * levels(own_key, shape, cuts, -0.22, 0.18)
    return jnp.clip(values, -limit, limit).astype(kind)


def setup_inputs(seed: int = 0) -> dict:
    arg_keys = jax.random.split(jax.random.key(seed), 14)
    return {
        "tokens": draw_tokens(jax.random.fold_in(arg_keys[13], 71), 0),
        "velocity_grad": centred(arg_keys[1], (MICRO, IMAGES_MB, PATCHES, D), 1.0, 6.0, ((1, 4), (2, 4))),
        "bins": set_ends(jax.random.randint(arg_keys[2], (MICRO, IMAGES_MB), 0, NBINS), jax.random.fold_in(arg_keys[2], 1), 0, NBINS - 1).astype(jnp.int32),
        "labels": set_ends(jax.random.randint(arg_keys[3], (MICRO, IMAGES_MB), 0, NCLASS), jax.random.fold_in(arg_keys[3], 1), 0, NCLASS - 1).astype(jnp.int32),
        "places": jax.vmap(lambda own: jax.random.permutation(own, PATCHES))(jax.random.split(arg_keys[4], MICRO * IMAGES_MB)).reshape((MICRO, IMAGES_MB, PATCHES)).astype(jnp.int32),
        "class_table": centred(arg_keys[5], (NCLASS, D), 1.0, 6.0),
        "mod_weight": centred(arg_keys[6], (2, D, 6, D), D ** -0.5, 0.1875, ((0, 2), (3, 4))),
        "qkv_weight": centred(arg_keys[7], (2, 3, D, D), D ** -0.5, 0.1875, ((0, 2), (3, 4))),
        "out_weight": centred(arg_keys[8], (2, D, D), HEAD_DIM ** -0.5, 0.75, ((0, 2), (1, 4))),
        "gate_up_weight": centred(arg_keys[9], (2, 2, D, FF), D ** -0.5, 0.1875, ((0, 2), (3, 4))),
        "down_weight": centred(arg_keys[10], (2, FF, D), FF ** -0.5, 0.109375, ((0, 2), (1, 4))),
        "q_gain": jnp.clip(jnp.exp(math.log(2.0) - 0.6931472 * jax.random.uniform(arg_keys[11], (2, D), jnp.float32) ** levels(arg_keys[11], (2, D), ((0, 2), (1, 4)), -0.2, 0.2)), 1.0, 2.0).astype(jnp.bfloat16),
        "k_gain": jnp.clip(jnp.exp(math.log(2.0) - 0.6931472 * jax.random.uniform(arg_keys[12], (2, D), jnp.float32) ** levels(arg_keys[12], (2, D), ((0, 2), (1, 4)), -0.2, 0.2)), 1.0, 2.0).astype(jnp.bfloat16),
    }


@jax.custom_vjp
def low(v):
    return lax.optimization_barrier(v.astype(jnp.bfloat16)).astype(jnp.float32)

@jax.custom_vjp
def low_back(v):
    return v

def low_keep(v):
    return (low(v), None)

def low_pass(kept, grad):
    return (grad,)

def back_keep(v):
    return (v, None)

def back_low(kept, grad):
    return (low(grad),)
low.defvjp(low_keep, low_pass)
low_back.defvjp(back_keep, back_low)
epsilon = 1e-06
highest = lax.Precision.HIGHEST

def rms_scale(values):
    return values * lax.rsqrt(lax.optimization_barrier(jnp.mean(values * values, axis=-1, keepdims=True)) + epsilon)

def time_embed(bin_row, feature_count):
    halfway = feature_count // 2
    frequency = jnp.exp(-math.log(10000.0) * jnp.arange(halfway, dtype=jnp.float32) / halfway)
    moment = (bin_row.astype(jnp.float32) + 0.5) * (1000.0 / NBINS)
    angles = moment[:, None] * frequency[None, :]
    return jnp.concatenate([jnp.cos(angles), jnp.sin(angles)], axis=-1)

def rope_tables(place_row):
    quarter = HEAD_DIM // 4
    frequency = 10000.0 ** (-jnp.arange(quarter, dtype=jnp.float32) / quarter)
    row_pos = (place_row // GRID).astype(jnp.float32)
    col_pos = (place_row % GRID).astype(jnp.float32)
    angles = jnp.stack([row_pos[..., None] * frequency, col_pos[..., None] * frequency], axis=-2)
    return (jnp.cos(angles), jnp.sin(angles))

def rotate(values, cosine, sine_table):
    layout = values.shape
    pieces = values.reshape(layout[:-1] + (2, 2, layout[-1] // 4))
    former = pieces[..., 0, :]
    latter = pieces[..., 1, :]
    cos_wide = cosine[:, :, None]
    sin_wide = sine_table[:, :, None]
    turned = jnp.stack([former * cos_wide - latter * sin_wide, latter * cos_wide + former * sin_wide], axis=-2)
    return turned.reshape(layout)

def block(stream, silu_cond, weights, cosine, sine_table):
    mod_weight, qkv_weight, out_weight, gate_up_weight, down_weight, query_gain, key_gain = weights
    modulation = jnp.einsum('id,djf->ijf', low(silu_cond), mod_weight, precision=highest)
    shift_one = modulation[:, 0:1, :]
    scale_one = modulation[:, 1:2, :]
    gate_one = modulation[:, 2:3, :]
    shift_two = modulation[:, 3:4, :]
    scale_two = modulation[:, 4:5, :]
    gate_two = modulation[:, 5:6, :]
    images = stream.shape[0]
    tokens_all = stream.shape[1]
    normed_one = low(rms_scale(stream) * (1.0 + scale_one) + shift_one)
    projected = jnp.einsum('ipd,kde->kipe', normed_one, qkv_weight, precision=highest)
    projected = projected.reshape(3, images, tokens_all, HEADS, HEAD_DIM)
    query_raw = low_back(projected[0])
    key_raw = low_back(projected[1])
    valued = low(low_back(projected[2]))
    query = low(rotate(rms_scale(query_raw) * query_gain.reshape(HEADS, HEAD_DIM), cosine, sine_table))
    keyed = low(rotate(rms_scale(key_raw) * key_gain.reshape(HEADS, HEAD_DIM), cosine, sine_table))
    scores = low_back(jnp.einsum('iphe,iqhe->ihpq', query, keyed, precision=highest) * HEAD_DIM ** (-0.5))
    shifted = scores - lax.optimization_barrier(jnp.max(scores, axis=-1, keepdims=True))
    powered = jnp.exp(shifted)
    attn_probs = low(powered / lax.optimization_barrier(jnp.sum(powered, axis=-1, keepdims=True)))
    mixed_heads = jnp.einsum('ihpq,iqhe->iphe', attn_probs, valued, precision=highest)
    mixed_heads = low(low_back(mixed_heads.reshape(images, tokens_all, HEADS * HEAD_DIM)))
    attended = low_back(jnp.einsum('ipe,ed->ipd', mixed_heads, out_weight, precision=highest))
    middle = stream + gate_one * attended
    normed_two = low(rms_scale(middle) * (1.0 + scale_two) + shift_two)
    gate_up = jnp.einsum('ipd,kdf->kipf', normed_two, gate_up_weight, precision=highest)
    hidden = low(jax.nn.silu(low_back(gate_up[0])) * low_back(gate_up[1]))
    feedfwd = low_back(jnp.einsum('ipf,fd->ipd', hidden, down_weight, precision=highest))
    return (middle, middle + gate_two * feedfwd)

def reference(tokens, velocity_grad, bins, labels, places, class_table, mod_weight, qkv_weight, out_weight, gate_up_weight, down_weight, q_gain, k_gain):

    def forward(tokens_f, table_f, mod_f, qkv_f, out_f, gate_up_f, down_f, query_gain_f, key_gain_f, shifts):
        encoder = (mod_f[0], qkv_f[0], out_f[0], gate_up_f[0], down_f[0], query_gain_f[0], key_gain_f[0])
        decoder = (mod_f[1], qkv_f[1], out_f[1], gate_up_f[1], down_f[1], query_gain_f[1], key_gain_f[1])

        def one_micro(carry, items):
            tok_rows, shift_rows, bin_row, label_row, place_row = items
            silu_cond = jax.nn.silu(time_embed(bin_row, D) + table_f[label_row])
            cosine, sine_table = rope_tables(place_row)
            mid_enc, out_enc = block(tok_rows, silu_cond, encoder, cosine, sine_table)
            latent = low(low_back(out_enc))
            dec_in = latent + shift_rows
            mid_dec, out_dec = block(dec_in, silu_cond, decoder, cosine, sine_table)
            enc_sums = jnp.stack([jnp.sum(tok_rows * tok_rows), jnp.sum(mid_enc * mid_enc), jnp.sum(out_enc * out_enc)])
            dec_sums = jnp.stack([jnp.sum(dec_in * dec_in), jnp.sum(mid_dec * mid_dec), jnp.sum(out_dec * out_dec)])
            return (carry + jnp.stack([enc_sums, dec_sums]), (latent, out_dec))
        totals, outputs = lax.scan(jax.checkpoint(one_micro), jnp.zeros((2, 3), jnp.float32), (tokens_f, shifts, bins, labels, places))
        stats = jnp.sqrt(totals / (MICRO * IMAGES_MB * PATCHES * D))
        return (outputs[0], outputs[1], stats)
    shifts = jnp.zeros(tokens.shape, jnp.float32)
    primal_out, pull_back = jax.vjp(forward, tokens.astype(jnp.float32), class_table.astype(jnp.float32), mod_weight.astype(jnp.float32), qkv_weight.astype(jnp.float32), out_weight.astype(jnp.float32), gate_up_weight.astype(jnp.float32), down_weight.astype(jnp.float32), q_gain.astype(jnp.float32), k_gain.astype(jnp.float32), shifts)
    latents, velocity, stats = primal_out
    grads = pull_back((jnp.zeros_like(latents), velocity_grad.astype(jnp.float32), jnp.zeros_like(stats)))
    block_outputs = jnp.stack([latents, velocity]).astype(jnp.bfloat16)
    input_grads = jnp.stack([grads[0], grads[9]])
    return (block_outputs, input_grads, grads[2], grads[3], grads[4], grads[5], grads[6], grads[7], grads[8], grads[1], stats)
```

```python
import functools
import math

import jax
import jax.numpy as jnp
import numpy as np
from jax import lax
from jax.experimental import pallas as pl
from jax.experimental.pallas import tpu as pltpu
from jax.sharding import PartitionSpec as P

MESH = pl.DeviceIdType.MESH
HEAD_DIM = 72
LANES = 128
NBINS = 1000
GRID = 16
EPS = 1e-06
BF = jnp.bfloat16
F32 = jnp.float32
SCALE = HEAD_DIM**-0.5


def lane_of():
    quarter = HEAD_DIM // 4
    lanes = np.zeros((HEAD_DIM,), np.int64)
    for half in range(2):
        for part in range(2):
            for i in range(quarter):
                lanes[half * 2 * quarter + part * quarter + i] = part * 64 + half * quarter + i
    return lanes


def head_select(heads):
    select = np.zeros((heads * HEAD_DIM, heads * LANES), np.float32)
    lanes = lane_of()
    for h in range(heads):
        for f in range(HEAD_DIM):
            select[h * HEAD_DIM + f, h * LANES + lanes[f]] = 1.0
    return select


def angle_table():
    quarter = HEAD_DIM // 4
    frequency = (10000.0 ** (-np.arange(quarter, dtype=np.float32) / np.float32(quarter))).astype(np.float32)
    lanes = lane_of().reshape(2, 2, quarter)
    table = np.zeros((2 * GRID, 2 * LANES), np.float32)
    for place in range(GRID):
        angle = np.float32(place) * frequency
        for half in range(2):
            for part in range(2):
                sign = -1.0 if part == 0 else 1.0
                table[half * GRID + place, lanes[half, part]] = np.cos(angle)
                table[half * GRID + place, LANES + lanes[half, part]] = sign * np.sin(angle)
    return table


def dot(a, b):
    return lax.dot_general(a, b, (((1,), (0,)), ((), ())), preferred_element_type=F32)


def dot_nt(a, b):
    return lax.dot_general(a, b, (((1,), (1,)), ((), ())), preferred_element_type=F32)


def dot_tn(a, b):
    return lax.dot_general(a, b, (((0,), (0,)), ((), ())), preferred_element_type=F32)


def chunks_of(size, width):
    return [(at, min(width, size - at)) for at in range(0, size, width)]


def main_kernel(
    images,
    heads,
    tok,
    vel,
    mod,
    cosine,
    sine,
    wqkv,
    wout,
    wgu,
    wdn,
    gains,
    zout,
    dxout,
    dmod,
    gacc,
    sacc,
    a1_hbm,
    a2_hbm,
    dffn_hbm,
    dattn_hbm,
    hid_hbm,
    mix_hbm,
    dgu_hbm,
    dqkv_hbm,
    xin,
    din,
    a1f,
    a2f,
    dffn,
    dattn,
    x1s,
    attns,
    ffns,
    keep,
    send_a,
    recv_a,
    send_y,
    recv_y,
    dx1s,
    mix_st,
    hid_st,
    dgu_st,
    dqkv_st,
    ag_sems,
    rs_sems,
    zx_sems,
    out_sems,
    in_sems,
):
    rows = tok.shape[1]
    width = tok.shape[2]
    hidden = wdn.shape[0]
    wide = chunks_of(width, 512)
    section = lax.axis_index("section")
    me = lax.axis_index("tensor")
    sib = me + 1 - 2 * lax.rem(me, 2)
    across = lax.rem(me + 2, 4)
    other = 1 - section
    enc = section == 0
    dec = section == 1

    load_x = pltpu.make_async_copy(tok, xin, in_sems.at[0])
    load_d = pltpu.make_async_copy(vel, din, in_sems.at[1])

    @pl.when(enc)
    def _():
        load_x.start()

    @pl.when(dec)
    def _():
        load_d.start()

    barrier = pltpu.get_barrier_semaphore()
    pl.semaphore_signal(barrier, inc=1, device_id={"tensor": sib}, device_id_type=MESH)
    pl.semaphore_signal(barrier, inc=1, device_id={"tensor": across}, device_id_type=MESH)
    pl.semaphore_signal(barrier, inc=1, device_id={"section": other}, device_id_type=MESH)

    gacc[...] = jnp.zeros_like(gacc)
    sacc[...] = jnp.zeros_like(sacc)
    dmod[...] = jnp.zeros_like(dmod)

    @pl.when(enc)
    def _():
        load_x.wait()

    @pl.when(dec)
    def _():
        load_d.wait()

    pl.semaphore_wait(barrier, 3)

    def remote(src, dst, send_sem, recv_sem, where):
        return pltpu.make_async_remote_copy(
            src_ref=src, dst_ref=dst, send_sem=send_sem, recv_sem=recv_sem, device_id=where, device_id_type=MESH
        )

    def gather(which, buf, n):
        over_y = remote(
            buf.at[n, pl.ds(0, rows)],
            buf.at[n, pl.ds(rows, rows)],
            ag_sems.at[which, 0, n],
            ag_sems.at[which, 1, n],
            {"tensor": across},
        )
        to_sib = remote(
            buf.at[n, pl.ds(0, rows)],
            buf.at[n, pl.ds(2 * rows, rows)],
            ag_sems.at[which, 2, n],
            ag_sems.at[which, 3, n],
            {"tensor": sib},
        )
        relay = remote(
            buf.at[n, pl.ds(rows, rows)],
            buf.at[n, pl.ds(3 * rows, rows)],
            ag_sems.at[which, 4, n],
            ag_sems.at[which, 5, n],
            {"tensor": sib},
        )
        return over_y, to_sib, relay

    def gather_start(which, buf, n):
        over_y, to_sib, relay = gather(which, buf, n)
        over_y.start()
        to_sib.start()

    def gather_relay(which, buf, n):
        over_y, to_sib, relay = gather(which, buf, n)
        over_y.wait_recv()
        relay.start()

    def gather_wait(which, buf, n):
        over_y, to_sib, relay = gather(which, buf, n)
        to_sib.wait_recv()
        relay.wait_recv()

    def gather_drain(which, buf, n):
        over_y, to_sib, relay = gather(which, buf, n)
        over_y.wait_send()
        to_sib.wait_send()
        relay.wait_send()

    def scatter(which, n):
        kind, slot = which % 2, lax.rem(n, 2)
        to_sib = remote(
            send_a.at[kind],
            recv_a.at[kind, slot],
            rs_sems.at[which, 0, n],
            rs_sems.at[which, 1, n],
            {"tensor": sib},
        )
        over_y = remote(
            send_y.at[kind],
            recv_y.at[kind, slot],
            rs_sems.at[which, 2, n],
            rs_sems.at[which, 3, n],
            {"tensor": across},
        )
        return kind, slot, to_sib, over_y

    def scatter_put(which, at, size, values):
        kind = which % 2
        keep[kind, :, pl.ds(at, size)] = values[0 : 2 * rows]
        send_a[kind, :, pl.ds(at, size)] = values[2 * rows : 4 * rows].astype(BF)

    def scatter_start(which, n):
        kind, slot, to_sib, over_y = scatter(which, n)
        to_sib.start()

    def scatter_middle(which, n):
        kind, slot, to_sib, over_y = scatter(which, n)
        to_sib.wait()
        send_y[kind] = (keep[kind, rows : 2 * rows] + recv_a[kind, slot, rows : 2 * rows].astype(F32)).astype(BF)
        over_y.start()

    def scatter_end(which, n):
        kind, slot, to_sib, over_y = scatter(which, n)
        over_y.wait()
        return (
            keep[kind, 0:rows] + recv_a[kind, slot, 0:rows].astype(F32) + recv_y[kind, slot].astype(F32)
        )

    def z_copy(n):
        return remote(zout.at[n], xin.at[n], zx_sems.at[0, n], zx_sems.at[1, n], {"section": other})

    def dz_copy(n):
        return remote(xin.at[n], din.at[n], zx_sems.at[2, n], zx_sems.at[3, n], {"section": other})

    def mod_row(n, row):
        return mod[n, pl.ds(row, 1), :]

    def inverse_rms(values):
        return lax.rsqrt(jnp.mean(values * values, axis=-1, keepdims=True) + EPS)

    def column_sum(values):
        return jnp.sum(values, axis=0, keepdims=True)

    def modulated(values, shift, scale):
        return (values * inverse_rms(values)) * (1.0 + scale) + shift

    def norm_back(values, grad, scale):
        inv = inverse_rms(values)
        normed = values * inv
        d_normed = grad * (1.0 + scale)
        d_values = inv * (d_normed - normed * jnp.mean(d_normed * normed, axis=-1, keepdims=True))
        return d_values, column_sum(grad), column_sum(grad * normed)

    def head_norm(raw):
        inv = lax.rsqrt(jnp.sum(raw * raw, axis=-1, keepdims=True) * (1.0 / HEAD_DIM) + EPS)
        return inv, raw * inv

    def turn(values, c, s):
        return values * c + pltpu.roll(values, 64, 1) * s

    def turn_back(values, c, s):
        return values * c - pltpu.roll(values, 64, 1) * s

    def softmax(scores):
        powered = jnp.exp(scores - jnp.max(scores, axis=-1, keepdims=True))
        return powered * (1.0 / jnp.sum(powered, axis=-1, keepdims=True))

    def out_copy(which, n):
        src, dst = (
            (a1f.at[n], a1_hbm.at[n]),
            (a2f.at[n], a2_hbm.at[n]),
            (dffn.at[n], dffn_hbm.at[n]),
            (dattn.at[n], dattn_hbm.at[n]),
            (hid_st, hid_hbm.at[n]),
            (mix_st, mix_hbm.at[n]),
            (dgu_st, dgu_hbm.at[n]),
            (dqkv_st, dqkv_hbm.at[n]),
        )[which]
        return pltpu.make_async_copy(src, dst, out_sems.at[which, n])

    def staged_ready(which, n):
        @pl.when(n > 0)
        def _():
            out_copy(which, n - 1).wait()

    def attn_in(n):
        @pl.when(dec)
        def _():
            z_copy(n).wait_recv()

        values = xin[n].astype(F32)
        sacc[0:1, :] += column_sum(values * values)
        a1f[n, 0:rows, :] = modulated(values, mod_row(n, 0), mod_row(n, 1)).astype(BF)
        gather_start(0, a1f, n)

    def attn_compute(n):
        gather_wait(0, a1f, n)
        staged_ready(5, n)
        a1 = a1f[n]
        c, s = cosine[n], sine[n]
        for pair in range(heads // 2):
            span = pl.ds(pair * 2 * LANES, 2 * LANES)
            q2 = dot(a1, wqkv[0, :, span])
            k2 = dot(a1, wqkv[1, :, span])
            v2 = dot(a1, wqkv[2, :, span]).astype(BF)
            for half in range(2):
                at = (pair * 2 + half) * LANES
                cut = slice(half * LANES, (half + 1) * LANES)
                q = turn(head_norm(q2[:, cut])[1] * gains[0:1, at : at + LANES], c, s).astype(BF)
                k = turn(head_norm(k2[:, cut])[1] * gains[1:2, at : at + LANES], c, s).astype(BF)
                probs = softmax(dot_nt(q, k) * SCALE).astype(BF)
                mix_st[:, at : at + LANES] = dot(probs, v2[:, cut]).astype(BF)
        mixed = mix_st[...]
        for at, size in wide:
            scatter_put(0, at, size, dot(mixed, wout[:, pl.ds(at, size)]))
        scatter_start(0, n)
        out_copy(5, n).start()
        out_copy(0, n).start()
        gather_drain(0, a1f, n)

    def ffn_in(n):
        attended = scatter_end(0, n)
        attns[n] = attended.astype(BF)
        values = xin[n].astype(F32) + mod_row(n, 2) * attended
        x1s[n] = values
        sacc[1:2, :] += column_sum(values * values)
        a2f[n, 0:rows, :] = modulated(values, mod_row(n, 3), mod_row(n, 4)).astype(BF)
        gather_start(1, a2f, n)

    def ffn_compute(n):
        gather_wait(1, a2f, n)
        a2 = a2f[n]
        for at, size in chunks_of(hidden, 256):
            span = pl.ds(at, size)
            gate_val = dot(a2, wgu[0, :, span])
            up_val = dot(a2, wgu[1, :, span])
            hid_st[:, span] = (gate_val * jax.nn.sigmoid(gate_val) * up_val).astype(BF)
        units = hid_st[...]
        for at, size in wide:
            scatter_put(1, at, size, dot(units, wdn[:, pl.ds(at, size)]))
        scatter_start(1, n)
        out_copy(1, n).start()
        gather_drain(1, a2f, n)

    def block_out(n):
        feedfwd = scatter_end(1, n)
        ffns[n] = feedfwd.astype(BF)
        values = x1s[n] + mod_row(n, 5) * feedfwd
        sacc[2:3, :] += column_sum(values * values)
        zout[n] = values.astype(BF)

        @pl.when(enc)
        def _():
            z_copy(n).start()

    def ffn_grad_in(n):
        @pl.when(enc)
        def _():
            dz_copy(n).wait_recv()

        grad = din[n].astype(F32)
        dffn[n, 0:rows, :] = (mod_row(n, 5) * grad).astype(BF)
        gather_start(2, dffn, n)
        dmod[n, 5:6, :] = column_sum(grad * ffns[n].astype(F32))

    def ffn_grad_compute(n):
        gather_wait(2, dffn, n)
        staged_ready(4, n)
        staged_ready(6, n)
        grad = dffn[n]
        a2 = a2f[n]
        for at, size in chunks_of(hidden, 256):
            span = pl.ds(at, size)
            gate_val = dot(a2, wgu[0, :, span])
            up_val = dot(a2, wgu[1, :, span])
            d_hidden = dot_nt(grad, wdn[span, :])
            sig = jax.nn.sigmoid(gate_val)
            act = gate_val * sig
            hid_st[:, span] = (act * up_val).astype(BF)
            dgu_st[:, span] = (d_hidden * up_val * (sig + act * (1.0 - sig))).astype(BF)
            dgu_st[:, pl.ds(hidden + at, size)] = (d_hidden * act).astype(BF)
        d_gate = dgu_st[:, 0:hidden]
        d_up = dgu_st[:, hidden : 2 * hidden]
        for at, size in wide:
            span = pl.ds(at, size)
            scatter_put(2, at, size, dot_nt(d_gate, wgu[0, span, :]) + dot_nt(d_up, wgu[1, span, :]))
        scatter_start(2, n)
        out_copy(4, n).start()
        out_copy(6, n).start()
        out_copy(2, n).start()
        gather_drain(2, dffn, n)

    def attn_grad_in(n):
        d_a2 = scatter_end(2, n)
        grad, d_shift, d_scale = norm_back(x1s[n], d_a2, mod_row(n, 4))
        grad = grad + din[n].astype(F32)
        dx1s[lax.rem(n, 2)] = grad
        dattn[n, 0:rows, :] = (mod_row(n, 2) * grad).astype(BF)
        gather_start(3, dattn, n)
        dmod[n, 2:3, :] = column_sum(grad * attns[n].astype(F32))
        dmod[n, 3:4, :] = d_shift
        dmod[n, 4:5, :] = d_scale

    def attn_grad_compute(n):
        gather_wait(3, dattn, n)
        staged_ready(7, n)
        grad = dattn[n]
        a1 = a1f[n]
        c, s = cosine[n], sine[n]
        lanes_all = heads * LANES
        for pair in range(heads // 2):
            span = pl.ds(pair * 2 * LANES, 2 * LANES)
            q2 = dot(a1, wqkv[0, :, span])
            k2 = dot(a1, wqkv[1, :, span])
            v2 = dot(a1, wqkv[2, :, span]).astype(BF)
            d_mix2 = dot_nt(grad, wout[span, :]).astype(BF)
            for half in range(2):
                at = (pair * 2 + half) * LANES
                cut = slice(half * LANES, (half + 1) * LANES)
                q_gain, k_gain = gains[0:1, at : at + LANES], gains[1:2, at : at + LANES]
                q_inv, q_norm = head_norm(q2[:, cut])
                k_inv, k_norm = head_norm(k2[:, cut])
                q = turn(q_norm * q_gain, c, s).astype(BF)
                k = turn(k_norm * k_gain, c, s).astype(BF)
                v, d_mix = v2[:, cut], d_mix2[:, cut]
                probs = softmax(dot_nt(q, k) * SCALE)
                d_probs = dot_nt(d_mix, v)
                d_v = dot_tn(probs.astype(BF), d_mix)
                d_scores = (probs * (d_probs - jnp.sum(probs * d_probs, axis=-1, keepdims=True))).astype(BF)
                d_q = turn_back(dot(d_scores, k) * SCALE, c, s)
                d_k = turn_back(dot_tn(d_scores, q) * SCALE, c, s)
                gacc[0:1, at : at + LANES] += column_sum(d_q * q_norm)
                gacc[1:2, at : at + LANES] += column_sum(d_k * k_norm)
                d_q = d_q * q_gain
                d_k = d_k * k_gain
                d_q = q_inv * (d_q - q_norm * (jnp.sum(d_q * q_norm, axis=-1, keepdims=True) * (1.0 / HEAD_DIM)))
                d_k = k_inv * (d_k - k_norm * (jnp.sum(d_k * k_norm, axis=-1, keepdims=True) * (1.0 / HEAD_DIM)))
                dqkv_st[:, at : at + LANES] = d_q.astype(BF)
                dqkv_st[:, lanes_all + at : lanes_all + at + LANES] = d_k.astype(BF)
                dqkv_st[:, 2 * lanes_all + at : 2 * lanes_all + at + LANES] = d_v.astype(BF)
        for at, size in wide:
            span = pl.ds(at, size)
            total = dot_nt(dqkv_st[:, 0:lanes_all], wqkv[0, span, :])
            total += dot_nt(dqkv_st[:, lanes_all : 2 * lanes_all], wqkv[1, span, :])
            total += dot_nt(dqkv_st[:, 2 * lanes_all : 3 * lanes_all], wqkv[2, span, :])
            scatter_put(3, at, size, total)
        scatter_start(3, n)
        out_copy(7, n).start()
        out_copy(3, n).start()
        gather_drain(3, dattn, n)

    def block_grad_out(n):
        d_a1 = scatter_end(3, n)
        grad, d_shift, d_scale = norm_back(xin[n].astype(F32), d_a1, mod_row(n, 1))
        grad = grad + dx1s[lax.rem(n, 2)]
        dxout[n] = grad
        dmod[n, 0:1, :] = d_shift
        dmod[n, 1:2, :] = d_scale

        @pl.when(dec)
        def _():
            xin[n] = grad.astype(BF)
            dz_copy(n).start()

    def stage(n, body):
        @pl.when((n >= 0) & (n < images))
        def _():
            body(n)

    def forward_step(step, carry):
        j = step - 1
        stage(j, attn_compute)
        stage(j - 1, lambda n: gather_relay(1, a2f, n))
        stage(j - 2, block_out)
        stage(j, lambda n: scatter_middle(0, n))
        stage(j + 1, attn_in)
        stage(j - 1, ffn_compute)
        stage(j + 1, lambda n: gather_relay(0, a1f, n))
        stage(j, ffn_in)
        stage(j - 1, lambda n: scatter_middle(1, n))
        return carry

    lax.fori_loop(0, images + 3, forward_step, 0)

    def backward_step(step, carry):
        j = step - 1
        stage(j, ffn_grad_compute)
        stage(j - 1, lambda n: gather_relay(3, dattn, n))
        stage(j - 2, block_grad_out)
        stage(j, lambda n: scatter_middle(2, n))
        stage(j + 1, ffn_grad_in)
        stage(j - 1, attn_grad_compute)
        stage(j + 1, lambda n: gather_relay(2, dffn, n))
        stage(j, attn_grad_in)
        stage(j - 1, lambda n: scatter_middle(3, n))
        return carry

    lax.fori_loop(0, images + 3, backward_step, 0)

    for which in (4, 5, 6, 7):
        out_copy(which, images - 1).wait()

    def drain(n, carry):
        for which in (0, 1, 2, 3):
            out_copy(which, n).wait()

        @pl.when(enc)
        def _():
            z_copy(n).wait_send()

        @pl.when(dec)
        def _():
            dz_copy(n).wait_send()

        return carry

    lax.fori_loop(0, images, drain, 0)


def run_main(tok, vel, mod, cosine, sine, wqkv, wout, wgu, wdn, gains):
    images, rows, width = tok.shape
    tokens = 4 * rows
    lanes_all = wout.shape[0]
    heads = lanes_all // LANES
    hidden = wdn.shape[0]
    vmem = pl.BlockSpec(memory_space=pltpu.VMEM)
    anywhere = pl.BlockSpec(memory_space=pl.ANY)

    def hbm(last):
        return jax.ShapeDtypeStruct((images, tokens, last), BF)

    out_shape = (
        jax.ShapeDtypeStruct((images, rows, width), BF),
        jax.ShapeDtypeStruct((images, rows, width), F32),
        jax.ShapeDtypeStruct((images, 8, width), F32),
        jax.ShapeDtypeStruct((8, lanes_all), F32),
        jax.ShapeDtypeStruct((8, width), F32),
        hbm(width),
        hbm(width),
        hbm(width),
        hbm(width),
        hbm(hidden),
        hbm(lanes_all),
        hbm(2 * hidden),
        hbm(3 * lanes_all),
    )
    scratch = [
        pltpu.VMEM((images, rows, width), BF),
        pltpu.VMEM((images, rows, width), BF),
        pltpu.VMEM((images, tokens, width), BF),
        pltpu.VMEM((images, tokens, width), BF),
        pltpu.VMEM((images, tokens, width), BF),
        pltpu.VMEM((images, tokens, width), BF),
        pltpu.VMEM((images, rows, width), F32),
        pltpu.VMEM((images, rows, width), BF),
        pltpu.VMEM((images, rows, width), BF),
        pltpu.VMEM((2, 2 * rows, width), F32),
        pltpu.VMEM((2, 2 * rows, width), BF),
        pltpu.VMEM((2, 2, 2 * rows, width), BF),
        pltpu.VMEM((2, rows, width), BF),
        pltpu.VMEM((2, 2, rows, width), BF),
        pltpu.VMEM((2, rows, width), F32),
        pltpu.VMEM((tokens, lanes_all), BF),
        pltpu.VMEM((tokens, hidden), BF),
        pltpu.VMEM((tokens, 2 * hidden), BF),
        pltpu.VMEM((tokens, 3 * lanes_all), BF),
        pltpu.SemaphoreType.DMA((4, 6, images)),
        pltpu.SemaphoreType.DMA((4, 4, images)),
        pltpu.SemaphoreType.DMA((4, images)),
        pltpu.SemaphoreType.DMA((8, images)),
        pltpu.SemaphoreType.DMA((2,)),
    ]
    return pl.pallas_call(
        functools.partial(main_kernel, images, heads),
        out_shape=out_shape,
        in_specs=[anywhere, anywhere] + [vmem] * 8,
        out_specs=[vmem] * 5 + [anywhere] * 8,
        scratch_shapes=scratch,
        compiler_params=pltpu.CompilerParams(
            collective_id=0, has_side_effects=True, vmem_limit_bytes=62 * 2**20
        ),
    )(tok, vel, mod, cosine, sine, wqkv, wout, wgu, wdn, gains)


def time_embed(bin_row, feature_count):
    halfway = feature_count // 2
    frequency = jnp.exp(-math.log(10000.0) * jnp.arange(halfway, dtype=F32) / halfway)
    moment = (bin_row.astype(F32) + 0.5) * (1000.0 / NBINS)
    angles = moment[:, None] * frequency[None, :]
    return jnp.concatenate([jnp.cos(angles), jnp.sin(angles)], axis=-1)


def per_device(
    tokens,
    velocity_grad,
    bins,
    labels,
    places,
    class_table,
    mod_weight,
    qkv_weight,
    out_weight,
    gate_up_weight,
    down_weight,
    q_gain,
    k_gain,
):
    micro, per_micro, rows, width = tokens.shape
    images = micro * per_micro
    dp = lax.axis_size("dp")
    me = lax.axis_index("tensor")
    heads = q_gain.shape[1] // HEAD_DIM
    select = jnp.asarray(head_select(heads), BF)

    bins_all = lax.all_gather(bins.reshape(images), "dp", axis=0, tiled=True)
    labels_all = lax.all_gather(labels.reshape(images), "dp", axis=0, tiled=True)
    one_hot = labels_all[:, None] == jnp.arange(class_table.shape[0], dtype=jnp.int32)[None, :]
    cond_all = time_embed(bins_all, width) + jnp.dot(one_hot.astype(BF), class_table, preferred_element_type=F32)
    silu_all = jax.nn.silu(cond_all).astype(BF)
    first = lax.axis_index("dp") * images
    cond = lax.dynamic_slice_in_dim(cond_all, first, images, 0)
    silu_low = lax.dynamic_slice_in_dim(silu_all, first, images, 0)
    mod_w = mod_weight[0]
    columns = jnp.einsum("id,djf->ijf", silu_low, mod_w, preferred_element_type=F32)
    modulation = lax.all_gather(columns, "tensor", axis=2, tiled=True)

    order = jnp.stack([me, (me + 2) % 4, me + 1 - 2 * (me % 2), (me + 2) % 4 + 1 - 2 * (me % 2)])
    placed = jnp.take(places.reshape(images, 4, rows), order, axis=1).reshape(images * 4 * rows)
    grid = jnp.arange(GRID, dtype=jnp.int32)[None, :]
    marks = jnp.concatenate([placed[:, None] // GRID == grid, placed[:, None] % GRID == grid], axis=1).astype(F32)
    angles = jnp.dot(marks, jnp.asarray(angle_table()), precision=lax.Precision.HIGHEST)
    angles = angles.reshape(images, 4 * rows, 2 * LANES)

    wqkv = jnp.einsum("jde,ef->jdf", qkv_weight[0], select, preferred_element_type=F32).astype(BF)
    wout = jnp.einsum("ef,ed->fd", select, out_weight[0], preferred_element_type=F32).astype(BF)
    gains = jnp.dot(jnp.concatenate([q_gain, k_gain], axis=0), select, preferred_element_type=F32)

    results = run_main(
        tokens.reshape(images, rows, width),
        velocity_grad.reshape(images, rows, width),
        modulation,
        angles[..., :LANES],
        angles[..., LANES:],
        wqkv,
        wout,
        gate_up_weight[0],
        down_weight[0],
        gains,
    )
    z_rows, dx_rows, dmod, gain_sums, squares, a1, a2, d_ffn, d_attn, units, mixed, d_gu, d_qkv = results

    def weight_grad(left, right):
        return jnp.einsum("ntd,ntf->df", left, right, preferred_element_type=F32).astype(BF)

    hidden = units.shape[2]
    lanes_all = heads * LANES
    g_gate = weight_grad(a2, d_gu[..., :hidden])
    g_up = weight_grad(a2, d_gu[..., hidden:])
    g_down = weight_grad(units, d_ffn)
    g_qkv = weight_grad(a1, d_qkv).reshape(width, 3, lanes_all)
    g_qkv = jnp.einsum("djf,ef->jde", g_qkv, select, preferred_element_type=F32).astype(BF)
    g_out = jnp.einsum("ef,fd->ed", select, weight_grad(mixed, d_attn), preferred_element_type=F32).astype(BF)
    g_gains = jnp.einsum("jf,ef->je", gain_sums[0:2], select.astype(F32), precision=lax.Precision.HIGHEST)
    summed = lax.psum((jnp.stack([g_gate, g_up]), g_down, g_qkv, g_out), "dp")
    gains_sum = lax.psum(g_gains, "dp")
    gate_up_grad, down_grad, qkv_grad, out_grad = [item.astype(F32)[None] for item in summed]

    dmod_low = lax.psum_scatter(dmod[:, 0:6].astype(BF), "tensor", scatter_dimension=2, tiled=True)
    dmod_all = lax.all_gather(dmod_low, "dp", axis=0, tiled=True)
    mod_grad = jnp.einsum("id,ijf->djf", silu_all, dmod_all, preferred_element_type=F32)[None]
    grad_silu = jnp.einsum("ijf,djf->id", dmod_low, mod_w, preferred_element_type=F32)
    sig = jax.nn.sigmoid(cond)
    grad_cond = grad_silu * (sig + cond * sig * (1.0 - sig))
    spread = lax.dynamic_update_slice_in_dim(jnp.zeros((dp * images, width), F32), grad_cond, first, 0)
    spread = lax.psum(spread, ("section", "dp", "tensor"))
    class_grad = jnp.dot(one_hot.astype(F32).T, spread, precision=lax.Precision.HIGHEST)

    square_totals = lax.psum(jnp.sum(squares[0:3], axis=1), ("dp", "tensor"))
    count = images * rows * width * dp * lax.axis_size("tensor")
    stats = jnp.sqrt(square_totals / count)[None, :]
    whole = (1, micro, per_micro, rows, width)
    return (
        z_rows.reshape(whole),
        dx_rows.reshape(whole),
        mod_grad,
        qkv_grad,
        out_grad,
        gate_up_grad,
        down_grad,
        gains_sum[0:1],
        gains_sum[1:2],
        class_grad,
        stats,
    )


def solution(mesh):
    return jax.shard_map(
        per_device,
        mesh=mesh,
        in_specs=(
            P(None, "dp", "tensor", None),
            P(None, "dp", "tensor", None),
            P(None, "dp"),
            P(None, "dp"),
            P(None, "dp", None),
            P(),
            P("section", None, None, "tensor"),
            P("section", None, None, "tensor"),
            P("section", "tensor", None),
            P("section", None, None, "tensor"),
            P("section", "tensor", None),
            P("section", "tensor"),
            P("section", "tensor"),
        ),
        out_specs=(
            P("section", None, "dp", "tensor", None),
            P("section", None, "dp", "tensor", None),
            P("section", None, None, "tensor"),
            P("section", None, None, "tensor"),
            P("section", "tensor", None),
            P("section", None, None, "tensor"),
            P("section", "tensor", None),
            P("section", "tensor"),
            P("section", "tensor"),
            P(),
            P("section", None),
        ),
        check_vma=False,
    )
```

```python
import functools
import math

import jax
import jax.numpy as jnp
import numpy as np
from jax import lax
from jax.experimental import pallas as pl
from jax.experimental.pallas import tpu as pltpu
from jax.sharding import PartitionSpec as P

MESH = pl.DeviceIdType.MESH
HEAD_DIM = 72
LANES = 128
NBINS = 1000
GRID = 16
EPS = 1e-06
BF = jnp.bfloat16
F32 = jnp.float32
SCALE = HEAD_DIM**-0.5


def lane_of():
    quarter = HEAD_DIM // 4
    lanes = np.zeros((HEAD_DIM,), np.int64)
    for half in range(2):
        for part in range(2):
            for i in range(quarter):
                lanes[half * 2 * quarter + part * quarter + i] = part * 64 + half * quarter + i
    return lanes


def head_select(heads):
    select = np.zeros((heads * HEAD_DIM, heads * LANES), np.float32)
    lanes = lane_of()
    for h in range(heads):
        for f in range(HEAD_DIM):
            select[h * HEAD_DIM + f, h * LANES + lanes[f]] = 1.0
    return select


def angle_table():
    quarter = HEAD_DIM // 4
    frequency = (10000.0 ** (-np.arange(quarter, dtype=np.float32) / np.float32(quarter))).astype(np.float32)
    lanes = lane_of().reshape(2, 2, quarter)
    table = np.zeros((2 * GRID, 2 * LANES), np.float32)
    for place in range(GRID):
        angle = np.float32(place) * frequency
        for half in range(2):
            for part in range(2):
                sign = -1.0 if part == 0 else 1.0
                table[half * GRID + place, lanes[half, part]] = np.cos(angle)
                table[half * GRID + place, LANES + lanes[half, part]] = sign * np.sin(angle)
    return table


def dot(a, b):
    return lax.dot_general(a, b, (((1,), (0,)), ((), ())), preferred_element_type=F32)


def dot_nt(a, b):
    return lax.dot_general(a, b, (((1,), (1,)), ((), ())), preferred_element_type=F32)


def dot_tn(a, b):
    return lax.dot_general(a, b, (((0,), (0,)), ((), ())), preferred_element_type=F32)


def chunks_of(size, width):
    return [(at, min(width, size - at)) for at in range(0, size, width)]


def main_kernel(
    images,
    heads,
    tok,
    vel,
    mod_cols,
    cosine,
    sine,
    wqkv,
    wout,
    wgu,
    wdn,
    gains,
    zout,
    dxout,
    dmod_part,
    gacc,
    sacc,
    a1_hbm,
    a2_hbm,
    dffn_hbm,
    dattn_hbm,
    hid_hbm,
    mix_hbm,
    dgu_hbm,
    dqkv_hbm,
    xin,
    din,
    a1f,
    a2f,
    dffn,
    dattn,
    x1s,
    attns,
    ffns,
    keep,
    send_a,
    recv_a,
    send_y,
    recv_y,
    dx1s,
    mix_st,
    hid_st,
    dgu_st,
    dqkv_st,
    mod,
    mod_recv,
    dmod,
    dmod_recv,
    mod_sems,
    dmod_sems,
    ag_sems,
    rs_sems,
    zx_sems,
    out_sems,
    in_sems,
):
    rows = tok.shape[1]
    width = tok.shape[2]
    hidden = wdn.shape[0]
    wide = chunks_of(width, 512)
    section = lax.axis_index("section")
    me = lax.axis_index("tensor")
    sib = me + 1 - 2 * lax.rem(me, 2)
    across = lax.rem(me + 2, 4)
    diag = lax.rem(sib + 2, 4)
    peers = (sib, across, diag)
    other = 1 - section
    enc = section == 0
    dec = section == 1

    load_x = pltpu.make_async_copy(tok, xin, in_sems.at[0])
    load_d = pltpu.make_async_copy(vel, din, in_sems.at[1])

    @pl.when(enc)
    def _():
        load_x.start()

    @pl.when(dec)
    def _():
        load_d.start()

    barrier = pltpu.get_barrier_semaphore()
    pl.semaphore_signal(barrier, inc=1, device_id={"tensor": sib}, device_id_type=MESH)
    pl.semaphore_signal(barrier, inc=1, device_id={"tensor": across}, device_id_type=MESH)
    pl.semaphore_signal(barrier, inc=1, device_id={"tensor": diag}, device_id_type=MESH)
    pl.semaphore_signal(barrier, inc=1, device_id={"section": other}, device_id_type=MESH)

    mod[...] = jnp.zeros_like(mod)
    gacc[...] = jnp.zeros_like(gacc)
    sacc[...] = jnp.zeros_like(sacc)
    dmod[...] = jnp.zeros_like(dmod)

    pl.semaphore_wait(barrier, 4)

    def remote(src, dst, send_sem, recv_sem, where):
        return pltpu.make_async_remote_copy(
            src_ref=src, dst_ref=dst, send_sem=send_sem, recv_sem=recv_sem, device_id=where, device_id_type=MESH
        )

    def its_tiles(device):
        return pl.ds(pl.multiple_of(device * (2 * LANES), LANES), 3 * LANES)

    def mod_copy(k):
        return remote(mod_cols, mod_recv.at[k], mod_sems.at[0, k], mod_sems.at[1, k], {"tensor": peers[k]})

    def dmod_copy(k, n):
        return remote(
            dmod.at[n, :, its_tiles(peers[k])],
            dmod_recv.at[k, n],
            dmod_sems.at[0, k, n],
            dmod_sems.at[1, k, n],
            {"tensor": peers[k]},
        )

    for k in (1, 2, 0):
        mod_copy(k).start()
    mod[:, :, its_tiles(me)] = mod_cols[...]

    @pl.when(enc)
    def _():
        load_x.wait()

    @pl.when(dec)
    def _():
        load_d.wait()

    for k in range(3):
        mod_copy(k).wait()
        mod[:, :, its_tiles(peers[k])] += mod_recv[k]

    def gather(which, buf, n, kind):
        src, dst, where = ((0, rows, across), (0, 2 * rows, sib), (rows, 3 * rows, sib))[kind]
        return remote(
            buf.at[n, pl.ds(src, rows)],
            buf.at[n, pl.ds(dst, rows)],
            ag_sems.at[which, 2 * kind, n],
            ag_sems.at[which, 2 * kind + 1, n],
            {"tensor": where},
        )

    def gather_start(which, buf, n):
        gather(which, buf, n, 0).start()
        gather(which, buf, n, 1).start()

    def gather_relay(which, buf, n):
        gather(which, buf, n, 0).wait_recv()
        gather(which, buf, n, 2).start()

    def gather_wait(which, buf, n):
        gather(which, buf, n, 1).wait_recv()
        gather(which, buf, n, 2).wait_recv()

    def gather_drain(which, buf, n):
        for kind in range(3):
            gather(which, buf, n, kind).wait_send()

    def to_sibling(which, n):
        kind = which % 2
        return remote(
            send_a.at[kind],
            recv_a.at[kind, lax.rem(n, 2)],
            rs_sems.at[which, 0, n],
            rs_sems.at[which, 1, n],
            {"tensor": sib},
        )

    def over_y(which, n):
        kind = which % 2
        return remote(
            send_y.at[kind],
            recv_y.at[kind, lax.rem(n, 2)],
            rs_sems.at[which, 2, n],
            rs_sems.at[which, 3, n],
            {"tensor": across},
        )

    def scatter_put(which, at, size, values):
        kind = which % 2
        keep[kind, :, pl.ds(at, size)] = values[0 : 2 * rows]
        send_a[kind, :, pl.ds(at, size)] = values[2 * rows : 4 * rows].astype(BF)

    def scatter_start(which, n):
        to_sibling(which, n).start()

    def scatter_middle(which, n):
        kind, slot = which % 2, lax.rem(n, 2)
        to_sibling(which, n).wait()
        send_y[kind] = (keep[kind, rows : 2 * rows] + recv_a[kind, slot, rows : 2 * rows].astype(F32)).astype(BF)
        over_y(which, n).start()

    def scatter_end(which, n):
        kind, slot = which % 2, lax.rem(n, 2)
        over_y(which, n).wait()
        return keep[kind, 0:rows] + recv_a[kind, slot, 0:rows].astype(F32) + recv_y[kind, slot].astype(F32)

    def z_copy(n):
        return remote(zout.at[n], xin.at[n], zx_sems.at[0, n], zx_sems.at[1, n], {"section": other})

    def dz_copy(n):
        return remote(xin.at[n], din.at[n], zx_sems.at[2, n], zx_sems.at[3, n], {"section": other})

    def mod_row(n, row):
        return mod[n, pl.ds(row, 1), :]

    def inverse_rms(values):
        return lax.rsqrt(jnp.mean(values * values, axis=-1, keepdims=True) + EPS)

    def column_sum(values):
        return jnp.sum(values, axis=0, keepdims=True)

    def modulated(values, shift, scale):
        return (values * inverse_rms(values)) * (1.0 + scale) + shift

    def norm_back(values, grad, scale):
        inv = inverse_rms(values)
        normed = values * inv
        d_normed = grad * (1.0 + scale)
        d_values = inv * (d_normed - normed * jnp.mean(d_normed * normed, axis=-1, keepdims=True))
        return d_values, column_sum(grad), column_sum(grad * normed)

    def head_norm(raw):
        inv = lax.rsqrt(jnp.sum(raw * raw, axis=-1, keepdims=True) * (1.0 / HEAD_DIM) + EPS)
        return inv, raw * inv

    def turn(values, c, s):
        return values * c + pltpu.roll(values, 64, 1) * s

    def turn_back(values, c, s):
        return values * c - pltpu.roll(values, 64, 1) * s

    def softmax(scores):
        powered = jnp.exp(scores - jnp.max(scores, axis=-1, keepdims=True))
        return powered * (1.0 / jnp.sum(powered, axis=-1, keepdims=True))

    def out_copy(which, n):
        src = (a1f, a2f, dffn, dattn, hid_st, mix_st, dgu_st, dqkv_st)[which]
        dst = (a1_hbm, a2_hbm, dffn_hbm, dattn_hbm, hid_hbm, mix_hbm, dgu_hbm, dqkv_hbm)[which]
        return pltpu.make_async_copy(src.at[n] if which < 4 else src, dst.at[n], out_sems.at[which, n])

    def staged_ready(which, n):
        @pl.when(n > 0)
        def _():
            out_copy(which, n - 1).wait()

    def attn_in(n):
        @pl.when(dec)
        def _():
            z_copy(n).wait_recv()

        values = xin[n].astype(F32)
        sacc[0:1, :] += column_sum(values * values)
        a1f[n, 0:rows, :] = modulated(values, mod_row(n, 0), mod_row(n, 1)).astype(BF)
        gather_start(0, a1f, n)

    def attn_compute(n):
        gather_wait(0, a1f, n)
        staged_ready(5, n)
        a1 = a1f[n]
        c, s = cosine[n], sine[n]
        for pair in range(heads // 2):
            span = pl.ds(pair * 2 * LANES, 2 * LANES)
            q2 = dot(a1, wqkv[0, :, span])
            k2 = dot(a1, wqkv[1, :, span])
            v2 = dot(a1, wqkv[2, :, span]).astype(BF)
            for half in range(2):
                at = (pair * 2 + half) * LANES
                cut = slice(half * LANES, (half + 1) * LANES)
                q = turn(head_norm(q2[:, cut])[1] * gains[0:1, at : at + LANES], c, s).astype(BF)
                k = turn(head_norm(k2[:, cut])[1] * gains[1:2, at : at + LANES], c, s).astype(BF)
                probs = softmax(dot_nt(q, k) * SCALE).astype(BF)
                mix_st[:, at : at + LANES] = dot(probs, v2[:, cut]).astype(BF)
        mixed = mix_st[...]
        for at, size in wide:
            scatter_put(0, at, size, dot(mixed, wout[:, pl.ds(at, size)]))
        scatter_start(0, n)
        out_copy(5, n).start()
        out_copy(0, n).start()
        gather_drain(0, a1f, n)

    def ffn_in(n):
        attended = scatter_end(0, n)
        attns[n] = attended.astype(BF)
        values = xin[n].astype(F32) + mod_row(n, 2) * attended
        x1s[n] = values
        sacc[1:2, :] += column_sum(values * values)
        a2f[n, 0:rows, :] = modulated(values, mod_row(n, 3), mod_row(n, 4)).astype(BF)
        gather_start(1, a2f, n)

    def ffn_compute(n):
        gather_wait(1, a2f, n)
        a2 = a2f[n]
        for at, size in chunks_of(hidden, 256):
            span = pl.ds(at, size)
            gate_val = dot(a2, wgu[0, :, span])
            up_val = dot(a2, wgu[1, :, span])
            hid_st[:, span] = (gate_val * jax.nn.sigmoid(gate_val) * up_val).astype(BF)
        units = hid_st[...]
        for at, size in wide:
            scatter_put(1, at, size, dot(units, wdn[:, pl.ds(at, size)]))
        scatter_start(1, n)
        out_copy(1, n).start()
        gather_drain(1, a2f, n)

    def block_out(n):
        feedfwd = scatter_end(1, n)
        ffns[n] = feedfwd.astype(BF)
        values = x1s[n] + mod_row(n, 5) * feedfwd
        sacc[2:3, :] += column_sum(values * values)
        zout[n] = values.astype(BF)

        @pl.when(enc)
        def _():
            z_copy(n).start()

    def ffn_grad_in(n):
        @pl.when(enc)
        def _():
            dz_copy(n).wait_recv()

        grad = din[n].astype(F32)
        dffn[n, 0:rows, :] = (mod_row(n, 5) * grad).astype(BF)
        gather_start(2, dffn, n)
        dmod[n, 5:6, :] = column_sum(grad * ffns[n].astype(F32))

    def ffn_grad_compute(n):
        gather_wait(2, dffn, n)
        staged_ready(4, n)
        staged_ready(6, n)
        grad = dffn[n]
        a2 = a2f[n]
        for at, size in chunks_of(hidden, 256):
            span = pl.ds(at, size)
            gate_val = dot(a2, wgu[0, :, span])
            up_val = dot(a2, wgu[1, :, span])
            d_hidden = dot_nt(grad, wdn[span, :])
            sig = jax.nn.sigmoid(gate_val)
            act = gate_val * sig
            hid_st[:, span] = (act * up_val).astype(BF)
            dgu_st[:, span] = (d_hidden * up_val * (sig + act * (1.0 - sig))).astype(BF)
            dgu_st[:, pl.ds(hidden + at, size)] = (d_hidden * act).astype(BF)
        d_gate = dgu_st[:, 0:hidden]
        d_up = dgu_st[:, hidden : 2 * hidden]
        for at, size in wide:
            span = pl.ds(at, size)
            scatter_put(2, at, size, dot_nt(d_gate, wgu[0, span, :]) + dot_nt(d_up, wgu[1, span, :]))
        scatter_start(2, n)
        out_copy(4, n).start()
        out_copy(6, n).start()
        out_copy(2, n).start()
        gather_drain(2, dffn, n)

    def attn_grad_in(n):
        d_a2 = scatter_end(2, n)
        grad, d_shift, d_scale = norm_back(x1s[n], d_a2, mod_row(n, 4))
        grad = grad + din[n].astype(F32)
        dx1s[lax.rem(n, 2)] = grad
        dattn[n, 0:rows, :] = (mod_row(n, 2) * grad).astype(BF)
        gather_start(3, dattn, n)
        dmod[n, 2:3, :] = column_sum(grad * attns[n].astype(F32))
        dmod[n, 3:4, :] = d_shift
        dmod[n, 4:5, :] = d_scale

    def attn_grad_compute(n):
        gather_wait(3, dattn, n)
        staged_ready(7, n)
        grad = dattn[n]
        a1 = a1f[n]
        c, s = cosine[n], sine[n]
        lanes_all = heads * LANES
        for pair in range(heads // 2):
            span = pl.ds(pair * 2 * LANES, 2 * LANES)
            q2 = dot(a1, wqkv[0, :, span])
            k2 = dot(a1, wqkv[1, :, span])
            v2 = dot(a1, wqkv[2, :, span]).astype(BF)
            d_mix2 = dot_nt(grad, wout[span, :]).astype(BF)
            for half in range(2):
                at = (pair * 2 + half) * LANES
                cut = slice(half * LANES, (half + 1) * LANES)
                q_gain, k_gain = gains[0:1, at : at + LANES], gains[1:2, at : at + LANES]
                q_inv, q_norm = head_norm(q2[:, cut])
                k_inv, k_norm = head_norm(k2[:, cut])
                q = turn(q_norm * q_gain, c, s).astype(BF)
                k = turn(k_norm * k_gain, c, s).astype(BF)
                v, d_mix = v2[:, cut], d_mix2[:, cut]
                probs = softmax(dot_nt(q, k) * SCALE)
                d_probs = dot_nt(d_mix, v)
                d_v = dot_tn(probs.astype(BF), d_mix)
                d_scores = (probs * (d_probs - jnp.sum(probs * d_probs, axis=-1, keepdims=True))).astype(BF)
                d_q = turn_back(dot(d_scores, k) * SCALE, c, s)
                d_k = turn_back(dot_tn(d_scores, q) * SCALE, c, s)
                gacc[0:1, at : at + LANES] += column_sum(d_q * q_norm)
                gacc[1:2, at : at + LANES] += column_sum(d_k * k_norm)
                d_q = d_q * q_gain
                d_k = d_k * k_gain
                d_q = q_inv * (d_q - q_norm * (jnp.sum(d_q * q_norm, axis=-1, keepdims=True) * (1.0 / HEAD_DIM)))
                d_k = k_inv * (d_k - k_norm * (jnp.sum(d_k * k_norm, axis=-1, keepdims=True) * (1.0 / HEAD_DIM)))
                dqkv_st[:, at : at + LANES] = d_q.astype(BF)
                dqkv_st[:, lanes_all + at : lanes_all + at + LANES] = d_k.astype(BF)
                dqkv_st[:, 2 * lanes_all + at : 2 * lanes_all + at + LANES] = d_v.astype(BF)
        for at, size in wide:
            span = pl.ds(at, size)
            total = dot_nt(dqkv_st[:, 0:lanes_all], wqkv[0, span, :])
            total += dot_nt(dqkv_st[:, lanes_all : 2 * lanes_all], wqkv[1, span, :])
            total += dot_nt(dqkv_st[:, 2 * lanes_all : 3 * lanes_all], wqkv[2, span, :])
            scatter_put(3, at, size, total)
        scatter_start(3, n)
        out_copy(7, n).start()
        out_copy(3, n).start()
        gather_drain(3, dattn, n)

    def block_grad_out(n):
        d_a1 = scatter_end(3, n)
        grad, d_shift, d_scale = norm_back(xin[n].astype(F32), d_a1, mod_row(n, 1))
        grad = grad + dx1s[lax.rem(n, 2)]
        dxout[n] = grad
        dmod[n, 0:1, :] = d_shift
        dmod[n, 1:2, :] = d_scale

        @pl.when(dec)
        def _():
            xin[n] = grad.astype(BF)
            dz_copy(n).start()

        for k in range(3):
            dmod_copy(k, n).start()

    def stage(n, body):
        @pl.when((n >= 0) & (n < images))
        def _():
            body(n)

    def forward_step(step, carry):
        j = step - 1
        stage(j, attn_compute)
        stage(j - 1, lambda n: gather_relay(1, a2f, n))
        stage(j - 2, block_out)
        stage(j, lambda n: scatter_middle(0, n))
        stage(j + 1, attn_in)
        stage(j - 1, ffn_compute)
        stage(j + 1, lambda n: gather_relay(0, a1f, n))
        stage(j, ffn_in)
        stage(j - 1, lambda n: scatter_middle(1, n))
        return carry

    lax.fori_loop(0, images + 3, forward_step, 0)

    def backward_step(step, carry):
        j = step - 1
        stage(j, ffn_grad_compute)
        stage(j - 1, lambda n: gather_relay(3, dattn, n))
        stage(j - 2, block_grad_out)
        stage(j, lambda n: scatter_middle(2, n))
        stage(j + 1, ffn_grad_in)
        stage(j - 1, attn_grad_compute)
        stage(j + 1, lambda n: gather_relay(2, dffn, n))
        stage(j, attn_grad_in)
        stage(j - 1, lambda n: scatter_middle(3, n))
        return carry

    lax.fori_loop(0, images + 3, backward_step, 0)

    for which in (4, 5, 6, 7):
        out_copy(which, images - 1).wait()

    def drain(n, carry):
        for which in (0, 1, 2, 3):
            out_copy(which, n).wait()
        part = dmod[n, :, its_tiles(me)]
        for k in range(3):
            dmod_copy(k, n).wait()
            part += dmod_recv[k, n]
        dmod_part[n] = part.astype(BF)

        @pl.when(enc)
        def _():
            z_copy(n).wait_send()

        @pl.when(dec)
        def _():
            dz_copy(n).wait_send()

        return carry

    lax.fori_loop(0, images, drain, 0)


def run_main(tok, vel, mod_cols, cosine, sine, wqkv, wout, wgu, wdn, gains):
    images, rows, width = tok.shape
    tokens = 4 * rows
    lanes_all = wout.shape[0]
    heads = lanes_all // LANES
    hidden = wdn.shape[0]
    vmem = pl.BlockSpec(memory_space=pltpu.VMEM)
    anywhere = pl.BlockSpec(memory_space=pl.ANY)

    def hbm(last):
        return jax.ShapeDtypeStruct((images, tokens, last), BF)

    out_shape = (
        jax.ShapeDtypeStruct((images, rows, width), BF),
        jax.ShapeDtypeStruct((images, rows, width), F32),
        jax.ShapeDtypeStruct((images, 8, 3 * LANES), BF),
        jax.ShapeDtypeStruct((8, lanes_all), F32),
        jax.ShapeDtypeStruct((8, width), F32),
        hbm(width),
        hbm(width),
        hbm(width),
        hbm(width),
        hbm(hidden),
        hbm(lanes_all),
        hbm(2 * hidden),
        hbm(3 * lanes_all),
    )
    scratch = [
        pltpu.VMEM((images, rows, width), BF),
        pltpu.VMEM((images, rows, width), BF),
        pltpu.VMEM((images, tokens, width), BF),
        pltpu.VMEM((images, tokens, width), BF),
        pltpu.VMEM((images, tokens, width), BF),
        pltpu.VMEM((images, tokens, width), BF),
        pltpu.VMEM((images, rows, width), F32),
        pltpu.VMEM((images, rows, width), BF),
        pltpu.VMEM((images, rows, width), BF),
        pltpu.VMEM((2, 2 * rows, width), F32),
        pltpu.VMEM((2, 2 * rows, width), BF),
        pltpu.VMEM((2, 2, 2 * rows, width), BF),
        pltpu.VMEM((2, rows, width), BF),
        pltpu.VMEM((2, 2, rows, width), BF),
        pltpu.VMEM((2, rows, width), F32),
        pltpu.VMEM((tokens, lanes_all), BF),
        pltpu.VMEM((tokens, hidden), BF),
        pltpu.VMEM((tokens, 2 * hidden), BF),
        pltpu.VMEM((tokens, 3 * lanes_all), BF),
        pltpu.VMEM((images, 8, width), F32),
        pltpu.VMEM((3, images, 8, 3 * LANES), F32),
        pltpu.VMEM((images, 8, width), F32),
        pltpu.VMEM((3, images, 8, 3 * LANES), F32),
        pltpu.SemaphoreType.DMA((2, 3)),
        pltpu.SemaphoreType.DMA((2, 3, images)),
        pltpu.SemaphoreType.DMA((4, 6, images)),
        pltpu.SemaphoreType.DMA((4, 4, images)),
        pltpu.SemaphoreType.DMA((4, images)),
        pltpu.SemaphoreType.DMA((8, images)),
        pltpu.SemaphoreType.DMA((2,)),
    ]
    return pl.pallas_call(
        functools.partial(main_kernel, images, heads),
        out_shape=out_shape,
        in_specs=[anywhere, anywhere] + [vmem] * 8,
        out_specs=[vmem] * 5 + [anywhere] * 8,
        scratch_shapes=scratch,
        compiler_params=pltpu.CompilerParams(
            collective_id=0, has_side_effects=True, vmem_limit_bytes=62 * 2**20
        ),
    )(tok, vel, mod_cols, cosine, sine, wqkv, wout, wgu, wdn, gains)


def flat_plan(width, hidden, qkv_blocks, out_rows):
    gu_blocks, blocks = 2 * hidden // LANES, width // LANES
    half_down = blocks * hidden // 2
    qkv_cut, out_cut = qkv_blocks // 2, blocks - 1
    first = (gu_blocks // 2) * width + half_down + qkv_cut * width + out_cut * out_rows
    second = (gu_blocks - gu_blocks // 2) * width + half_down + (qkv_blocks - qkv_cut) * width
    second += (blocks - out_cut) * out_rows
    chunk = width // 2
    half = -(-max(first, second) // chunk) * chunk

    def pieces(segment, block):
        if segment == 0:
            cut = gu_blocks // 2
            return [(block * width if block < cut else half + (block - cut) * width, 0, width)]
        at = (gu_blocks // 2) * width
        at_second = half + (gu_blocks - gu_blocks // 2) * width
        if segment == 1:
            low, high = block * hidden, (block + 1) * hidden
            if high <= half_down:
                return [(at + low, 0, hidden)]
            if low >= half_down:
                return [(at_second + low - half_down, 0, hidden)]
            return [(at + low, 0, half_down - low), (at_second, half_down - low, high - half_down)]
        at, at_second = at + half_down, at_second + half_down
        if segment == 2:
            if block < qkv_cut:
                return [(at + block * width, 0, width)]
            return [(at_second + (block - qkv_cut) * width, 0, width)]
        at, at_second = at + qkv_cut * width, at_second + (qkv_blocks - qkv_cut) * width
        if block < out_cut:
            return [(at + block * out_rows, 0, out_rows)]
        return [(at_second + (block - out_cut) * out_rows, 0, out_rows)]

    return half, chunk, pieces


def tail_kernel(
    dp,
    a2_hbm,
    dgu_hbm,
    hid_hbm,
    dffn_hbm,
    a1_hbm,
    dqkv_hbm,
    mix_hbm,
    dattn_hbm,
    pick_qkv,
    pick_out,
    summand,
    dmod_low,
    extra,
    totals,
    dmod_all,
    sum_all,
    extra_all,
    left_a,
    right_a,
    left_b,
    right_b,
    left_c,
    turned,
    own,
    arrived,
    sum_st,
    sum_recv,
    load_sems,
    part_sems,
    total_sems,
    sum_sems,
    all_sems,
):
    section = lax.axis_index("section")
    place = lax.axis_index("dp")
    me = lax.axis_index("tensor")
    sib = me + 1 - 2 * lax.rem(me, 2)
    across = lax.rem(me + 2, 4)
    width, hidden = left_a.shape[1], left_b.shape[1]
    qkv_blocks, out_rows = pick_qkv.shape[1] // LANES, pick_out.shape[0]
    half, chunk, pieces = flat_plan(width, hidden, qkv_blocks, out_rows)
    count = half // chunk

    loads = [
        pltpu.make_async_copy(src, dst, load_sems.at[i])
        for i, (src, dst) in enumerate(
            (
                (a2_hbm, left_a),
                (dgu_hbm, right_a),
                (hid_hbm, left_b),
                (dffn_hbm, right_b),
                (mix_hbm, left_c),
                (a1_hbm, left_a),
                (dqkv_hbm, right_a),
                (dattn_hbm, right_b),
            )
        )
    ]
    for i in range(5):
        loads[i].start()

    barrier = pltpu.get_barrier_semaphore()
    for where in ({"tensor": sib}, {"tensor": across}, {"section": 1 - section}):
        pl.semaphore_signal(barrier, inc=1, device_id=where, device_id_type=MESH)
    for k in range(1, dp):
        pl.semaphore_signal(barrier, inc=1, device_id={"dp": lax.rem(place + k, dp)}, device_id_type=MESH)

    def put(segment, block, value):
        for at, low, size in pieces(segment, block):
            own[at : at + size, :] = value[low : low + size].astype(BF)

    def put_pair(segment, block, value):
        for i in range(value.shape[1] // LANES):
            put(segment, block + i, value[:, i * LANES : (i + 1) * LANES])

    def turn_left(ref):
        tokens, cols = ref.shape
        for at in range(0, tokens, 256):
            turned[0:cols, at : at + 256] = ref[at : at + 256, :].T

    def gate_up_blocks(*blocks):
        for block in blocks:
            value = dot(turned[...], right_a[:, block * LANES : (block + 2) * LANES])
            put_pair(0, block, value)

    def qkv_tiles(*tiles):
        for tile in tiles:
            value = dot_tn(left_a[:, tile * LANES : (tile + 1) * LANES], right_a[...]).astype(BF)
            value = dot(value, pick_qkv[...])
            for block in range(qkv_blocks):
                (at, _, _), = pieces(2, block)
                cut = slice(block * LANES, (block + 1) * LANES)
                own[at + tile * LANES : at + (tile + 1) * LANES, :] = value[:, cut].astype(BF)

    def portion(i):
        gu_blocks, tiles = right_a.shape[1] // LANES, width // LANES
        gu_blocks = 2 * hidden // LANES
        if i == 0:
            loads[0].wait()
            turn_left(left_a)
            loads[5].start()
            loads[1].wait()
            gate_up_blocks(0, gu_blocks // 2)
        elif i == 1:
            gate_up_blocks(2, gu_blocks // 2 + 2)
        elif i == 2:
            gate_up_blocks(*range(4, gu_blocks // 2, 2), *range(gu_blocks // 2 + 4, gu_blocks, 2))
            loads[6].start()
        elif i == 3:
            loads[2].wait()
            turn_left(left_b)
            loads[3].wait()
            for block in range(0, tiles, 2):
                cut = slice(block * LANES, min(width, (block + 2) * LANES))
                put_pair(1, block, dot(turned[0:hidden, :], right_b[:, cut]))
            loads[7].start()
        elif i in (4, 5, 6):
            if i == 4:
                loads[5].wait()
                loads[6].wait()
            third = -(-tiles // 3)
            qkv_tiles(*range((i - 4) * third, min(tiles, (i - 3) * third)))
        elif i == 7:
            loads[4].wait()
            loads[7].wait()
            value = dot(pick_out[...], dot_tn(left_c[...], right_b[...]).astype(BF))
            put_pair(3, 0, value)
            (at, _, size), = pieces(3, tiles - 1)
            own[at + size :, :] = jnp.zeros((2 * half - at - size, LANES), BF)

    def along(direction, onward):
        step = 1 if (direction == 0) == onward else dp - 1
        return {"dp": lax.rem(place + step, dp)}

    def behind(direction):
        return place if direction == 0 else dp - 1 - place

    def rows_of(direction, c):
        return pl.ds(pl.multiple_of(direction * half + c * chunk, chunk), chunk)

    def part_copy(direction, c):
        return pltpu.make_async_remote_copy(
            src_ref=own.at[rows_of(direction, c)],
            dst_ref=arrived.at[rows_of(direction, c)],
            send_sem=part_sems.at[direction, 0, c],
            recv_sem=part_sems.at[direction, 1, c],
            device_id=along(direction, True),
            device_id_type=MESH,
        )

    def total_copy(direction, c):
        return pltpu.make_async_remote_copy(
            src_ref=totals.at[rows_of(direction, c)],
            dst_ref=totals.at[rows_of(direction, c)],
            send_sem=total_sems.at[direction, 0, c],
            recv_sem=total_sems.at[direction, 1, c],
            device_id=along(direction, False),
            device_id_type=MESH,
        )

    def add_part(direction, c):
        begins, ends = behind(direction) == 0, behind(direction) == dp - 1
        rows = rows_of(direction, c)

        @pl.when(begins)
        def _():
            part_copy(direction, c).start()

        @pl.when(jnp.logical_not(begins))
        def _():
            part_copy(direction, c).wait_recv()
            value = (own[rows, :].astype(F32) + arrived[rows, :].astype(F32)).astype(BF)

            @pl.when(ends)
            def _():
                totals[rows, :] = value
                total_copy(direction, c).start()

            @pl.when(jnp.logical_not(ends))
            def _():
                own[rows, :] = value
                part_copy(direction, c).start()

    def pass_total(direction, c):
        begins, ends = behind(direction) == 0, behind(direction) == dp - 1

        @pl.when(jnp.logical_not(ends))
        def _():
            total_copy(direction, c).wait_recv()

            @pl.when(jnp.logical_not(begins))
            def _():
                total_copy(direction, c).start()

    skew = 2

    def chunk_step(step):
        for direction in range(2):
            c = step - skew * behind(direction)

            @pl.when((c >= 0) & (c < count))
            def _():
                add_part(direction, c)

        for direction in range(2):
            u = step - skew * (2 * (dp - 1) - behind(direction))

            @pl.when((u >= 0) & (u < count))
            def _():
                pass_total(direction, u)

    def sum_copy(which):
        where = ({"section": 1 - section}, {"tensor": sib}, {"tensor": across})[which]
        height = (8, 16, 16)[which]
        src = summand if which == 0 else sum_st.at[which - 1]
        return pltpu.make_async_remote_copy(
            src_ref=src.at[pl.ds(0, height)],
            dst_ref=sum_recv.at[which, pl.ds(0, height)],
            send_sem=sum_sems.at[which, 0],
            recv_sem=sum_sems.at[which, 1],
            device_id=where,
            device_id_type=MESH,
        )

    def all_copy(which, k, outgoing):
        ref = (dmod_all, sum_all, extra_all)[which]
        peer = lax.rem(place + k, dp)
        slot = place if outgoing else peer
        return pltpu.make_async_remote_copy(
            src_ref=ref.at[slot],
            dst_ref=ref.at[slot],
            send_sem=all_sems.at[which, 0, k],
            recv_sem=all_sems.at[which, 1, slot],
            device_id={"dp": peer},
            device_id_type=MESH,
        )

    def small(step):
        if step == 0:
            dmod_all[place] = dmod_low[...]
            for k in range(1, dp):
                all_copy(0, k, True).start()
            sum_copy(0).start()
        elif step == 1:
            sum_copy(0).wait()
            sum_st[0] = summand[...]
            sum_st[0, 0:8, :] += sum_recv[0, 0:8, :]
            sum_copy(1).start()
        elif step == 2:
            sum_copy(1).wait()
            sum_st[1] = sum_st[0] + sum_recv[1]
            sum_copy(2).start()
        elif step == 3:
            sum_copy(2).wait()
            total = sum_st[1] + sum_recv[2]
            sum_all[place] = total.astype(BF)
            squares = total[8:16, 0:LANES]
            for i in range(1, width // LANES):
                squares += total[8:16, i * LANES : (i + 1) * LANES]
            extra_all[place, 0:8, :] = extra[...]
            extra_all[place, 8:16, :] = jnp.zeros_like(extra)
            extra_all[place, 8:16, 0:LANES] = squares
            for k in range(1, dp):
                all_copy(1, k, True).start()
                all_copy(2, k, True).start()

    portion(0)
    pl.semaphore_wait(barrier, 3 + dp - 1)
    for step in range(8):
        chunk_step(step)
        small(step)
        portion(step + 1)

    def later_step(step, carry):
        chunk_step(step)
        return carry

    lax.fori_loop(8, count + 2 * skew * (dp - 1), later_step, 0)

    for which in range(3):
        for k in range(1, dp):
            all_copy(which, k, True).wait_send()
            all_copy(which, k, False).wait_recv()

    def drain(c, carry):
        for direction in range(2):

            @pl.when(behind(direction) != dp - 1)
            def _():
                part_copy(direction, c).wait_send()

            @pl.when(behind(direction) != 0)
            def _():
                total_copy(direction, c).wait_send()

        return carry

    lax.fori_loop(0, count, drain, 0)


def run_tail(dp, a2, dgu, hid, dffn, a1, dqkv, mix, dattn, pick_qkv, pick_out, summand, dmod_low, extra):
    tokens, width = a2.shape
    hidden = hid.shape[1]
    out_rows, lanes_all = pick_out.shape
    vmem = pl.BlockSpec(memory_space=pltpu.VMEM)
    anywhere = pl.BlockSpec(memory_space=pl.ANY)
    half, chunk, _ = flat_plan(width, hidden, pick_qkv.shape[1] // LANES, out_rows)
    return pl.pallas_call(
        functools.partial(tail_kernel, dp),
        out_shape=(
            jax.ShapeDtypeStruct((2 * half, LANES), BF),
            jax.ShapeDtypeStruct((dp,) + dmod_low.shape, BF),
            jax.ShapeDtypeStruct((dp,) + summand.shape, BF),
            jax.ShapeDtypeStruct((dp, 16, extra.shape[1]), F32),
        ),
        in_specs=[anywhere] * 8 + [vmem] * 5,
        out_specs=[vmem] * 4,
        scratch_shapes=[
            pltpu.VMEM((tokens, width), BF),
            pltpu.VMEM((tokens, dgu.shape[1]), BF),
            pltpu.VMEM((tokens, hidden), BF),
            pltpu.VMEM((tokens, width), BF),
            pltpu.VMEM((tokens, lanes_all), BF),
            pltpu.VMEM((width, tokens), BF),
            pltpu.VMEM((2 * half, LANES), BF),
            pltpu.VMEM((2 * half, LANES), BF),
            pltpu.VMEM((2,) + summand.shape, F32),
            pltpu.VMEM((3,) + summand.shape, F32),
            pltpu.SemaphoreType.DMA((8,)),
            pltpu.SemaphoreType.DMA((2, 2, half // chunk)),
            pltpu.SemaphoreType.DMA((2, 2, half // chunk)),
            pltpu.SemaphoreType.DMA((3, 2)),
            pltpu.SemaphoreType.DMA((3, 2, dp)),
        ],
        compiler_params=pltpu.CompilerParams(
            collective_id=1, has_side_effects=True, vmem_limit_bytes=62 * 2**20
        ),
    )(a2, dgu, hid, dffn, a1, dqkv, mix, dattn, pick_qkv, pick_out, summand, dmod_low, extra)


def finish_kernel(
    flat_hbm, gu_hbm, down_hbm, qkv_hbm, out_hbm, flat, gate_up, down, qkv, out, load_sems, store_sems
):
    width, hidden = gate_up.shape[1], gate_up.shape[2]
    part, blocks = out.shape[0], width // LANES
    whole = part // LANES * LANES
    rest = part - whole
    qkv_blocks = 3 * whole // LANES + 1
    half, _, pieces = flat_plan(width, hidden, qkv_blocks, part)
    hidden_blocks = hidden // LANES
    groups = (
        [(0, b) for b in range(hidden_blocks)],
        [(0, hidden_blocks + b) for b in range(hidden_blocks)],
        [(1, b) for b in range(blocks)],
        [(2, b) for b in range(qkv_blocks)],
        [(3, b) for b in range(blocks)],
    )
    loads = []
    for group in groups:
        spans = []
        for segment, block in group:
            for at, _, size in pieces(segment, block):
                if spans and spans[-1][0] + spans[-1][1] == at:
                    spans[-1][1] += size
                else:
                    spans.append([at, size])
        copies = []
        for at, size in spans:
            rows = pl.ds(at, size)
            sem = load_sems.at[len(loads), len(copies)]
            copies.append(pltpu.make_async_copy(flat_hbm.at[rows], flat.at[rows], sem))
            copies[-1].start()
        loads.append(copies)
    stores = (
        pltpu.make_async_copy(gate_up.at[0], gu_hbm.at[0], store_sems.at[0]),
        pltpu.make_async_copy(gate_up.at[1], gu_hbm.at[1], store_sems.at[1]),
        pltpu.make_async_copy(down, down_hbm, store_sems.at[2]),
        pltpu.make_async_copy(qkv, qkv_hbm, store_sems.at[3]),
        pltpu.make_async_copy(out, out_hbm, store_sems.at[4]),
    )
    for i, group in enumerate(groups):
        for copy in loads[i]:
            copy.wait()
        for segment, block in group:
            for at, low, size in pieces(segment, block):
                value = flat[at : at + size, :].astype(F32)
                rows = slice(low, low + size)
                if segment == 0:
                    local = block % hidden_blocks
                    gate_up[block // hidden_blocks, rows, local * LANES : (local + 1) * LANES] = value
                elif segment == 1:
                    down[rows, block * LANES : (block + 1) * LANES] = value
                elif segment == 3:
                    out[rows, block * LANES : (block + 1) * LANES] = value
                elif block < qkv_blocks - 1:
                    j, local = block // (whole // LANES), block % (whole // LANES)
                    qkv[j, rows, local * LANES : (local + 1) * LANES] = value
                else:
                    for j in range(3):
                        moved = value if j == 0 else pltpu.roll(value, LANES - j * rest, 1)
                        qkv[j, rows, whole:part] = moved[:, 0:rest]
        stores[i].start()
    for copy in stores:
        copy.wait()


def run_finish(flat, width, hidden, part):
    anywhere = pl.BlockSpec(memory_space=pl.ANY)
    shapes = ((2, width, hidden), (hidden, width), (3, width, part), (part, width))
    return pl.pallas_call(
        finish_kernel,
        out_shape=tuple(jax.ShapeDtypeStruct(shape, F32) for shape in shapes),
        in_specs=[anywhere],
        out_specs=[anywhere] * 4,
        scratch_shapes=[pltpu.VMEM(flat.shape, BF)]
        + [pltpu.VMEM(shape, F32) for shape in shapes]
        + [pltpu.SemaphoreType.DMA((5, 2)), pltpu.SemaphoreType.DMA((5,))],
        compiler_params=pltpu.CompilerParams(vmem_limit_bytes=48 * 2**20),
    )(flat)


def time_embed(bin_row, feature_count):
    halfway = feature_count // 2
    frequency = jnp.exp(-math.log(10000.0) * jnp.arange(halfway, dtype=F32) / halfway)
    moment = (bin_row.astype(F32) + 0.5) * (1000.0 / NBINS)
    angles = moment[:, None] * frequency[None, :]
    return jnp.concatenate([jnp.cos(angles), jnp.sin(angles)], axis=-1)


def per_device(
    tokens,
    velocity_grad,
    bins,
    labels,
    places,
    class_table,
    mod_weight,
    qkv_weight,
    out_weight,
    gate_up_weight,
    down_weight,
    q_gain,
    k_gain,
):
    micro, per_micro, rows, width = tokens.shape
    images = micro * per_micro
    dp = lax.axis_size("dp")
    me = lax.axis_index("tensor")
    heads = q_gain.shape[1] // HEAD_DIM
    select = jnp.asarray(head_select(heads), BF)

    def condition(bin_row, label_row):
        one_hot = label_row[:, None] == jnp.arange(class_table.shape[0], dtype=jnp.int32)[None, :]
        picked = jnp.dot(one_hot.astype(BF), class_table, preferred_element_type=F32)
        return time_embed(bin_row, width) + picked, one_hot

    cond, _ = condition(bins.reshape(images), labels.reshape(images))
    silu_low = jax.nn.silu(cond).astype(BF)
    mod_w = mod_weight[0]
    part = width // 4
    columns = jnp.einsum("id,djf->ijf", silu_low, mod_w, preferred_element_type=F32)
    shift = me * (part - 2 * LANES)
    mod_cols = lax.dynamic_update_slice(jnp.zeros((images, 8, 3 * LANES), F32), columns, (0, 0, shift))

    order = jnp.stack([me, (me + 2) % 4, me + 1 - 2 * (me % 2), (me + 2) % 4 + 1 - 2 * (me % 2)])
    placed = jnp.take(places.reshape(images, 4, rows), order, axis=1).reshape(images * 4 * rows)
    grid = jnp.arange(GRID, dtype=jnp.int32)[None, :]
    marks = jnp.concatenate([placed[:, None] // GRID == grid, placed[:, None] % GRID == grid], axis=1).astype(F32)
    angles = jnp.dot(marks, jnp.asarray(angle_table()), precision=lax.Precision.HIGHEST)
    angles = angles.reshape(images, 4 * rows, 2 * LANES)

    wqkv = jnp.einsum("jde,ef->jdf", qkv_weight[0], select, preferred_element_type=F32).astype(BF)
    wout = jnp.einsum("ef,ed->fd", select, out_weight[0], preferred_element_type=F32).astype(BF)
    gains = jnp.dot(jnp.concatenate([q_gain, k_gain], axis=0), select, preferred_element_type=F32)

    results = run_main(
        tokens.reshape(images, rows, width),
        velocity_grad.reshape(images, rows, width),
        mod_cols,
        angles[..., :LANES],
        angles[..., LANES:],
        wqkv,
        wout,
        gate_up_weight[0],
        down_weight[0],
        gains,
    )
    z_rows, dx_rows, dmod_part, gain_sums, squares, a1, a2, d_ffn, d_attn, units, mixed, d_gu, d_qkv = results

    dmod_mine = lax.dynamic_slice(dmod_part, (0, 0, shift), (images, 6, part))
    grad_silu = jnp.einsum("ijf,djf->id", dmod_mine, mod_w, preferred_element_type=F32)
    sig = jax.nn.sigmoid(cond)
    grad_cond = grad_silu * (sig + cond * sig * (1.0 - sig))
    summand = jnp.concatenate([grad_cond, squares], axis=0)
    lanes_all = heads * LANES
    numbers = jnp.stack([bins.reshape(images), labels.reshape(images)]).astype(F32)
    extra = jnp.concatenate([gain_sums[0:2], jnp.pad(numbers, ((0, 4), (0, lanes_all - images)))], axis=0)

    select_np = head_select(heads)
    full = part // LANES * LANES
    pick = np.zeros((3 * lanes_all, 3 * full + LANES), np.float32)
    for j in range(3):
        rows_j = slice(j * lanes_all, (j + 1) * lanes_all)
        pick[rows_j, j * full : (j + 1) * full] = select_np.T[:, :full]
        rest_at = 3 * full + j * (part - full)
        pick[rows_j, rest_at : rest_at + part - full] = select_np.T[:, full:]
    flat = images * 4 * rows
    flat_grads, dmod_all, sum_all, extra_all = run_tail(
        dp,
        a2.reshape(flat, width),
        d_gu.reshape(flat, d_gu.shape[2]),
        units.reshape(flat, units.shape[2]),
        d_ffn.reshape(flat, width),
        a1.reshape(flat, width),
        d_qkv.reshape(flat, d_qkv.shape[2]),
        mixed.reshape(flat, lanes_all),
        d_attn.reshape(flat, width),
        jnp.asarray(pick, BF),
        select,
        summand,
        dmod_part.reshape(images * 8, 3 * LANES),
        extra,
    )
    gate_up_grad, down_grad, qkv_grad, out_grad = [
        item[None] for item in run_finish(flat_grads, width, units.shape[2], part)
    ]

    gains_sum = jnp.sum(extra_all[:, 0:2], axis=0)
    gains_sum = jnp.einsum("jf,ef->je", gains_sum, select.astype(F32), precision=lax.Precision.HIGHEST)
    bins_all = extra_all[:, 2, :images].reshape(dp * images).astype(jnp.int32)
    labels_all = extra_all[:, 3, :images].reshape(dp * images).astype(jnp.int32)
    cond_all, one_hot = condition(bins_all, labels_all)
    silu_all = jax.nn.silu(cond_all).astype(BF)
    dmod_all = lax.dynamic_slice(
        dmod_all.reshape(dp * images, 8, 3 * LANES), (0, 0, shift), (dp * images, 6, part)
    )
    mod_grad = jnp.einsum("id,ijf->djf", silu_all, dmod_all, preferred_element_type=F32)[None]
    grad_cond_all = sum_all[:, 0:8].reshape(dp * images, width)
    class_grad = jnp.dot(one_hot.astype(BF).T, grad_cond_all, preferred_element_type=F32)
    square_totals = jnp.sum(extra_all[:, 8:11, 0:LANES], axis=(0, 2))
    count = images * rows * width * dp * lax.axis_size("tensor")
    stats = jnp.sqrt(square_totals / count)[None, :]
    whole = (1, micro, per_micro, rows, width)
    return (
        z_rows.reshape(whole),
        dx_rows.reshape(whole),
        mod_grad,
        qkv_grad,
        out_grad,
        gate_up_grad,
        down_grad,
        gains_sum[0:1],
        gains_sum[1:2],
        class_grad,
        stats,
    )


def solution(mesh):
    return jax.shard_map(
        per_device,
        mesh=mesh,
        in_specs=(
            P(None, "dp", "tensor", None),
            P(None, "dp", "tensor", None),
            P(None, "dp"),
            P(None, "dp"),
            P(None, "dp", None),
            P(),
            P("section", None, None, "tensor"),
            P("section", None, None, "tensor"),
            P("section", "tensor", None),
            P("section", None, None, "tensor"),
            P("section", "tensor", None),
            P("section", "tensor"),
            P("section", "tensor"),
        ),
        out_specs=(
            P("section", None, "dp", "tensor", None),
            P("section", None, "dp", "tensor", None),
            P("section", None, None, "tensor"),
            P("section", None, None, "tensor"),
            P("section", "tensor", None),
            P("section", None, None, "tensor"),
            P("section", "tensor", None),
            P("section", "tensor"),
            P("section", "tensor"),
            P(),
            P("section", None),
        ),
        check_vma=False,
    )
```

```python
import functools
import math

import jax
import jax.numpy as jnp
import numpy as np
from jax import lax
from jax.experimental import pallas as pl
from jax.experimental.pallas import tpu as pltpu
from jax.sharding import PartitionSpec as P

MESH = pl.DeviceIdType.MESH
HEAD_DIM = 72
LANES = 128
NBINS = 1000
GRID = 16
EPS = 1e-06
BF = jnp.bfloat16
F32 = jnp.float32
SCALE = HEAD_DIM**-0.5

KEEP, SLOTS, PACK = 2, 4, 4
LENT = 3
ORDERS = (
    (
        0, 1, 2, 8, 3, 16, 9, 24, 4, 17, 10, 32, 25, 18, 40, 11, 26, 48,
        33, 56, 19, 34, 41, 27, 49, 64, 12, 42, 57, 50, 35, 58, 65, 20, 5, 43,
        28, 66, 51, 59, 13, 36, 6, 21, 67, 44, 29, 52, 60, 37, 7, 68, 14, 22,
        45, 30, 15, 53, 61, 23, 38, 31, 69, 46, 39, 54, 47, 62, 70, 55, 63, 71,
        72, 73, 80, 88, 81, 96, 89, 97, 104, 105, 112, 113, 120, 74, 121, 82, 128, 90,
        98, 75, 106, 136, 83, 129, 91, 114, 76, 99, 122, 84, 107, 130, 92, 100, 115, 137,
        77, 123, 85, 78, 108, 93, 86, 138, 101, 94, 79, 116, 102, 131, 124, 87, 109, 110,
        95, 139, 117, 103, 132, 125, 111, 133, 118, 140, 126, 119, 141, 134, 127, 142, 135, 143,
    ),
    (
        72, 73, 74, 75, 76, 77, 80, 78, 0, 8, 1, 16, 81, 9, 24, 2, 82, 83,
        84, 17, 32, 25, 10, 18, 3, 40, 33, 85, 88, 86, 11, 26, 96, 19, 4, 34,
        41, 48, 27, 89, 12, 104, 42, 97, 20, 35, 49, 112, 5, 28, 90, 56, 105, 79,
        98, 43, 120, 91, 113, 36, 13, 128, 121, 106, 6, 44, 21, 7, 129, 92, 136, 14,
        29, 87, 99, 114, 100, 15, 22, 137, 64, 30, 122, 37, 107, 23, 38, 50, 57, 45,
        108, 115, 130, 58, 31, 93, 46, 123, 116, 138, 101, 94, 131, 39, 124, 102, 65, 139,
        109, 132, 51, 47, 110, 66, 95, 59, 52, 117, 140, 118, 103, 125, 67, 111, 133, 126,
        119, 60, 53, 134, 141, 61, 127, 142, 68, 54, 135, 69, 62, 55, 63, 143, 70, 71,
    ),
)


def lane_of():
    quarter = HEAD_DIM // 4
    lanes = np.zeros((HEAD_DIM,), np.int64)
    for half in range(2):
        for part in range(2):
            for i in range(quarter):
                lanes[half * 2 * quarter + part * quarter + i] = part * 64 + half * quarter + i
    return lanes


def head_select(heads):
    select = np.zeros((heads * HEAD_DIM, heads * LANES), np.float32)
    lanes = lane_of()
    for h in range(heads):
        for f in range(HEAD_DIM):
            select[h * HEAD_DIM + f, h * LANES + lanes[f]] = 1.0
    return select


def angle_table():
    quarter = HEAD_DIM // 4
    frequency = (10000.0 ** (-np.arange(quarter, dtype=np.float32) / np.float32(quarter))).astype(np.float32)
    lanes = lane_of().reshape(2, 2, quarter)
    table = np.zeros((2 * GRID, 2 * LANES), np.float32)
    for place in range(GRID):
        angle = np.float32(place) * frequency
        for half in range(2):
            for part in range(2):
                sign = -1.0 if part == 0 else 1.0
                table[half * GRID + place, lanes[half, part]] = np.cos(angle)
                table[half * GRID + place, LANES + lanes[half, part]] = sign * np.sin(angle)
    return table


def dot(a, b):
    return lax.dot_general(a, b, (((1,), (0,)), ((), ())), preferred_element_type=F32)


def dot_nt(a, b):
    return lax.dot_general(a, b, (((1,), (1,)), ((), ())), preferred_element_type=F32)


def dot_tn(a, b):
    return lax.dot_general(a, b, (((0,), (0,)), ((), ())), preferred_element_type=F32)


def order_words(order, base):
    words = []
    for at in range(0, len(order), PACK):
        words.append(sum(entry * base**i for i, entry in enumerate(order[at : at + PACK])))
    while len(words) & (len(words) - 1):
        words.append(0)
    return words


def chunks_of(size, width):
    return [(at, min(width, size - at)) for at in range(0, size, width)]


def main_kernel(
    images,
    heads,
    tok,
    vel,
    mod_cols,
    cosine,
    sine,
    wqkv,
    wout,
    wgu,
    wdn,
    gains,
    zout,
    dxout,
    dmod_part,
    gacc,
    sacc,
    a1_hbm,
    a2_hbm,
    dffn_hbm,
    dattn_hbm,
    hid_hbm,
    mix_hbm,
    dgu_hbm,
    dqkv_hbm,
    xin,
    din,
    a1f,
    a2f,
    dffn,
    dattn,
    x1s,
    attns,
    ffns,
    keep,
    send_a,
    recv_a,
    send_y,
    recv_y,
    mix_st,
    units_st,
    hid_st,
    dgu_st,
    dqkv_st,
    mod,
    mod_recv,
    dmod,
    dmod_recv,
    mod_sems,
    dmod_sems,
    ag_sems,
    rs_sems,
    zx_sems,
    out_sems,
    in_sems,
):
    rows = tok.shape[1]
    width = tok.shape[2]
    hidden = wdn.shape[0]
    wide = chunks_of(width, 512)
    section = lax.axis_index("section")
    me = lax.axis_index("tensor")
    sib = me + 1 - 2 * lax.rem(me, 2)
    across = lax.rem(me + 2, 4)
    diag = lax.rem(sib + 2, 4)
    peers = (sib, across, diag)
    other = 1 - section
    enc = section == 0
    dec = section == 1

    load_x = pltpu.make_async_copy(tok, xin, in_sems.at[0])
    load_d = pltpu.make_async_copy(vel, din, in_sems.at[1])

    @pl.when(enc)
    def _():
        load_x.start()

    @pl.when(dec)
    def _():
        load_d.start()

    barrier = pltpu.get_barrier_semaphore()
    pl.semaphore_signal(barrier, inc=1, device_id={"tensor": sib}, device_id_type=MESH)
    pl.semaphore_signal(barrier, inc=1, device_id={"tensor": across}, device_id_type=MESH)
    pl.semaphore_signal(barrier, inc=1, device_id={"tensor": diag}, device_id_type=MESH)
    pl.semaphore_signal(barrier, inc=1, device_id={"section": other}, device_id_type=MESH)

    mod[...] = jnp.zeros_like(mod)
    gacc[...] = jnp.zeros_like(gacc)
    sacc[...] = jnp.zeros_like(sacc)
    dmod[...] = jnp.zeros_like(dmod)

    pl.semaphore_wait(barrier, 4)

    def remote(src, dst, send_sem, recv_sem, where):
        return pltpu.make_async_remote_copy(
            src_ref=src, dst_ref=dst, send_sem=send_sem, recv_sem=recv_sem, device_id=where, device_id_type=MESH
        )

    def its_tiles(device):
        return pl.ds(pl.multiple_of(device * (2 * LANES), LANES), 3 * LANES)

    def mod_copy(k):
        return remote(mod_cols, mod_recv.at[k], mod_sems.at[0, k], mod_sems.at[1, k], {"tensor": peers[k]})

    def dmod_copy(k, n):
        return remote(
            dmod.at[n, :, its_tiles(peers[k])],
            dmod_recv.at[k, n],
            dmod_sems.at[0, k, n],
            dmod_sems.at[1, k, n],
            {"tensor": peers[k]},
        )

    for k in (1, 2, 0):
        mod_copy(k).start()
    mod[:, :, its_tiles(me)] = mod_cols[...]

    @pl.when(enc)
    def _():
        load_x.wait()

    @pl.when(dec)
    def _():
        load_d.wait()

    for k in range(3):
        mod_copy(k).wait()
        mod[:, :, its_tiles(peers[k])] += mod_recv[k]

    def gather(which, buf, n, kind):
        src, dst, where = ((0, rows, across), (0, 2 * rows, sib), (rows, 3 * rows, sib))[kind]
        return remote(
            buf.at[n, pl.ds(src, rows)],
            buf.at[n, pl.ds(dst, rows)],
            ag_sems.at[which, 2 * kind, n],
            ag_sems.at[which, 2 * kind + 1, n],
            {"tensor": where},
        )

    def gather_start(which, buf, n):
        gather(which, buf, n, 0).start()
        gather(which, buf, n, 1).start()

    def gather_relay(which, buf, n):
        gather(which, buf, n, 0).wait_recv()
        gather(which, buf, n, 2).start()

    def gather_wait(which, buf, n):
        gather(which, buf, n, 1).wait_recv()
        gather(which, buf, n, 2).wait_recv()

    def gather_drain(which, buf, n):
        for kind in range(3):
            gather(which, buf, n, kind).wait_send()

    def to_sibling(which, n):
        return remote(
            send_a.at[which, lax.rem(n, KEEP)],
            recv_a.at[which, lax.rem(n, SLOTS)],
            rs_sems.at[which, 0, n],
            rs_sems.at[which, 1, n],
            {"tensor": sib},
        )

    def over_y(which, n):
        return remote(
            send_y.at[which, lax.rem(n, KEEP)],
            recv_y.at[which, lax.rem(n, SLOTS)],
            rs_sems.at[which, 2, n],
            rs_sems.at[which, 3, n],
            {"tensor": across},
        )

    def scatter_put(which, n, at, size, values):
        kind, own = which, lax.rem(n, KEEP)
        keep[kind, own, :, pl.ds(at, size)] = values[0 : 2 * rows]
        send_a[kind, own, :, pl.ds(at, size)] = values[2 * rows : 4 * rows].astype(BF)

    def scatter_start(which, n):
        to_sibling(which, n).start()

    def scatter_middle(which, n):
        kind, own, slot = which, lax.rem(n, KEEP), lax.rem(n, SLOTS)
        to_sibling(which, n).wait()
        theirs = recv_a[kind, slot, rows : 2 * rows].astype(F32)
        send_y[kind, own] = (keep[kind, own, rows : 2 * rows] + theirs).astype(BF)
        over_y(which, n).start()

    def scatter_end(which, n):
        kind, own, slot = which, lax.rem(n, KEEP), lax.rem(n, SLOTS)
        over_y(which, n).wait()
        mine = keep[kind, own, 0:rows] + recv_a[kind, slot, 0:rows].astype(F32)
        return mine + recv_y[kind, slot].astype(F32)

    def z_copy(n):
        return remote(zout.at[n], xin.at[n], zx_sems.at[0, n], zx_sems.at[1, n], {"section": other})

    def dz_copy(n):
        return remote(xin.at[n], din.at[n], zx_sems.at[2, n], zx_sems.at[3, n], {"section": other})

    def mod_row(n, row):
        return mod[n, pl.ds(row, 1), :]

    def inverse_rms(values):
        return lax.rsqrt(jnp.mean(values * values, axis=-1, keepdims=True) + EPS)

    def column_sum(values):
        return jnp.sum(values, axis=0, keepdims=True)

    def modulated(values, shift, scale):
        return (values * inverse_rms(values)) * (1.0 + scale) + shift

    def norm_back(values, grad, scale):
        inv = inverse_rms(values)
        normed = values * inv
        d_normed = grad * (1.0 + scale)
        d_values = inv * (d_normed - normed * jnp.mean(d_normed * normed, axis=-1, keepdims=True))
        return d_values, column_sum(grad), column_sum(grad * normed)

    def head_norm(raw):
        inv = lax.rsqrt(jnp.sum(raw * raw, axis=-1, keepdims=True) * (1.0 / HEAD_DIM) + EPS)
        return inv, raw * inv

    def turn(values, c, s):
        return values * c + pltpu.roll(values, 64, 1) * s

    def turn_back(values, c, s):
        return values * c - pltpu.roll(values, 64, 1) * s

    def softmax(scores):
        powered = jnp.exp(scores - jnp.max(scores, axis=-1, keepdims=True))
        return powered * (1.0 / jnp.sum(powered, axis=-1, keepdims=True))

    def out_copy(which, n):
        src = (a1f, a2f, dffn, dattn, hid_st, mix_st, dgu_st, dqkv_st)[which]
        dst = (a1_hbm, a2_hbm, dffn_hbm, dattn_hbm, hid_hbm, mix_hbm, dgu_hbm, dqkv_hbm)[which]
        return pltpu.make_async_copy(src.at[n] if which < 4 else src, dst.at[n], out_sems.at[which, n])

    def staged_ready(which, n):
        @pl.when(n > 0)
        def _():
            out_copy(which, n - 1).wait()

    def attn_in(n):
        @pl.when(dec)
        def _():
            z_copy(n).wait_recv()

        values = xin[n].astype(F32)
        sacc[0:1, :] += column_sum(values * values)
        a1f[n, 0:rows, :] = modulated(values, mod_row(n, 0), mod_row(n, 1)).astype(BF)
        gather_start(0, a1f, n)

    def attn_compute(n):
        gather_wait(0, a1f, n)
        staged_ready(5, n)
        a1 = a1f[n]
        c, s = cosine[n], sine[n]
        for pair in range(heads // 2):
            span = pl.ds(pair * 2 * LANES, 2 * LANES)
            q2 = dot_nt(a1, wqkv[0, span, :])
            k2 = dot_nt(a1, wqkv[1, span, :])
            v2 = dot_nt(a1, wqkv[2, span, :]).astype(BF)
            for half in range(2):
                at = (pair * 2 + half) * LANES
                cut = slice(half * LANES, (half + 1) * LANES)
                q = turn(head_norm(q2[:, cut])[1] * gains[0:1, at : at + LANES], c, s).astype(BF)
                k = turn(head_norm(k2[:, cut])[1] * gains[1:2, at : at + LANES], c, s).astype(BF)
                probs = softmax(dot_nt(q, k) * SCALE).astype(BF)
                mix_st[:, at : at + LANES] = dot(probs, v2[:, cut]).astype(BF)
        mixed = mix_st[...]
        for at, size in wide:
            scatter_put(0, n, at, size, dot(mixed, wout[:, pl.ds(at, size)]))
        scatter_start(0, n)
        out_copy(5, n).start()
        out_copy(0, n).start()
        gather_drain(0, a1f, n)

    def ffn_in(n):
        attended = scatter_end(0, n)
        attns[n] = attended.astype(BF)
        values = xin[n].astype(F32) + mod_row(n, 2) * attended
        x1s[n] = values
        sacc[1:2, :] += column_sum(values * values)
        a2f[n, 0:rows, :] = modulated(values, mod_row(n, 3), mod_row(n, 4)).astype(BF)
        gather_start(1, a2f, n)

    def ffn_compute(n):
        @pl.when(enc)
        def _():
            gather_wait(1, a2f, n)

        a2 = a2f[n]
        for at, size in chunks_of(hidden, 256):
            span = pl.ds(at, size)
            gate_val = dot(a2, wgu[0, :, span])
            up_val = dot(a2, wgu[1, :, span])
            units_st[:, span] = (gate_val * jax.nn.sigmoid(gate_val) * up_val).astype(BF)
        units = units_st[...]
        for at, size in wide:
            scatter_put(1, n, at, size, dot(units, wdn[:, pl.ds(at, size)]))
        scatter_start(1, n)
        out_copy(1, n).start()
        gather_drain(1, a2f, n)

    def block_out(n):
        feedfwd = scatter_end(1, n)
        ffns[n] = feedfwd.astype(BF)
        values = x1s[n] + mod_row(n, 5) * feedfwd
        sacc[2:3, :] += column_sum(values * values)
        zout[n] = values.astype(BF)

        @pl.when(enc)
        def _():
            z_copy(n).start()

        @pl.when(dec)
        def _():
            dmod[n, 5:6, :] = column_sum(din[n].astype(F32) * feedfwd)
            send_dmod(n)

    def send_dmod(n):
        for k in range(3):
            dmod_copy(k, n).start()

    def ffn_grad_in(n):
        @pl.when(enc)
        def _():
            dz_copy(n).wait_recv()

        grad = din[n].astype(F32)
        dffn[n, 0:rows, :] = (mod_row(n, 5) * grad).astype(BF)
        gather_start(2, dffn, n)

        @pl.when(enc)
        def _():
            dmod[n, 5:6, :] = column_sum(grad * ffns[n].astype(F32))

    def ffn_grad_compute(n):
        @pl.when(dec)
        def _():
            gather_wait(1, a2f, n)

        gather_wait(2, dffn, n)
        staged_ready(4, n)
        staged_ready(6, n)
        grad = dffn[n]
        a2 = a2f[n]
        for at, size in chunks_of(hidden, 256):
            span = pl.ds(at, size)
            gate_val = dot(a2, wgu[0, :, span])
            up_val = dot(a2, wgu[1, :, span])
            d_hidden = dot_nt(grad, wdn[span, :])
            sig = jax.nn.sigmoid(gate_val)
            act = gate_val * sig
            hid_st[:, span] = (act * up_val).astype(BF)
            dgu_st[:, span] = (d_hidden * up_val * (sig + act * (1.0 - sig))).astype(BF)
            dgu_st[:, pl.ds(hidden + at, size)] = (d_hidden * act).astype(BF)
        d_gate = dgu_st[:, 0:hidden]
        d_up = dgu_st[:, hidden : 2 * hidden]
        for at, size in wide:
            span = pl.ds(at, size)
            scatter_put(2, n, at, size, dot_nt(d_gate, wgu[0, span, :]) + dot_nt(d_up, wgu[1, span, :]))
        scatter_start(2, n)
        out_copy(4, n).start()
        out_copy(6, n).start()
        out_copy(2, n).start()
        gather_drain(2, dffn, n)

    def attn_grad_in(n):
        d_a2 = scatter_end(2, n)
        grad, d_shift, d_scale = norm_back(x1s[n], d_a2, mod_row(n, 4))
        grad = grad + din[n].astype(F32)
        dxout[n] = grad
        dattn[n, 0:rows, :] = (mod_row(n, 2) * grad).astype(BF)
        gather_start(3, dattn, n)
        dmod[n, 2:3, :] = column_sum(grad * attns[n].astype(F32))
        dmod[n, 3:4, :] = d_shift
        dmod[n, 4:5, :] = d_scale

    def attn_grad_compute(n):
        gather_wait(3, dattn, n)
        staged_ready(7, n)
        grad = dattn[n]
        a1 = a1f[n]
        c, s = cosine[n], sine[n]
        lanes_all = heads * LANES
        for pair in range(heads // 2):
            span = pl.ds(pair * 2 * LANES, 2 * LANES)
            q2 = dot_nt(a1, wqkv[0, span, :])
            k2 = dot_nt(a1, wqkv[1, span, :])
            v2 = dot_nt(a1, wqkv[2, span, :]).astype(BF)
            d_mix2 = dot_nt(grad, wout[span, :]).astype(BF)
            for half in range(2):
                at = (pair * 2 + half) * LANES
                cut = slice(half * LANES, (half + 1) * LANES)
                q_gain, k_gain = gains[0:1, at : at + LANES], gains[1:2, at : at + LANES]
                q_inv, q_norm = head_norm(q2[:, cut])
                k_inv, k_norm = head_norm(k2[:, cut])
                q = turn(q_norm * q_gain, c, s).astype(BF)
                k = turn(k_norm * k_gain, c, s).astype(BF)
                v, d_mix = v2[:, cut], d_mix2[:, cut]
                probs = softmax(dot_nt(q, k) * SCALE)
                d_probs = dot_nt(d_mix, v)
                d_v = dot_tn(probs.astype(BF), d_mix)
                d_scores = (probs * (d_probs - jnp.sum(probs * d_probs, axis=-1, keepdims=True))).astype(BF)
                d_q = turn_back(dot(d_scores, k) * SCALE, c, s)
                d_k = turn_back(dot_tn(d_scores, q) * SCALE, c, s)
                gacc[0:1, at : at + LANES] += column_sum(d_q * q_norm)
                gacc[1:2, at : at + LANES] += column_sum(d_k * k_norm)
                d_q = d_q * q_gain
                d_k = d_k * k_gain
                d_q = q_inv * (d_q - q_norm * (jnp.sum(d_q * q_norm, axis=-1, keepdims=True) * (1.0 / HEAD_DIM)))
                d_k = k_inv * (d_k - k_norm * (jnp.sum(d_k * k_norm, axis=-1, keepdims=True) * (1.0 / HEAD_DIM)))
                dqkv_st[:, at : at + LANES] = d_q.astype(BF)
                dqkv_st[:, lanes_all + at : lanes_all + at + LANES] = d_k.astype(BF)
                dqkv_st[:, 2 * lanes_all + at : 2 * lanes_all + at + LANES] = d_v.astype(BF)
        for at, size in wide:
            span = pl.ds(at, size)
            total = dot(dqkv_st[:, 0:lanes_all], wqkv[0, :, span])
            total += dot(dqkv_st[:, lanes_all : 2 * lanes_all], wqkv[1, :, span])
            total += dot(dqkv_st[:, 2 * lanes_all : 3 * lanes_all], wqkv[2, :, span])
            scatter_put(3, n, at, size, total)
        scatter_start(3, n)
        out_copy(7, n).start()
        out_copy(3, n).start()
        gather_drain(3, dattn, n)

    def block_grad_out(n):
        d_a1 = scatter_end(3, n)
        grad, d_shift, d_scale = norm_back(xin[n].astype(F32), d_a1, mod_row(n, 1))
        grad = grad + dxout[n]
        dxout[n] = grad
        dmod[n, 0:1, :] = d_shift
        dmod[n, 1:2, :] = d_scale

        @pl.when(dec)
        def _():
            xin[n] = grad.astype(BF)
            dz_copy(n).start()

        @pl.when(enc)
        def _():
            send_dmod(n)

    works = (
        attn_in,
        lambda n: gather_relay(0, a1f, n),
        attn_compute,
        lambda n: scatter_middle(0, n),
        ffn_in,
        lambda n: gather_relay(1, a2f, n),
        ffn_compute,
        lambda n: scatter_middle(1, n),
        block_out,
        ffn_grad_in,
        lambda n: gather_relay(2, dffn, n),
        ffn_grad_compute,
        lambda n: scatter_middle(2, n),
        attn_grad_in,
        lambda n: gather_relay(3, dattn, n),
        attn_grad_compute,
        lambda n: scatter_middle(3, n),
        block_grad_out,
    )

    def run_work(work, n, low, high):
        if high - low == 1:
            works[low](n)
            return
        middle = (low + high) // 2

        @pl.when(work < middle)
        def _():
            run_work(work, n, low, middle)

        @pl.when(work >= middle)
        def _():
            run_work(work, n, middle, high)

    base = len(works) * images
    tables = [order_words(order, base) for order in ORDERS]

    def entry_of(i):
        rest, values = i, [low + section * (high - low) for low, high in zip(*tables)]
        while len(values) > 1:
            bit, rest = lax.rem(rest, 2), lax.div(rest, 2)
            values = [low + bit * (high - low) for low, high in zip(values[0::2], values[1::2])]
        return values[0]

    def word_step(i, carry):
        def work_step(_, word):
            entry, word = lax.rem(word, base), lax.div(word, base)
            work, n = lax.div(entry, images), lax.rem(entry, images)
            run_work(work, n, 0, len(works))
            return word

        lax.fori_loop(0, PACK, work_step, entry_of(i))
        return carry

    lax.fori_loop(0, base // PACK, word_step, 0)

    for which in (4, 5, 6, 7):
        out_copy(which, images - 1).wait()

    def drain(n, carry):
        for which in (0, 1, 2, 3):
            out_copy(which, n).wait()
        part = dmod[n, :, its_tiles(me)]
        for k in range(3):
            dmod_copy(k, n).wait()
            part += dmod_recv[k, n]
        dmod_part[n] = part.astype(BF)

        @pl.when(enc)
        def _():
            z_copy(n).wait_send()

        @pl.when(dec)
        def _():
            dz_copy(n).wait_send()

        return carry

    lax.fori_loop(0, images, drain, 0)


def run_main(tok, vel, mod_cols, cosine, sine, wqkv, wout, wgu, wdn, gains):
    images, rows, width = tok.shape
    tokens = 4 * rows
    lanes_all = wout.shape[0]
    heads = lanes_all // LANES
    hidden = wdn.shape[0]
    vmem = pl.BlockSpec(memory_space=pltpu.VMEM)
    anywhere = pl.BlockSpec(memory_space=pl.ANY)

    def hbm(last):
        return jax.ShapeDtypeStruct((images, tokens, last), BF)

    out_shape = (
        jax.ShapeDtypeStruct((images, rows, width), BF),
        jax.ShapeDtypeStruct((images, rows, width), F32),
        jax.ShapeDtypeStruct((images, 8, 3 * LANES), BF),
        jax.ShapeDtypeStruct((8, lanes_all), F32),
        jax.ShapeDtypeStruct((8, width), F32),
        hbm(width),
        hbm(width),
        hbm(width),
        hbm(width),
        hbm(hidden),
        hbm(lanes_all),
        hbm(2 * hidden),
        hbm(3 * lanes_all),
    )
    scratch = [
        pltpu.VMEM((images, rows, width), BF),
        pltpu.VMEM((images, rows, width), BF),
        pltpu.VMEM((images, tokens, width), BF),
        pltpu.VMEM((images, tokens, width), BF),
        pltpu.VMEM((images, tokens, width), BF),
        pltpu.VMEM((images, tokens, width), BF),
        pltpu.VMEM((images, rows, width), F32),
        pltpu.VMEM((images, rows, width), BF),
        pltpu.VMEM((images, rows, width), BF),
        pltpu.VMEM((4, KEEP, 2 * rows, width), F32),
        pltpu.VMEM((4, KEEP, 2 * rows, width), BF),
        pltpu.VMEM((4, SLOTS, 2 * rows, width), BF),
        pltpu.VMEM((4, KEEP, rows, width), BF),
        pltpu.VMEM((4, SLOTS, rows, width), BF),
        pltpu.VMEM((tokens, lanes_all), BF),
        pltpu.VMEM((tokens, hidden), BF),
        pltpu.VMEM((tokens, hidden), BF),
        pltpu.VMEM((tokens, 2 * hidden), BF),
        pltpu.VMEM((tokens, 3 * lanes_all), BF),
        pltpu.VMEM((images, 8, width), F32),
        pltpu.VMEM((3, images, 8, 3 * LANES), F32),
        pltpu.VMEM((images, 8, width), F32),
        pltpu.VMEM((3, images, 8, 3 * LANES), F32),
        pltpu.SemaphoreType.DMA((2, 3)),
        pltpu.SemaphoreType.DMA((2, 3, images)),
        pltpu.SemaphoreType.DMA((4, 6, images)),
        pltpu.SemaphoreType.DMA((4, 4, images)),
        pltpu.SemaphoreType.DMA((4, images)),
        pltpu.SemaphoreType.DMA((8, images)),
        pltpu.SemaphoreType.DMA((2,)),
    ]
    return pl.pallas_call(
        functools.partial(main_kernel, images, heads),
        out_shape=out_shape,
        in_specs=[anywhere, anywhere] + [vmem] * 8,
        out_specs=[vmem] * 5 + [anywhere] * 8,
        scratch_shapes=scratch,
        compiler_params=pltpu.CompilerParams(
            collective_id=0, has_side_effects=True, vmem_limit_bytes=62 * 2**20
        ),
    )(tok, vel, mod_cols, cosine, sine, wqkv, wout, wgu, wdn, gains)


def flat_plan(width, hidden, part):
    blocks = width // LANES
    segments = ((2 * hidden // LANES, width), (blocks, hidden), (blocks, 3 * part), (blocks, part))
    halves = [count * rows // 2 for count, rows in segments]
    half, chunk = sum(halves), width // 2
    assert half % chunk == 0

    def pieces(segment, block):
        rows, cut, at = segments[segment][1], halves[segment], sum(halves[:segment])
        low, high = block * rows, (block + 1) * rows
        if high <= cut:
            return [(at + low, 0, rows)]
        if low >= cut:
            return [(half + at + low - cut, 0, rows)]
        return [(at + low, 0, cut - low), (half + at, cut - low, high - cut)]

    return half, chunk, pieces


def tail_kernel(
    dp,
    a2_hbm,
    dgu_hbm,
    hid_hbm,
    dffn_hbm,
    a1_hbm,
    dqkv_hbm,
    mix_hbm,
    dattn_hbm,
    pick,
    summand,
    dmod_low,
    extra,
    totals,
    dmod_all,
    sum_all,
    extra_all,
    left_a,
    right_a,
    left_b,
    right_b,
    turned,
    own,
    arrived,
    sum_st,
    sum_recv,
    load_sems,
    part_sems,
    total_sems,
    sum_sems,
    all_sems,
    x_part_sems,
    x_total_sems,
    here,
):
    section = lax.axis_index("section")
    place = lax.axis_index("dp")
    me = lax.axis_index("tensor")
    sib = me + 1 - 2 * lax.rem(me, 2)
    across = lax.rem(me + 2, 4)
    enc, dec = section == 0, section == 1
    width, hidden = left_a.shape[1], left_b.shape[1]
    part, lanes_all = pick.shape
    half, chunk, pieces = flat_plan(width, hidden, part)
    whole = half // chunk
    count = jnp.where(enc, whole - LENT, whole + LENT)

    loads = [
        pltpu.make_async_copy(src, dst, load_sems.at[i])
        for i, (src, dst) in enumerate(
            (
                (a2_hbm, left_a),
                (dgu_hbm, right_a),
                (hid_hbm, left_b),
                (dffn_hbm, right_b),
                (mix_hbm, left_b.at[:, pl.ds(0, lanes_all)]),
                (a1_hbm, left_a),
                (dqkv_hbm, right_a),
                (dattn_hbm, right_b),
            )
        )
    ]
    for i in range(4):
        loads[i].start()

    barrier = pltpu.get_barrier_semaphore()
    for where in ({"tensor": sib}, {"tensor": across}):
        pl.semaphore_signal(barrier, inc=1, device_id=where, device_id_type=MESH)

    @pl.when(dec)
    def _():
        pl.semaphore_signal(barrier, inc=1, device_id={"section": 0}, device_id_type=MESH)

    for k in range(1, dp):
        pl.semaphore_signal(barrier, inc=1, device_id={"dp": lax.rem(place + k, dp)}, device_id_type=MESH)

    def put(segment, block, first, value):
        for at, low, size in pieces(segment, block):
            begin, end = max(low, first), min(low + size, first + value.shape[0])
            if begin < end:
                own[at + begin - low : at + end - low, :] = value[begin - first : end - first].astype(BF)

    def put_wide(segment, block, first, value):
        for i in range(value.shape[1] // LANES):
            put(segment, block + i, first, value[:, i * LANES : (i + 1) * LANES])

    def turn_left(ref):
        tokens, cols = ref.shape
        for at in range(0, tokens, 256):
            turned[0:cols, at : at + 256] = ref[at : at + 256, :].T

    def gate_up_blocks(*blocks):
        for block in blocks:
            value = dot(turned[...], right_a[:, block * LANES : (block + 2) * LANES])
            put_wide(0, block, 0, value)

    def qkv_heads(*pairs):
        kept = 2 * HEAD_DIM
        for pair in pairs:
            value = dot_tn(right_a[:, pair * 2 * LANES : (pair + 1) * 2 * LANES], left_a[...]).astype(BF)
            put_wide(2, 0, pair * kept, dot(pick[0:kept, 0 : 2 * LANES], value))

    def portion(i):
        tiles, gu_half = width // LANES, hidden // LANES
        pairs = 3 * lanes_all // (2 * LANES)
        if i == 0:
            loads[0].wait()
            turn_left(left_a)
            loads[5].start()
            loads[1].wait()
            gate_up_blocks(0, gu_half)
        elif i == 1:
            gate_up_blocks(2, gu_half + 2)
        elif i == 2:
            gate_up_blocks(*range(4, gu_half, 2), *range(gu_half + 4, 2 * gu_half, 2))
            loads[6].start()
        elif i == 3:
            loads[2].wait()
            turn_left(left_b)
            loads[4].start()
            loads[3].wait()
            for block in range(0, tiles, 2):
                cut = slice(block * LANES, min(width, (block + 2) * LANES))
                put_wide(1, block, 0, dot(turned[0:hidden, :], right_b[:, cut]))
            loads[7].start()
        elif i == 4:
            loads[5].wait()
            loads[6].wait()
            qkv_heads(*range(0, pairs // 2))
        elif i == 5:
            qkv_heads(*range(pairs // 2, pairs))
        elif i == 6:
            loads[4].wait()
            loads[7].wait()
            value = dot(pick[...], dot_tn(left_b[:, 0:lanes_all], right_b[...]).astype(BF))
            put_wide(3, 0, 0, value)

    def along(direction, onward):
        step = 1 if (direction == 0) == onward else dp - 1
        return {"dp": lax.rem(place + step, dp)}

    def behind(direction):
        return place if direction == 0 else dp - 1 - place

    def rows_of(direction, c):
        lent = 2 * half + (direction * LENT + c - whole) * chunk
        return pl.ds(pl.multiple_of(jnp.where(c < whole, direction * half + c * chunk, lent), chunk), chunk)

    def lent_copy(ref, sems, direction, i, to_decoder):
        mine = rows_of(direction, whole - LENT + i)
        theirs = rows_of(direction, whole + i)
        return pltpu.make_async_remote_copy(
            src_ref=ref.at[mine if to_decoder else theirs],
            dst_ref=ref.at[theirs if to_decoder else mine],
            send_sem=sems.at[direction, 0, i],
            recv_sem=sems.at[direction, 1, i],
            device_id={"section": 1 if to_decoder else 0},
            device_id_type=MESH,
        )

    def lent_part(direction, i):
        return lent_copy(own, x_part_sems, direction, i, True)

    def lent_total(direction, i):
        return lent_copy(totals, x_total_sems, direction, i, False)

    def part_copy(direction, c):
        return pltpu.make_async_remote_copy(
            src_ref=own.at[rows_of(direction, c)],
            dst_ref=arrived.at[rows_of(direction, c)],
            send_sem=part_sems.at[direction, 0, c],
            recv_sem=part_sems.at[direction, 1, c],
            device_id=along(direction, True),
            device_id_type=MESH,
        )

    def total_copy(direction, c):
        return pltpu.make_async_remote_copy(
            src_ref=totals.at[rows_of(direction, c)],
            dst_ref=totals.at[rows_of(direction, c)],
            send_sem=total_sems.at[direction, 0, c],
            recv_sem=total_sems.at[direction, 1, c],
            device_id=along(direction, False),
            device_id_type=MESH,
        )

    def add_part(direction, c):
        begins, ends = behind(direction) == 0, behind(direction) == dp - 1
        rows = rows_of(direction, c)

        @pl.when(c >= whole)
        def _():
            lent_part(direction, c - whole).wait_recv()

        @pl.when(begins)
        def _():
            part_copy(direction, c).start()

        @pl.when(jnp.logical_not(begins))
        def _():
            part_copy(direction, c).wait_recv()
            value = (own[rows, :].astype(F32) + arrived[rows, :].astype(F32)).astype(BF)

            @pl.when(ends)
            def _():
                totals[rows, :] = value
                total_copy(direction, c).start()

            @pl.when(jnp.logical_not(ends))
            def _():
                own[rows, :] = value
                part_copy(direction, c).start()

    def pass_total(direction, c):
        begins, ends = behind(direction) == 0, behind(direction) == dp - 1

        @pl.when(jnp.logical_not(ends))
        def _():
            total_copy(direction, c).wait_recv()

            @pl.when(jnp.logical_not(begins))
            def _():
                total_copy(direction, c).start()

        @pl.when(c >= whole)
        def _():
            lent_total(direction, c - whole).start()

    skew = 2

    def chunk_step(step):
        for direction in range(2):
            c = step - skew * behind(direction)

            @pl.when((c >= 0) & (c < count))
            def _():
                add_part(direction, c)

        for direction in range(2):
            u = step - skew * (2 * (dp - 1) - behind(direction))

            @pl.when((u >= 0) & (u < count))
            def _():
                pass_total(direction, u)

        for i in range(4):

            @pl.when(step == jnp.where(enc, 4, 12) + i)
            def _():
                small(i)

    def sum_copy(which):
        where = ({"section": 1 - section}, {"tensor": sib}, {"tensor": across})[which]
        height = (8, 16, 16)[which]
        src = summand if which == 0 else sum_st.at[which - 1]
        return pltpu.make_async_remote_copy(
            src_ref=src.at[pl.ds(0, height)],
            dst_ref=sum_recv.at[which, pl.ds(0, height)],
            send_sem=sum_sems.at[which, 0],
            recv_sem=sum_sems.at[which, 1],
            device_id=where,
            device_id_type=MESH,
        )

    def all_copy(which, k, outgoing):
        ref = (dmod_all, sum_all, extra_all)[which]
        peer = lax.rem(place + k, dp)
        slot = place if outgoing else peer
        return pltpu.make_async_remote_copy(
            src_ref=ref.at[slot],
            dst_ref=ref.at[slot],
            send_sem=all_sems.at[which, 0, k],
            recv_sem=all_sems.at[which, 1, slot],
            device_id={"dp": peer},
            device_id_type=MESH,
        )

    def small(step):
        if step == 0:
            dmod_all[place] = dmod_low[...]
            for k in range(1, dp):
                all_copy(0, k, True).start()

            @pl.when(dec)
            def _():
                pl.semaphore_wait(here, 1)

            sum_copy(0).start()
        elif step == 1:
            sum_copy(0).wait()
            sum_st[0] = summand[...]
            sum_st[0, 0:8, :] += sum_recv[0, 0:8, :]
            sum_copy(1).start()
        elif step == 2:
            sum_copy(1).wait()
            sum_st[1] = sum_st[0] + sum_recv[1]
            sum_copy(2).start()
        elif step == 3:
            sum_copy(2).wait()
            total = sum_st[1] + sum_recv[2]
            sum_all[place] = total.astype(BF)
            squares = total[8:16, 0:LANES]
            for i in range(1, width // LANES):
                squares += total[8:16, i * LANES : (i + 1) * LANES]
            extra_all[place, 0:8, :] = extra[...]
            extra_all[place, 8:16, :] = jnp.zeros_like(extra)
            extra_all[place, 8:16, 0:LANES] = squares
            for k in range(1, dp):
                all_copy(1, k, True).start()
                all_copy(2, k, True).start()

    portion(0)
    pl.semaphore_wait(barrier, jnp.where(enc, dp + 2, dp + 1))

    @pl.when(enc)
    def _():
        pl.semaphore_signal(here, inc=1, device_id={"section": 1}, device_id_type=MESH)

    for step in range(6):
        chunk_step(step)
        portion(step + 1)

    def lend(i, carry):
        for direction in range(2):
            lent_part(direction, i).start()
        return carry

    @pl.when(enc)
    def _():
        lax.fori_loop(0, LENT, lend, 0)

    def later_step(step, carry):
        chunk_step(step)
        return carry

    lax.fori_loop(6, whole + LENT + 2 * skew * (dp - 1), later_step, 0)

    def lent_back(i, carry):
        for direction in range(2):

            @pl.when(enc)
            def _():
                lent_part(direction, i).wait_send()
                lent_total(direction, i).wait_recv()

            @pl.when(dec)
            def _():
                lent_total(direction, i).wait_send()

        return carry

    lax.fori_loop(0, LENT, lent_back, 0)

    for which in range(3):
        for k in range(1, dp):
            all_copy(which, k, True).wait_send()
            all_copy(which, k, False).wait_recv()

    def drain(c, carry):
        for direction in range(2):

            @pl.when(behind(direction) != dp - 1)
            def _():
                part_copy(direction, c).wait_send()

            @pl.when(behind(direction) != 0)
            def _():
                total_copy(direction, c).wait_send()

        return carry

    lax.fori_loop(0, count, drain, 0)


def run_tail(dp, a2, dgu, hid, dffn, a1, dqkv, mix, dattn, pick, summand, dmod_low, extra):
    tokens, width = a2.shape
    hidden = hid.shape[1]
    vmem = pl.BlockSpec(memory_space=pltpu.VMEM)
    anywhere = pl.BlockSpec(memory_space=pl.ANY)
    half, chunk, _ = flat_plan(width, hidden, pick.shape[0])
    flat_rows, chunks = 2 * (half + LENT * chunk), half // chunk + LENT
    return pl.pallas_call(
        functools.partial(tail_kernel, dp),
        out_shape=(
            jax.ShapeDtypeStruct((flat_rows, LANES), BF),
            jax.ShapeDtypeStruct((dp,) + dmod_low.shape, BF),
            jax.ShapeDtypeStruct((dp,) + summand.shape, BF),
            jax.ShapeDtypeStruct((dp, 16, extra.shape[1]), F32),
        ),
        in_specs=[anywhere] * 8 + [vmem] * 4,
        out_specs=[vmem] * 4,
        scratch_shapes=[
            pltpu.VMEM((tokens, width), BF),
            pltpu.VMEM((tokens, dgu.shape[1]), BF),
            pltpu.VMEM((tokens, hidden), BF),
            pltpu.VMEM((tokens, width), BF),
            pltpu.VMEM((width, tokens), BF),
            pltpu.VMEM((flat_rows, LANES), BF),
            pltpu.VMEM((flat_rows, LANES), BF),
            pltpu.VMEM((2,) + summand.shape, F32),
            pltpu.VMEM((3,) + summand.shape, F32),
            pltpu.SemaphoreType.DMA((8,)),
            pltpu.SemaphoreType.DMA((2, 2, chunks)),
            pltpu.SemaphoreType.DMA((2, 2, chunks)),
            pltpu.SemaphoreType.DMA((3, 2)),
            pltpu.SemaphoreType.DMA((3, 2, dp)),
            pltpu.SemaphoreType.DMA((2, 2, LENT)),
            pltpu.SemaphoreType.DMA((2, 2, LENT)),
            pltpu.SemaphoreType.REGULAR,
        ],
        compiler_params=pltpu.CompilerParams(
            collective_id=1, has_side_effects=True, vmem_limit_bytes=62 * 2**20
        ),
    )(a2, dgu, hid, dffn, a1, dqkv, mix, dattn, pick, summand, dmod_low, extra)


def finish_kernel(
    flat_hbm, gu_hbm, down_hbm, qkv_hbm, out_hbm, flat, gate_up, down, qkv, out, load_sems, store_sems
):
    width, hidden = gate_up.shape[1], gate_up.shape[2]
    part, blocks, hidden_blocks = out.shape[0], width // LANES, hidden // LANES
    _, _, pieces = flat_plan(width, hidden, part)
    groups = (
        [(0, b) for b in range(hidden_blocks)],
        [(0, hidden_blocks + b) for b in range(hidden_blocks)],
        [(1, b) for b in range(blocks)],
        [(2, b) for b in range(blocks)],
        [(3, b) for b in range(blocks)],
    )
    loads = []
    for group in groups:
        spans = []
        for segment, block in group:
            for at, _, size in pieces(segment, block):
                if spans and spans[-1][0] + spans[-1][1] == at:
                    spans[-1][1] += size
                else:
                    spans.append([at, size])
        copies = []
        for at, size in spans:
            rows = pl.ds(at, size)
            sem = load_sems.at[len(loads), len(copies)]
            copies.append(pltpu.make_async_copy(flat_hbm.at[rows], flat.at[rows], sem))
            copies[-1].start()
        loads.append(copies)
    stores = (
        pltpu.make_async_copy(gate_up.at[0], gu_hbm.at[0], store_sems.at[0]),
        pltpu.make_async_copy(gate_up.at[1], gu_hbm.at[1], store_sems.at[1]),
        pltpu.make_async_copy(down, down_hbm, store_sems.at[2]),
        pltpu.make_async_copy(qkv, qkv_hbm, store_sems.at[3]),
        pltpu.make_async_copy(out, out_hbm, store_sems.at[4]),
    )
    for i, group in enumerate(groups):
        for copy in loads[i]:
            copy.wait()
        for segment, block in group:
            for at, low, size in pieces(segment, block):
                value = flat[at : at + size, :].astype(F32)
                rows = slice(low, low + size)
                cols = slice(block * LANES, (block + 1) * LANES)
                if segment == 0:
                    local = block % hidden_blocks
                    gate_up[block // hidden_blocks, rows, local * LANES : (local + 1) * LANES] = value
                elif segment == 1:
                    down[rows, cols] = value
                elif segment == 2:
                    qkv[rows, cols] = value
                else:
                    out[rows, cols] = value
        stores[i].start()
    for copy in stores:
        copy.wait()


def run_finish(flat, width, hidden, part):
    anywhere = pl.BlockSpec(memory_space=pl.ANY)
    shapes = ((2, width, hidden), (hidden, width), (3 * part, width), (part, width))
    return pl.pallas_call(
        finish_kernel,
        out_shape=tuple(jax.ShapeDtypeStruct(shape, F32) for shape in shapes),
        in_specs=[anywhere],
        out_specs=[anywhere] * 4,
        scratch_shapes=[pltpu.VMEM(flat.shape, BF)]
        + [pltpu.VMEM(shape, F32) for shape in shapes]
        + [pltpu.SemaphoreType.DMA((5, 2)), pltpu.SemaphoreType.DMA((5,))],
        compiler_params=pltpu.CompilerParams(vmem_limit_bytes=48 * 2**20),
    )(flat)


def time_embed(bin_row, feature_count):
    halfway = feature_count // 2
    frequency = jnp.exp(-math.log(10000.0) * jnp.arange(halfway, dtype=F32) / halfway)
    moment = (bin_row.astype(F32) + 0.5) * (1000.0 / NBINS)
    angles = moment[:, None] * frequency[None, :]
    return jnp.concatenate([jnp.cos(angles), jnp.sin(angles)], axis=-1)


def per_device(
    tokens,
    velocity_grad,
    bins,
    labels,
    places,
    class_table,
    mod_weight,
    qkv_weight,
    out_weight,
    gate_up_weight,
    down_weight,
    q_gain,
    k_gain,
):
    micro, per_micro, rows, width = tokens.shape
    images = micro * per_micro
    dp = lax.axis_size("dp")
    me = lax.axis_index("tensor")
    heads = q_gain.shape[1] // HEAD_DIM
    select = jnp.asarray(head_select(heads), BF)

    def condition(bin_row, label_row):
        one_hot = label_row[:, None] == jnp.arange(class_table.shape[0], dtype=jnp.int32)[None, :]
        picked = jnp.dot(one_hot.astype(BF), class_table, preferred_element_type=F32)
        return time_embed(bin_row, width) + picked, one_hot

    cond, _ = condition(bins.reshape(images), labels.reshape(images))
    silu_low = jax.nn.silu(cond).astype(BF)
    mod_w = mod_weight[0]
    part = width // 4
    columns = jnp.einsum("id,djf->ijf", silu_low, mod_w, preferred_element_type=F32)
    shift = me * (part - 2 * LANES)
    mod_cols = lax.dynamic_update_slice(jnp.zeros((images, 8, 3 * LANES), F32), columns, (0, 0, shift))

    order = jnp.stack([me, (me + 2) % 4, me + 1 - 2 * (me % 2), (me + 2) % 4 + 1 - 2 * (me % 2)])
    placed = jnp.take(places.reshape(images, 4, rows), order, axis=1).reshape(images * 4 * rows)
    grid = jnp.arange(GRID, dtype=jnp.int32)[None, :]
    marks = jnp.concatenate([placed[:, None] // GRID == grid, placed[:, None] % GRID == grid], axis=1).astype(F32)
    angles = jnp.dot(marks, jnp.asarray(angle_table()), precision=lax.Precision.HIGHEST)
    angles = angles.reshape(images, 4 * rows, 2 * LANES)

    wqkv = jnp.einsum("ef,jde->jfd", select, qkv_weight[0], preferred_element_type=F32).astype(BF)
    wout = jnp.einsum("ef,ed->fd", select, out_weight[0], preferred_element_type=F32).astype(BF)
    gains = jnp.dot(jnp.concatenate([q_gain, k_gain], axis=0), select, preferred_element_type=F32)

    results = run_main(
        tokens.reshape(images, rows, width),
        velocity_grad.reshape(images, rows, width),
        mod_cols,
        angles[..., :LANES],
        angles[..., LANES:],
        wqkv,
        wout,
        gate_up_weight[0],
        down_weight[0],
        gains,
    )
    z_rows, dx_rows, dmod_part, gain_sums, squares, a1, a2, d_ffn, d_attn, units, mixed, d_gu, d_qkv = results

    dmod_mine = lax.dynamic_slice(dmod_part, (0, 0, shift), (images, 6, part))
    grad_silu = jnp.einsum("ijf,djf->id", dmod_mine, mod_w, preferred_element_type=F32)
    sig = jax.nn.sigmoid(cond)
    grad_cond = grad_silu * (sig + cond * sig * (1.0 - sig))
    summand = jnp.concatenate([grad_cond, squares], axis=0)
    lanes_all = heads * LANES
    numbers = jnp.stack([bins.reshape(images), labels.reshape(images)]).astype(F32)
    extra = jnp.concatenate([gain_sums[0:2], jnp.pad(numbers, ((0, 4), (0, lanes_all - images)))], axis=0)

    flat = images * 4 * rows
    flat_grads, dmod_all, sum_all, extra_all = run_tail(
        dp,
        a2.reshape(flat, width),
        d_gu.reshape(flat, d_gu.shape[2]),
        units.reshape(flat, units.shape[2]),
        d_ffn.reshape(flat, width),
        a1.reshape(flat, width),
        d_qkv.reshape(flat, d_qkv.shape[2]),
        mixed.reshape(flat, lanes_all),
        d_attn.reshape(flat, width),
        select,
        summand,
        dmod_part.reshape(images * 8, 3 * LANES),
        extra,
    )
    finished = run_finish(flat_grads, width, units.shape[2], part)
    gate_up_grad, down_grad, out_grad = finished[0][None], finished[1][None], finished[3][None]
    qkv_grad = jnp.transpose(finished[2].reshape(3, part, width), (0, 2, 1))[None]

    gains_sum = jnp.sum(extra_all[:, 0:2], axis=0)
    gains_sum = jnp.einsum("jf,ef->je", gains_sum, select.astype(F32), precision=lax.Precision.HIGHEST)
    bins_all = extra_all[:, 2, :images].reshape(dp * images).astype(jnp.int32)
    labels_all = extra_all[:, 3, :images].reshape(dp * images).astype(jnp.int32)
    cond_all, one_hot = condition(bins_all, labels_all)
    silu_all = jax.nn.silu(cond_all).astype(BF)
    dmod_all = lax.dynamic_slice(
        dmod_all.reshape(dp * images, 8, 3 * LANES), (0, 0, shift), (dp * images, 6, part)
    )
    mod_grad = jnp.einsum("id,ijf->djf", silu_all, dmod_all, preferred_element_type=F32)[None]
    grad_cond_all = sum_all[:, 0:8].reshape(dp * images, width)
    class_grad = jnp.dot(one_hot.astype(BF).T, grad_cond_all, preferred_element_type=F32)
    square_totals = jnp.sum(extra_all[:, 8:11, 0:LANES], axis=(0, 2))
    count = images * rows * width * dp * lax.axis_size("tensor")
    stats = jnp.sqrt(square_totals / count)[None, :]
    whole = (1, micro, per_micro, rows, width)
    return (
        z_rows.reshape(whole),
        dx_rows.reshape(whole),
        mod_grad,
        qkv_grad,
        out_grad,
        gate_up_grad,
        down_grad,
        gains_sum[0:1],
        gains_sum[1:2],
        class_grad,
        stats,
    )


def solution(mesh):
    return jax.shard_map(
        per_device,
        mesh=mesh,
        in_specs=(
            P(None, "dp", "tensor", None),
            P(None, "dp", "tensor", None),
            P(None, "dp"),
            P(None, "dp"),
            P(None, "dp", None),
            P(),
            P("section", None, None, "tensor"),
            P("section", None, None, "tensor"),
            P("section", "tensor", None),
            P("section", None, None, "tensor"),
            P("section", "tensor", None),
            P("section", "tensor"),
            P("section", "tensor"),
        ),
        out_specs=(
            P("section", None, "dp", "tensor", None),
            P("section", None, "dp", "tensor", None),
            P("section", None, None, "tensor"),
            P("section", None, None, "tensor"),
            P("section", "tensor", None),
            P("section", None, None, "tensor"),
            P("section", "tensor", None),
            P("section", "tensor"),
            P("section", "tensor"),
            P(),
            P("section", None),
        ),
        check_vma=False,
    )
```

```python
import functools
import math

import jax
import jax.numpy as jnp
import numpy as np
from jax import lax
from jax.experimental import pallas as pl
from jax.experimental.pallas import tpu as pltpu
from jax.sharding import PartitionSpec as P

MESH = pl.DeviceIdType.MESH
HEAD_DIM = 72
LANES = 128
NBINS = 1000
GRID = 16
EPS = 1e-06
BF = jnp.bfloat16
F32 = jnp.float32
SCALE = HEAD_DIM**-0.5
LOG2E = math.log2(math.e)

KEEP, SLOTS, PACK = 2, 4, 4
LENT = 4
ORDERS = (
    (
        0, 1, 8, 2, 3, 16, 9, 24, 10, 4, 17, 32, 11, 25, 18, 40, 26, 48, 33,
        56, 19, 34, 12, 41, 64, 49, 27, 57, 42, 144, 50, 35, 65, 58, 20, 43, 5, 145,
        66, 28, 51, 13, 146, 59, 36, 6, 21, 67, 44, 52, 60, 147, 14, 7, 29, 68, 22,
        15, 37, 148, 30, 23, 38, 31, 45, 53, 61, 39, 46, 54, 69, 62, 149, 70, 47, 72,
        55, 80, 63, 150, 88, 71, 151, 96, 104, 73, 81, 89, 112, 74, 97, 120, 82, 128, 105,
        90, 136, 98, 113, 75, 121, 83, 106, 91, 114, 129, 99, 122, 76, 130, 137, 107, 84, 92,
        77, 115, 100, 138, 123, 78, 85, 108, 93, 86, 79, 131, 94, 116, 101, 102, 124, 87, 109,
        132, 95, 139, 117, 103, 110, 125, 111, 140, 133, 118, 126, 119, 141, 134, 127, 135, 142, 143,
    ),
    (
        72, 73, 74, 80, 75, 81, 82, 76, 83, 77, 0, 8, 78, 16, 1, 24, 84, 9, 32,
        79, 17, 40, 85, 2, 25, 88, 10, 33, 48, 56, 18, 96, 41, 3, 86, 26, 89, 11,
        104, 97, 19, 4, 64, 112, 34, 27, 49, 120, 42, 105, 57, 90, 12, 113, 35, 98, 20,
        65, 128, 43, 121, 28, 50, 106, 136, 91, 5, 36, 13, 129, 114, 58, 99, 21, 122, 44,
        51, 66, 29, 59, 130, 6, 92, 14, 37, 107, 22, 7, 137, 67, 138, 30, 15, 87, 52,
        60, 45, 100, 115, 23, 38, 123, 31, 108, 93, 53, 131, 46, 68, 61, 39, 94, 116, 139,
        101, 102, 124, 47, 69, 109, 132, 95, 117, 144, 110, 103, 125, 140, 54, 133, 145, 118, 146,
        55, 111, 62, 126, 141, 119, 134, 63, 127, 147, 135, 142, 148, 70, 149, 71, 150, 143, 151,
    ),
)


def lane_of():
    quarter = HEAD_DIM // 4
    lanes = np.zeros((HEAD_DIM,), np.int64)
    for half in range(2):
        for part in range(2):
            for i in range(quarter):
                lanes[half * 2 * quarter + part * quarter + i] = part * 64 + half * quarter + i
    return lanes


def head_select(heads):
    select = np.zeros((heads * HEAD_DIM, heads * LANES), np.float32)
    lanes = lane_of()
    for h in range(heads):
        for f in range(HEAD_DIM):
            select[h * HEAD_DIM + f, h * LANES + lanes[f]] = 1.0
    return select


def angle_table():
    quarter = HEAD_DIM // 4
    frequency = (10000.0 ** (-np.arange(quarter, dtype=np.float32) / np.float32(quarter))).astype(np.float32)
    lanes = lane_of().reshape(2, 2, quarter)
    table = np.zeros((2 * GRID, 2 * LANES), np.float32)
    for place in range(GRID):
        angle = np.float32(place) * frequency
        for half in range(2):
            for part in range(2):
                sign = -1.0 if part == 0 else 1.0
                table[half * GRID + place, lanes[half, part]] = np.cos(angle)
                table[half * GRID + place, LANES + lanes[half, part]] = sign * np.sin(angle)
    return table


def dot(a, b):
    return lax.dot_general(a, b, (((1,), (0,)), ((), ())), preferred_element_type=F32)


def dot_nt(a, b):
    return lax.dot_general(a, b, (((1,), (1,)), ((), ())), preferred_element_type=F32)


def dot_tn(a, b):
    return lax.dot_general(a, b, (((0,), (0,)), ((), ())), preferred_element_type=F32)


def order_words(order, base):
    words = []
    for at in range(0, len(order), PACK):
        words.append(sum(entry * base**i for i, entry in enumerate(order[at : at + PACK])))
    while len(words) & (len(words) - 1):
        words.append(0)
    return words


def chunks_of(size, width):
    return [(at, min(width, size - at)) for at in range(0, size, width)]


def main_kernel(
    images,
    heads,
    tok,
    vel,
    mod_cols,
    turns,
    qkv_hbm,
    out_hbm,
    wgu_hbm,
    wdn_hbm,
    q_gain,
    k_gain,
    select,
    zout,
    dxout,
    dmod_part,
    gacc,
    sacc,
    a1_hbm,
    a2_hbm,
    dffn_hbm,
    dattn_hbm,
    hid_hbm,
    mix_hbm,
    dgu_hbm,
    dqkv_hbm,
    wqkv,
    wout,
    wgu,
    wdn,
    gains,
    xin,
    din,
    a1f,
    a2f,
    dffn,
    dattn,
    x1s,
    attns,
    ffns,
    keep,
    send_a,
    recv_a,
    send_y,
    recv_y,
    mix_st,
    units_st,
    hid_st,
    dgu_st,
    dqkv_st,
    mod,
    mod_recv,
    dmod,
    dmod_sum,
    mod_sems,
    dmod_sems,
    ag_sems,
    rs_sems,
    zx_sems,
    out_sems,
    in_sems,
):
    rows = tok.shape[1]
    width = tok.shape[2]
    hidden = wdn.shape[0]
    wide = chunks_of(width, 512)
    section = lax.axis_index("section")
    me = lax.axis_index("tensor")
    sib = me + 1 - 2 * lax.rem(me, 2)
    across = lax.rem(me + 2, 4)
    diag = lax.rem(sib + 2, 4)
    peers = (sib, across, diag)
    other = 1 - section
    enc = section == 0
    dec = section == 1

    load_x = pltpu.make_async_copy(tok, xin, in_sems.at[0])
    load_d = pltpu.make_async_copy(vel, din, in_sems.at[1])
    tokens, part = dattn.shape[1], out_hbm.shape[0]
    groups = [qkv_hbm.at[j] for j in range(3)] + [out_hbm]
    load_w = [
        pltpu.make_async_copy(wgu_hbm, wgu, in_sems.at[2]),
        pltpu.make_async_copy(wdn_hbm, wdn, in_sems.at[3]),
    ]
    load_raw = []
    for j, group in enumerate(groups):
        for i, (at, size) in enumerate(((0, tokens), (tokens, part - tokens))):
            src, dst = group.at[pl.ds(at, size)], dattn.at[2 * j + i, pl.ds(0, size)]
            load_raw.append(pltpu.make_async_copy(src, dst, in_sems.at[4 + 2 * j + i]))
    for copy in load_raw:
        copy.start()

    @pl.when(enc)
    def _():
        load_x.start()

    @pl.when(dec)
    def _():
        load_d.start()

    barrier = pltpu.get_barrier_semaphore()
    pl.semaphore_signal(barrier, inc=1, device_id={"tensor": sib}, device_id_type=MESH)
    pl.semaphore_signal(barrier, inc=1, device_id={"tensor": across}, device_id_type=MESH)
    pl.semaphore_signal(barrier, inc=1, device_id={"tensor": diag}, device_id_type=MESH)
    pl.semaphore_signal(barrier, inc=1, device_id={"section": other}, device_id_type=MESH)

    mod[...] = jnp.zeros_like(mod)
    gacc[...] = jnp.zeros_like(gacc)
    sacc[...] = jnp.zeros_like(sacc)
    dmod[...] = jnp.zeros_like(dmod)

    pl.semaphore_wait(barrier, 4)

    def remote(src, dst, send_sem, recv_sem, where):
        return pltpu.make_async_remote_copy(
            src_ref=src, dst_ref=dst, send_sem=send_sem, recv_sem=recv_sem, device_id=where, device_id_type=MESH
        )

    def its_tiles(device):
        return pl.ds(pl.multiple_of(device * (2 * LANES), LANES), 3 * LANES)

    def mod_copy(k):
        return remote(mod_cols, mod_recv.at[k], mod_sems.at[0, k], mod_sems.at[1, k], {"tensor": peers[k]})

    def dmod_copy(k, n):
        return remote(
            dmod.at[n, :, its_tiles(peers[k])],
            mod_recv.at[k, n],
            dmod_sems.at[0, k, n],
            dmod_sems.at[1, k, n],
            {"tensor": peers[k]},
        )

    for k in (1, 2, 0):
        mod_copy(k).start()
    for copy in load_w:
        copy.start()
    mod[:, :, its_tiles(me)] = mod_cols[...]

    gains[0:1, :] = dot(q_gain[...], select[...])
    gains[1:2, :] = dot(k_gain[...], select[...])
    for j in range(4):
        load_raw[2 * j].wait()
        load_raw[2 * j + 1].wait()
        ref = wqkv.at[j] if j < 3 else wout
        for at, size in wide:
            span = pl.ds(at, size)
            value = dot_tn(select[0:tokens, :], dattn[2 * j, :, span])
            value += dot_tn(select[tokens:part, :], dattn[2 * j + 1, 0 : part - tokens, span])
            ref[:, span] = value.astype(BF)

    @pl.when(enc)
    def _():
        load_x.wait()

    @pl.when(dec)
    def _():
        load_d.wait()

    for k in range(3):
        mod_copy(k).wait()
        mod[:, :, its_tiles(peers[k])] += mod_recv[k]

    def gather(which, buf, n, kind):
        src, dst, where = ((0, rows, across), (0, 2 * rows, sib), (rows, 3 * rows, sib))[kind]
        return remote(
            buf.at[n, pl.ds(src, rows)],
            buf.at[n, pl.ds(dst, rows)],
            ag_sems.at[which, 2 * kind, n],
            ag_sems.at[which, 2 * kind + 1, n],
            {"tensor": where},
        )

    def gather_start(which, buf, n):
        gather(which, buf, n, 0).start()
        gather(which, buf, n, 1).start()

    def gather_relay(which, buf, n):
        gather(which, buf, n, 0).wait_recv()
        gather(which, buf, n, 2).start()

    def attn_relay(n):
        @pl.when(enc)
        def _():
            gather(0, a1f, n, 0).wait_recv()

        @pl.when(dec)
        def _():
            zy_pass(n).wait_recv()
            values = a1f[n, rows : 2 * rows, :].astype(F32)
            a1f[n, rows : 2 * rows, :] = modulated(values, mod_row(n, 0), mod_row(n, 1)).astype(BF)

        gather(0, a1f, n, 2).start()

    def gather_wait(which, buf, n):
        gather(which, buf, n, 1).wait_recv()
        gather(which, buf, n, 2).wait_recv()

    def gather_drain(which, buf, n):
        for kind in range(3):
            gather(which, buf, n, kind).wait_send()

    def to_sibling(which, n):
        return remote(
            send_a.at[which, lax.rem(n, KEEP)],
            recv_a.at[which, lax.rem(n, SLOTS)],
            rs_sems.at[which, 0, n],
            rs_sems.at[which, 1, n],
            {"tensor": sib},
        )

    def over_y(which, n):
        return remote(
            send_y.at[which, lax.rem(n, KEEP)],
            recv_y.at[which, lax.rem(n, SLOTS)],
            rs_sems.at[which, 2, n],
            rs_sems.at[which, 3, n],
            {"tensor": across},
        )

    def scatter_put(which, n, at, size, values):
        kind, own = which, lax.rem(n, KEEP)
        keep[kind, own, :, pl.ds(at, size)] = values[0 : 2 * rows]
        send_a[kind, own, :, pl.ds(at, size)] = values[2 * rows : 4 * rows].astype(BF)

    def scatter_start(which, n):
        to_sibling(which, n).start()

    def scatter_middle(which, n):
        kind, own, slot = which, lax.rem(n, KEEP), lax.rem(n, SLOTS)
        to_sibling(which, n).wait()
        theirs = recv_a[kind, slot, rows : 2 * rows].astype(F32)
        send_y[kind, own] = (keep[kind, own, rows : 2 * rows] + theirs).astype(BF)
        over_y(which, n).start()

    def scatter_end(which, n):
        kind, own, slot = which, lax.rem(n, KEEP), lax.rem(n, SLOTS)
        over_y(which, n).wait()
        mine = keep[kind, own, 0:rows] + recv_a[kind, slot, 0:rows].astype(F32)
        return mine + recv_y[kind, slot].astype(F32)

    def z_copy(n):
        return remote(zout.at[n], xin.at[n], zx_sems.at[0, n], zx_sems.at[1, n], {"section": other})

    def zy_copy(n):
        return remote(
            zout.at[n], dattn.at[n, pl.ds(rows, rows)], zx_sems.at[4, n], zx_sems.at[5, n], {"tensor": across}
        )

    def zy_pass(n):
        return remote(
            dattn.at[n, pl.ds(rows, rows)],
            a1f.at[n, pl.ds(rows, rows)],
            zx_sems.at[6, n],
            zx_sems.at[7, n],
            {"section": other},
        )

    def dz_copy(n):
        return remote(xin.at[n], din.at[n], zx_sems.at[2, n], zx_sems.at[3, n], {"section": other})

    def mod_row(n, row):
        return mod[n, pl.ds(row, 1), :]

    def inverse_rms(values):
        return lax.rsqrt(jnp.mean(values * values, axis=-1, keepdims=True) + EPS)

    def column_sum(values):
        return jnp.sum(values, axis=0, keepdims=True)

    def modulated(values, shift, scale):
        return (values * inverse_rms(values)) * (1.0 + scale) + shift

    def norm_back(values, grad, scale):
        inv = inverse_rms(values)
        normed = values * inv
        d_normed = grad * (1.0 + scale)
        d_values = inv * (d_normed - normed * jnp.mean(d_normed * normed, axis=-1, keepdims=True))
        return d_values, column_sum(grad), column_sum(grad * normed)

    def head_norm(raw):
        inv = lax.rsqrt(jnp.sum(raw * raw, axis=-1, keepdims=True) * (1.0 / HEAD_DIM) + EPS)
        return inv, raw * inv

    def turn(values, c, s):
        return values * c + pltpu.roll(values, 64, 1) * s

    def turn_back(values, c, s):
        return values * c - pltpu.roll(values, 64, 1) * s

    def softmax_parts(scaled, k):
        powered = jnp.exp2(dot_nt(scaled, k))
        return powered, 1.0 / jnp.sum(powered, axis=-1, keepdims=True)

    def out_copy(which, n):
        src = (a1f, a2f, dffn, dattn, hid_st, mix_st, dgu_st, dqkv_st)[which]
        dst = (a1_hbm, a2_hbm, dffn_hbm, dattn_hbm, hid_hbm, mix_hbm, dgu_hbm, dqkv_hbm)[which]
        return pltpu.make_async_copy(src.at[n] if which < 4 else src, dst.at[n], out_sems.at[which, n])

    def staged_ready(which, n):
        @pl.when(n > 0)
        def _():
            out_copy(which, n - 1).wait()

    def attn_in(n):
        @pl.when(dec)
        def _():
            z_copy(n).wait_recv()

        values = xin[n].astype(F32)
        sacc[0:1, :] += column_sum(values * values)
        a1f[n, 0:rows, :] = modulated(values, mod_row(n, 0), mod_row(n, 1)).astype(BF)

        @pl.when(enc)
        def _():
            gather(0, a1f, n, 0).start()

        gather(0, a1f, n, 1).start()

    def attn_compute(n):
        gather_wait(0, a1f, n)
        staged_ready(5, n)
        a1 = a1f[n]
        c, s = turns[n, :, 0:LANES], turns[n, :, LANES : 2 * LANES]
        for pair in range(heads // 2):
            span = pl.ds(pair * 2 * LANES, 2 * LANES)
            q2 = dot_nt(a1, wqkv[0, span, :])
            k2 = dot_nt(a1, wqkv[1, span, :])
            v2 = dot_nt(a1, wqkv[2, span, :]).astype(BF)
            for half in range(2):
                at = (pair * 2 + half) * LANES
                cut = slice(half * LANES, (half + 1) * LANES)
                q_gain = gains[0:1, at : at + LANES] * (SCALE * LOG2E)
                q = turn(head_norm(q2[:, cut])[1] * q_gain, c, s).astype(BF)
                k = turn(head_norm(k2[:, cut])[1] * gains[1:2, at : at + LANES], c, s).astype(BF)
                powered, inverse = softmax_parts(q, k)
                mix_st[:, at : at + LANES] = (dot(powered.astype(BF), v2[:, cut]) * inverse).astype(BF)
        mixed = mix_st[...]
        for at, size in wide:
            scatter_put(0, n, at, size, dot(mixed, wout[:, pl.ds(at, size)]))
        scatter_start(0, n)
        out_copy(5, n).start()
        out_copy(0, n).start()
        gather(0, a1f, n, 1).wait_send()
        gather(0, a1f, n, 2).wait_send()

        @pl.when(enc)
        def _():
            gather(0, a1f, n, 0).wait_send()

    def ffn_in(n):
        attended = scatter_end(0, n)
        attns[n] = attended.astype(BF)
        values = xin[n].astype(F32) + mod_row(n, 2) * attended
        x1s[n] = values
        sacc[1:2, :] += column_sum(values * values)
        a2f[n, 0:rows, :] = modulated(values, mod_row(n, 3), mod_row(n, 4)).astype(BF)
        gather_start(1, a2f, n)

    def ffn_down(n, units):
        for at, size in wide:
            scatter_put(1, n, at, size, dot(units, wdn[:, pl.ds(at, size)]))
        scatter_start(1, n)
        out_copy(1, n).start()
        gather_drain(1, a2f, n)

    def first_ffn(n):
        gather_wait(1, a2f, n)

        @pl.when(n == 0)
        def _():
            load_w[0].wait()
            load_w[1].wait()

    def ffn_compute(n):
        @pl.when(enc)
        def _():
            first_ffn(n)
            a2 = a2f[n]
            for at, size in chunks_of(hidden, 256):
                span = pl.ds(at, size)
                gate_val = dot(a2, wgu[0, :, span])
                up_val = dot(a2, wgu[1, :, span])
                units_st[:, span] = (gate_val * jax.nn.sigmoid(gate_val) * up_val).astype(BF)
            ffn_down(n, units_st[...])

    def block_out(n):
        feedfwd = scatter_end(1, n)
        ffns[n] = feedfwd.astype(BF)
        values = x1s[n] + mod_row(n, 5) * feedfwd
        sacc[2:3, :] += column_sum(values * values)
        zout[n] = values.astype(BF)

        @pl.when(enc)
        def _():
            z_copy(n).start()
            zy_copy(n).start()

        @pl.when(dec)
        def _():
            dmod[n, 5:6, :] = column_sum(din[n].astype(F32) * feedfwd)

    def pass_on(n):
        @pl.when(enc)
        def _():
            zy_copy(n).wait_recv()
            zy_pass(n).start()

        @pl.when(dec)
        def _():
            send_dmod(n)

    def send_dmod(n):
        for k in range(3):
            dmod_copy(k, n).start()

    def ffn_grad_in(n):
        @pl.when(enc)
        def _():
            zy_copy(n).wait_send()
            zy_pass(n).wait_send()
            dz_copy(n).wait_recv()

        grad = din[n].astype(F32)
        dffn[n, 0:rows, :] = (mod_row(n, 5) * grad).astype(BF)
        gather_start(2, dffn, n)

        @pl.when(enc)
        def _():
            dmod[n, 5:6, :] = column_sum(grad * ffns[n].astype(F32))

    def ffn_grad_compute(n):
        @pl.when(dec)
        def _():
            first_ffn(n)

        gather_wait(2, dffn, n)
        staged_ready(4, n)
        staged_ready(6, n)
        grad = dffn[n]
        a2 = a2f[n]
        for at, size in chunks_of(hidden, 256):
            span = pl.ds(at, size)
            gate_val = dot(a2, wgu[0, :, span])
            up_val = dot(a2, wgu[1, :, span])
            d_hidden = dot_nt(grad, wdn[span, :])
            sig = jax.nn.sigmoid(gate_val)
            act = gate_val * sig
            hid_st[:, span] = (act * up_val).astype(BF)
            dgu_st[:, span] = (d_hidden * up_val * (sig + act * (1.0 - sig))).astype(BF)
            dgu_st[:, pl.ds(hidden + at, size)] = (d_hidden * act).astype(BF)
        d_gate = dgu_st[:, 0:hidden]
        d_up = dgu_st[:, hidden : 2 * hidden]
        for at, size in wide:
            span = pl.ds(at, size)
            scatter_put(2, n, at, size, dot_nt(d_gate, wgu[0, span, :]) + dot_nt(d_up, wgu[1, span, :]))
        scatter_start(2, n)

        @pl.when(dec)
        def _():
            ffn_down(n, hid_st[...])

        out_copy(4, n).start()
        out_copy(6, n).start()
        out_copy(2, n).start()
        gather_drain(2, dffn, n)

    def attn_grad_in(n):
        d_a2 = scatter_end(2, n)
        grad, d_shift, d_scale = norm_back(x1s[n], d_a2, mod_row(n, 4))
        grad = grad + din[n].astype(F32)
        dxout[n] = grad
        dattn[n, 0:rows, :] = (mod_row(n, 2) * grad).astype(BF)
        gather_start(3, dattn, n)
        dmod[n, 2:3, :] = column_sum(grad * attns[n].astype(F32))
        dmod[n, 3:4, :] = d_shift
        dmod[n, 4:5, :] = d_scale

    def attn_grad_compute(n):
        gather_wait(3, dattn, n)
        staged_ready(7, n)
        grad = dattn[n]
        a1 = a1f[n]
        c, s = turns[n, :, 0:LANES], turns[n, :, LANES : 2 * LANES]
        lanes_all = heads * LANES
        for pair in range(heads // 2):
            span = pl.ds(pair * 2 * LANES, 2 * LANES)
            q2 = dot_nt(a1, wqkv[0, span, :])
            k2 = dot_nt(a1, wqkv[1, span, :])
            v2 = dot_nt(a1, wqkv[2, span, :]).astype(BF)
            d_mix2 = dot_nt(grad, wout[span, :])
            for half in range(2):
                at = (pair * 2 + half) * LANES
                cut = slice(half * LANES, (half + 1) * LANES)
                q_gain, k_gain = gains[0:1, at : at + LANES], gains[1:2, at : at + LANES]
                q_inv, q_norm = head_norm(q2[:, cut])
                k_inv, k_norm = head_norm(k2[:, cut])
                q = turn(q_norm * (q_gain * (SCALE * LOG2E)), c, s).astype(BF)
                k = turn(k_norm * k_gain, c, s).astype(BF)
                v = v2[:, cut]
                powered, inverse = softmax_parts(q, k)
                low = powered.astype(BF)
                mixed = dot(low, v) * inverse
                d_mix = d_mix2[:, cut] * inverse
                d_mix = d_mix.astype(BF)
                taken = jnp.sum(d_mix.astype(F32) * mixed, axis=-1, keepdims=True)
                d_v = dot_tn(low, d_mix)
                d_scores = (powered * (dot_nt(d_mix, v) - taken)).astype(BF)
                d_q = turn_back(dot(d_scores, k) * SCALE, c, s)
                d_k = turn_back(dot_tn(d_scores, q) * (1.0 / LOG2E), c, s)
                gacc[0:1, at : at + LANES] += column_sum(d_q * q_norm)
                gacc[1:2, at : at + LANES] += column_sum(d_k * k_norm)
                d_q = d_q * q_gain
                d_k = d_k * k_gain
                d_q = q_inv * (d_q - q_norm * (jnp.sum(d_q * q_norm, axis=-1, keepdims=True) * (1.0 / HEAD_DIM)))
                d_k = k_inv * (d_k - k_norm * (jnp.sum(d_k * k_norm, axis=-1, keepdims=True) * (1.0 / HEAD_DIM)))
                dqkv_st[:, at : at + LANES] = d_q.astype(BF)
                dqkv_st[:, lanes_all + at : lanes_all + at + LANES] = d_k.astype(BF)
                dqkv_st[:, 2 * lanes_all + at : 2 * lanes_all + at + LANES] = d_v.astype(BF)
        for at, size in wide:
            span = pl.ds(at, size)
            total = dot(dqkv_st[:, 0:lanes_all], wqkv[0, :, span])
            total += dot(dqkv_st[:, lanes_all : 2 * lanes_all], wqkv[1, :, span])
            total += dot(dqkv_st[:, 2 * lanes_all : 3 * lanes_all], wqkv[2, :, span])
            scatter_put(3, n, at, size, total)
        scatter_start(3, n)
        out_copy(7, n).start()
        out_copy(3, n).start()
        gather_drain(3, dattn, n)

    def block_grad_out(n):
        d_a1 = scatter_end(3, n)
        grad, d_shift, d_scale = norm_back(xin[n].astype(F32), d_a1, mod_row(n, 1))
        grad = grad + dxout[n]
        dxout[n] = grad
        dmod[n, 0:1, :] = d_shift
        dmod[n, 1:2, :] = d_scale

        @pl.when(dec)
        def _():
            xin[n] = grad.astype(BF)
            dz_copy(n).start()

        @pl.when(enc)
        def _():
            send_dmod(n)

    works = (
        attn_in,
        attn_relay,
        attn_compute,
        lambda n: scatter_middle(0, n),
        ffn_in,
        lambda n: gather_relay(1, a2f, n),
        ffn_compute,
        lambda n: scatter_middle(1, n),
        block_out,
        ffn_grad_in,
        lambda n: gather_relay(2, dffn, n),
        ffn_grad_compute,
        lambda n: scatter_middle(2, n),
        attn_grad_in,
        lambda n: gather_relay(3, dattn, n),
        attn_grad_compute,
        lambda n: scatter_middle(3, n),
        block_grad_out,
        pass_on,
    )

    def run_work(work, n, low, high):
        if high - low == 1:
            works[low](n)
            return
        middle = (low + high) // 2

        @pl.when(work < middle)
        def _():
            run_work(work, n, low, middle)

        @pl.when(work >= middle)
        def _():
            run_work(work, n, middle, high)

    base = len(works) * images
    tables = [order_words(order, base) for order in ORDERS]

    def entry_of(i):
        rest, values = i, [low + section * (high - low) for low, high in zip(*tables)]
        while len(values) > 1:
            bit, rest = lax.rem(rest, 2), lax.div(rest, 2)
            values = [low + bit * (high - low) for low, high in zip(values[0::2], values[1::2])]
        return values[0]

    def word_step(i, carry):
        def work_step(_, word):
            entry, word = lax.rem(word, base), lax.div(word, base)
            work, n = lax.div(entry, images), lax.rem(entry, images)
            run_work(work, n, 0, len(works))
            return word

        lax.fori_loop(0, PACK, work_step, entry_of(i))
        return carry

    lax.fori_loop(0, base // PACK, word_step, 0)

    for which in (4, 5, 6, 7):
        out_copy(which, images - 1).wait()

    def drain(n, carry):
        for which in (0, 1, 2, 3):
            out_copy(which, n).wait()
        part = dmod[n, :, its_tiles(me)]
        for k in range(3):
            dmod_copy(k, n).wait()
            part += mod_recv[k, n]
        for j in range(8):
            dmod_sum[j, pl.ds(n, 1), :] = part[j : j + 1]

        @pl.when(enc)
        def _():
            z_copy(n).wait_send()

        @pl.when(dec)
        def _():
            dz_copy(n).wait_send()

        return carry

    lax.fori_loop(0, images, drain, 0)
    dmod_part[...] = dmod_sum[...].astype(BF)


def run_main(tok, vel, mod_cols, turns, qkv, out, wgu, wdn, q_gain, k_gain, select):
    images, rows, width = tok.shape
    tokens = 4 * rows
    lanes_all = select.shape[1]
    heads = lanes_all // LANES
    hidden = wdn.shape[0]
    vmem = pl.BlockSpec(memory_space=pltpu.VMEM)
    anywhere = pl.BlockSpec(memory_space=pl.ANY)

    def hbm(last):
        return jax.ShapeDtypeStruct((images, tokens, last), BF)

    out_shape = (
        jax.ShapeDtypeStruct((images, rows, width), BF),
        jax.ShapeDtypeStruct((images, rows, width), F32),
        jax.ShapeDtypeStruct((8, images, 3 * LANES), BF),
        jax.ShapeDtypeStruct((8, lanes_all), F32),
        jax.ShapeDtypeStruct((8, width), F32),
        hbm(width),
        hbm(width),
        hbm(width),
        hbm(width),
        hbm(hidden),
        hbm(lanes_all),
        hbm(2 * hidden),
        hbm(3 * lanes_all),
    )
    scratch = [
        pltpu.VMEM((3, lanes_all, width), BF),
        pltpu.VMEM((lanes_all, width), BF),
        pltpu.VMEM(wgu.shape, BF),
        pltpu.VMEM(wdn.shape, BF),
        pltpu.VMEM((8, lanes_all), F32),
        pltpu.VMEM((images, rows, width), BF),
        pltpu.VMEM((images, rows, width), BF),
        pltpu.VMEM((images, tokens, width), BF),
        pltpu.VMEM((images, tokens, width), BF),
        pltpu.VMEM((images, tokens, width), BF),
        pltpu.VMEM((images, tokens, width), BF),
        pltpu.VMEM((images, rows, width), F32),
        pltpu.VMEM((images, rows, width), BF),
        pltpu.VMEM((images, rows, width), BF),
        pltpu.VMEM((4, KEEP, 2 * rows, width), F32),
        pltpu.VMEM((4, KEEP, 2 * rows, width), BF),
        pltpu.VMEM((4, SLOTS, 2 * rows, width), BF),
        pltpu.VMEM((4, KEEP, rows, width), BF),
        pltpu.VMEM((4, SLOTS, rows, width), BF),
        pltpu.VMEM((tokens, lanes_all), BF),
        pltpu.VMEM((tokens, hidden), BF),
        pltpu.VMEM((tokens, hidden), BF),
        pltpu.VMEM((tokens, 2 * hidden), BF),
        pltpu.VMEM((tokens, 3 * lanes_all), BF),
        pltpu.VMEM((images, 8, width), F32),
        pltpu.VMEM((3, images, 8, 3 * LANES), F32),
        pltpu.VMEM((images, 8, width), F32),
        pltpu.VMEM((8, images, 3 * LANES), F32),
        pltpu.SemaphoreType.DMA((2, 3)),
        pltpu.SemaphoreType.DMA((2, 3, images)),
        pltpu.SemaphoreType.DMA((4, 6, images)),
        pltpu.SemaphoreType.DMA((4, 4, images)),
        pltpu.SemaphoreType.DMA((8, images)),
        pltpu.SemaphoreType.DMA((8, images)),
        pltpu.SemaphoreType.DMA((12,)),
    ]
    return pl.pallas_call(
        functools.partial(main_kernel, images, heads),
        out_shape=out_shape,
        in_specs=[anywhere, anywhere] + [vmem] * 2 + [anywhere] * 4 + [vmem] * 3,
        out_specs=[vmem] * 5 + [anywhere] * 8,
        scratch_shapes=scratch,
        compiler_params=pltpu.CompilerParams(
            collective_id=0, has_side_effects=True, vmem_limit_bytes=62 * 2**20
        ),
    )(tok, vel, mod_cols, turns, qkv, out, wgu, wdn, q_gain, k_gain, select)


def flat_plan(width, hidden, part):
    blocks = width // LANES
    segments = ((2 * hidden // LANES, width), (blocks, hidden), (blocks, 3 * part), (blocks, part))
    halves = [count * rows // 2 for count, rows in segments]
    half, chunk = sum(halves), width // 2
    assert half % chunk == 0

    def pieces(segment, block):
        rows, cut, at = segments[segment][1], halves[segment], sum(halves[:segment])
        low, high = block * rows, (block + 1) * rows
        if high <= cut:
            return [(at + low, 0, rows)]
        if low >= cut:
            return [(half + at + low - cut, 0, rows)]
        return [(at + low, 0, cut - low), (half + at, cut - low, high - cut)]

    return half, chunk, pieces


def tail_kernel(
    dp,
    a2_hbm,
    dgu_hbm,
    hid_hbm,
    dffn_hbm,
    a1_hbm,
    dqkv_hbm,
    mix_hbm,
    dattn_hbm,
    mod_hbm,
    pick,
    cond,
    squares,
    silu,
    dmod_low,
    gain_sums,
    labels,
    totals,
    dmod_all,
    sum_all,
    extra_all,
    left_a,
    right_a,
    left_b,
    right_b,
    turned,
    own,
    arrived,
    mod_w,
    summand,
    sum_st,
    sum_recv,
    load_sems,
    part_sems,
    total_sems,
    sum_sems,
    all_sems,
    x_part_sems,
    x_total_sems,
    here,
):
    section = lax.axis_index("section")
    place = lax.axis_index("dp")
    me = lax.axis_index("tensor")
    sib = me + 1 - 2 * lax.rem(me, 2)
    across = lax.rem(me + 2, 4)
    enc, dec = section == 0, section == 1
    width, hidden = left_a.shape[1], left_b.shape[1]
    part, lanes_all = pick.shape
    half, chunk, pieces = flat_plan(width, hidden, part)
    whole = half // chunk
    count = jnp.where(enc, whole - LENT, whole + LENT)

    tokens, ahead = left_a.shape[0], 2 * LANES
    quarter = tokens // 4

    def some_rows(i):
        rows = pl.ds(i * quarter, quarter)
        return a2_hbm.at[rows], left_a.at[rows]

    def some_columns(at, size):
        cols = pl.ds(at, size)
        return dgu_hbm.at[:, cols], right_a.at[:, cols]

    loads = [
        pltpu.make_async_copy(src, dst, load_sems.at[i])
        for i, (src, dst) in enumerate(
            (
                some_rows(0),
                some_rows(1),
                some_rows(2),
                some_rows(3),
                some_columns(0, ahead),
                some_columns(hidden, ahead),
                some_columns(ahead, hidden - ahead),
                some_columns(hidden + ahead, hidden - ahead),
                (hid_hbm, left_b),
                (dffn_hbm, right_b),
                (mix_hbm, left_b.at[:, pl.ds(0, lanes_all)]),
                (a1_hbm, left_a),
                (dqkv_hbm, right_a),
                (dattn_hbm, right_b),
            )
        )
    ]
    for i in range(10):
        loads[i].start()

    mod_w[...] = jnp.zeros_like(mod_w)
    mine = pl.ds(pl.multiple_of(me * (part - 2 * LANES), 16), part)
    mod_loads = [pltpu.make_async_copy(mod_hbm.at[j], mod_w.at[j, mine], load_sems.at[14 + j]) for j in range(6)]
    for copy in mod_loads:
        copy.start()

    barrier = pltpu.get_barrier_semaphore()
    for where in ({"tensor": sib}, {"tensor": across}):
        pl.semaphore_signal(barrier, inc=1, device_id=where, device_id_type=MESH)

    @pl.when(dec)
    def _():
        pl.semaphore_signal(barrier, inc=1, device_id={"section": 0}, device_id_type=MESH)

    for k in range(1, dp):
        pl.semaphore_signal(barrier, inc=1, device_id={"dp": lax.rem(place + k, dp)}, device_id_type=MESH)

    def put(segment, block, first, value):
        for at, low, size in pieces(segment, block):
            begin, end = max(low, first), min(low + size, first + value.shape[0])
            if begin < end:
                own[at + begin - low : at + end - low, :] = value[begin - first : end - first].astype(BF)

    def put_wide(segment, block, first, value):
        for i in range(value.shape[1] // LANES):
            put(segment, block + i, first, value[:, i * LANES : (i + 1) * LANES])

    def turn_left(ref, first, last):
        cols = ref.shape[1]
        for at in range(first, last, 256):
            turned[0:cols, at : at + 256] = ref[at : at + 256, :].T

    def gate_up_blocks(*blocks):
        for block in blocks:
            value = dot(turned[...], right_a[:, block * LANES : (block + 2) * LANES])
            put_wide(0, block, 0, value)

    def qkv_heads(*pairs):
        kept = 2 * HEAD_DIM
        for pair in pairs:
            value = dot_tn(right_a[:, pair * 2 * LANES : (pair + 1) * 2 * LANES], left_a[...]).astype(BF)
            put_wide(2, 0, pair * kept, dot(pick[0:kept, 0 : 2 * LANES], value))

    def portion(i):
        tiles, gu_half = width // LANES, hidden // LANES
        pairs = 3 * lanes_all // (2 * LANES)
        if i == 0:
            for k in range(4):
                loads[k].wait()
                turn_left(left_a, k * quarter, (k + 1) * quarter)
            loads[11].start()
            loads[4].wait()
            gate_up_blocks(0)
            loads[5].wait()
            gate_up_blocks(gu_half)
        elif i == 1:
            loads[6].wait()
            loads[7].wait()
            gate_up_blocks(2, gu_half + 2)
        elif i == 2:
            gate_up_blocks(*range(4, gu_half, 2), *range(gu_half + 4, 2 * gu_half, 2))
            loads[12].start()
        elif i == 3:
            loads[8].wait()
            turn_left(left_b, 0, tokens)
            loads[10].start()
            loads[9].wait()
            for block in range(0, tiles, 2):
                cut = slice(block * LANES, min(width, (block + 2) * LANES))
                put_wide(1, block, 0, dot(turned[0:hidden, :], right_b[:, cut]))
            loads[13].start()
        elif i == 4:
            loads[11].wait()
            loads[12].wait()
            qkv_heads(*range(0, pairs // 2))
        elif i == 5:
            qkv_heads(*range(pairs // 2, pairs))
        elif i == 6:
            loads[10].wait()
            loads[13].wait()
            value = dot(pick[...], dot_tn(left_b[:, 0:lanes_all], right_b[...]).astype(BF))
            put_wide(3, 0, 0, value)

    def along(direction, onward):
        step = 1 if (direction == 0) == onward else dp - 1
        return {"dp": lax.rem(place + step, dp)}

    def behind(direction):
        return place if direction == 0 else dp - 1 - place

    def rows_of(direction, c):
        lent = 2 * half + (direction * LENT + c - whole) * chunk
        return pl.ds(pl.multiple_of(jnp.where(c < whole, direction * half + c * chunk, lent), chunk), chunk)

    def lent_copy(ref, sems, direction, i, to_decoder):
        mine = rows_of(direction, whole - LENT + i)
        theirs = rows_of(direction, whole + i)
        return pltpu.make_async_remote_copy(
            src_ref=ref.at[mine if to_decoder else theirs],
            dst_ref=ref.at[theirs if to_decoder else mine],
            send_sem=sems.at[direction, 0, i],
            recv_sem=sems.at[direction, 1, i],
            device_id={"section": 1 if to_decoder else 0},
            device_id_type=MESH,
        )

    def lent_part(direction, i):
        return lent_copy(own, x_part_sems, direction, i, True)

    def lent_total(direction, i):
        return lent_copy(totals, x_total_sems, direction, i, False)

    def part_copy(direction, c):
        return pltpu.make_async_remote_copy(
            src_ref=own.at[rows_of(direction, c)],
            dst_ref=arrived.at[rows_of(direction, c)],
            send_sem=part_sems.at[direction, 0, c],
            recv_sem=part_sems.at[direction, 1, c],
            device_id=along(direction, True),
            device_id_type=MESH,
        )

    def total_copy(direction, c):
        return pltpu.make_async_remote_copy(
            src_ref=totals.at[rows_of(direction, c)],
            dst_ref=totals.at[rows_of(direction, c)],
            send_sem=total_sems.at[direction, 0, c],
            recv_sem=total_sems.at[direction, 1, c],
            device_id=along(direction, False),
            device_id_type=MESH,
        )

    def add_part(direction, c):
        begins, ends = behind(direction) == 0, behind(direction) == dp - 1
        rows = rows_of(direction, c)

        @pl.when(c >= whole)
        def _():
            lent_part(direction, c - whole).wait_recv()

        @pl.when(begins)
        def _():
            part_copy(direction, c).start()

        @pl.when(jnp.logical_not(begins))
        def _():
            part_copy(direction, c).wait_recv()
            value = (own[rows, :].astype(F32) + arrived[rows, :].astype(F32)).astype(BF)

            @pl.when(ends)
            def _():
                totals[rows, :] = value
                total_copy(direction, c).start()

            @pl.when(jnp.logical_not(ends))
            def _():
                own[rows, :] = value
                part_copy(direction, c).start()

    def pass_total(direction, c):
        begins, ends = behind(direction) == 0, behind(direction) == dp - 1

        @pl.when(jnp.logical_not(ends))
        def _():
            total_copy(direction, c).wait_recv()

            @pl.when(jnp.logical_not(begins))
            def _():
                total_copy(direction, c).start()

        @pl.when(c >= whole)
        def _():
            lent_total(direction, c - whole).start()

    skew = 2

    def chunk_step(step):
        for direction in range(2):
            c = step - skew * behind(direction)

            @pl.when((c >= 0) & (c < count))
            def _():
                add_part(direction, c)

        for direction in range(2):
            u = step - skew * (2 * (dp - 1) - behind(direction))

            @pl.when((u >= 0) & (u < count))
            def _():
                pass_total(direction, u)

        for i in range(4):

            @pl.when(step == jnp.where(enc, 12, 22) + i)
            def _():
                small(i)

    def sum_copy(which):
        where = ({"section": 1 - section}, {"tensor": sib}, {"tensor": across})[which]
        height = (8, 16, 16)[which]
        src = summand if which == 0 else sum_st.at[which - 1]
        return pltpu.make_async_remote_copy(
            src_ref=src.at[pl.ds(0, height)],
            dst_ref=sum_recv.at[which, pl.ds(0, height)],
            send_sem=sum_sems.at[which, 0],
            recv_sem=sum_sems.at[which, 1],
            device_id=where,
            device_id_type=MESH,
        )

    def all_copy(which, k, outgoing):
        ref = (dmod_all, sum_all, extra_all)[which]
        peer = lax.rem(place + k, dp)
        slot = place if outgoing else peer
        return pltpu.make_async_remote_copy(
            src_ref=ref.at[slot],
            dst_ref=ref.at[slot],
            send_sem=all_sems.at[which, 0, k],
            recv_sem=all_sems.at[which, 1, slot],
            device_id={"dp": peer},
            device_id_type=MESH,
        )

    def small(step):
        if step == 0:
            dmod_all[place] = dmod_low[...]
            for k in range(1, dp):
                all_copy(0, k, True).start()

            for copy in mod_loads:
                copy.wait()
            images = cond.shape[0]
            grads = dmod_low[...].astype(F32)
            d_silu = dot(grads[0:images].astype(BF), mod_w[0])
            for j in range(1, 6):
                d_silu += dot(grads[j * images : (j + 1) * images].astype(BF), mod_w[j])
            sig = jax.nn.sigmoid(cond[...])
            summand[0:8, :] = d_silu * (sig + cond[...] * sig * (1.0 - sig))
            summand[8:16, :] = squares[...]

            @pl.when(dec)
            def _():
                pl.semaphore_wait(here, 1)

            sum_copy(0).start()
        elif step == 1:
            sum_copy(0).wait()
            sum_st[0] = summand[...]
            sum_st[0, 0:8, :] += sum_recv[0, 0:8, :]
            sum_copy(1).start()
        elif step == 2:
            sum_copy(1).wait()
            sum_st[1] = sum_st[0] + sum_recv[1]
            sum_copy(2).start()
        elif step == 3:
            sum_copy(2).wait()
            total = sum_st[1] + sum_recv[2]
            sum_all[place, 0:8, :] = total[0:8].astype(BF)
            sum_all[place, 8:16, :] = silu[...]
            square = total[8:16, 0:LANES]
            for i in range(1, width // LANES):
                square += total[8:16, i * LANES : (i + 1) * LANES]
            extra_all[place, 0:8, :] = gain_sums[...]
            extra_all[place, 8:16, :] = jnp.zeros_like(gain_sums)
            extra_all[place, 8:16, 0:LANES] = square
            for i in range(8):
                extra_all[place, 8 + i : 9 + i, LANES : 2 * LANES] = jnp.full((1, LANES), labels[i].astype(F32))
            for k in range(1, dp):
                all_copy(1, k, True).start()
                all_copy(2, k, True).start()

    portion(0)
    pl.semaphore_wait(barrier, jnp.where(enc, dp + 2, dp + 1))

    @pl.when(enc)
    def _():
        pl.semaphore_signal(here, inc=1, device_id={"section": 1}, device_id_type=MESH)

    for step in range(6):
        chunk_step(step)
        portion(step + 1)

    def lend(i, carry):
        for direction in range(2):
            lent_part(direction, i).start()
        return carry

    @pl.when(enc)
    def _():
        lax.fori_loop(0, LENT, lend, 0)

    def later_step(step, carry):
        chunk_step(step)
        return carry

    lax.fori_loop(6, whole + LENT + 2 * skew * (dp - 1), later_step, 0)

    def lent_back(i, carry):
        for direction in range(2):

            @pl.when(enc)
            def _():
                lent_part(direction, i).wait_send()
                lent_total(direction, i).wait_recv()

            @pl.when(dec)
            def _():
                lent_total(direction, i).wait_send()

        return carry

    lax.fori_loop(0, LENT, lent_back, 0)

    for which in range(3):
        for k in range(1, dp):
            all_copy(which, k, True).wait_send()
            all_copy(which, k, False).wait_recv()

    def drain(c, carry):
        for direction in range(2):

            @pl.when(behind(direction) != dp - 1)
            def _():
                part_copy(direction, c).wait_send()

            @pl.when(behind(direction) != 0)
            def _():
                total_copy(direction, c).wait_send()

        return carry

    lax.fori_loop(0, count, drain, 0)


def run_tail(dp, a2, dgu, hid, dffn, a1, dqkv, mix, dattn, mod_w, pick, cond, squares, silu, dmod_low, gain_sums, labels):
    tokens, width = a2.shape
    hidden = hid.shape[1]
    vmem = pl.BlockSpec(memory_space=pltpu.VMEM)
    anywhere = pl.BlockSpec(memory_space=pl.ANY)
    half, chunk, _ = flat_plan(width, hidden, pick.shape[0])
    flat_rows, chunks = 2 * (half + LENT * chunk), half // chunk + LENT
    return pl.pallas_call(
        functools.partial(tail_kernel, dp),
        out_shape=(
            jax.ShapeDtypeStruct((flat_rows, LANES), BF),
            jax.ShapeDtypeStruct((dp,) + dmod_low.shape, BF),
            jax.ShapeDtypeStruct((dp, 16, width), BF),
            jax.ShapeDtypeStruct((dp, 16, gain_sums.shape[1]), F32),
        ),
        in_specs=[anywhere] * 9 + [vmem] * 6 + [pl.BlockSpec(memory_space=pltpu.SMEM)],
        out_specs=[vmem] * 4,
        scratch_shapes=[
            pltpu.VMEM((tokens, width), BF),
            pltpu.VMEM((tokens, dgu.shape[1]), BF),
            pltpu.VMEM((tokens, hidden), BF),
            pltpu.VMEM((tokens, width), BF),
            pltpu.VMEM((width, tokens), BF),
            pltpu.VMEM((flat_rows, LANES), BF),
            pltpu.VMEM((flat_rows, LANES), BF),
            pltpu.VMEM((6, 3 * LANES, width), BF),
            pltpu.VMEM((16, width), F32),
            pltpu.VMEM((2, 16, width), F32),
            pltpu.VMEM((3, 16, width), F32),
            pltpu.SemaphoreType.DMA((20,)),
            pltpu.SemaphoreType.DMA((2, 2, chunks)),
            pltpu.SemaphoreType.DMA((2, 2, chunks)),
            pltpu.SemaphoreType.DMA((3, 2)),
            pltpu.SemaphoreType.DMA((3, 2, dp)),
            pltpu.SemaphoreType.DMA((2, 2, LENT)),
            pltpu.SemaphoreType.DMA((2, 2, LENT)),
            pltpu.SemaphoreType.REGULAR,
        ],
        compiler_params=pltpu.CompilerParams(
            collective_id=1, has_side_effects=True, vmem_limit_bytes=62 * 2**20
        ),
    )(a2, dgu, hid, dffn, a1, dqkv, mix, dattn, mod_w, pick, cond, squares, silu, dmod_low, gain_sums, labels)


def finish_kernel(
    count,
    flat_hbm,
    z_hbm,
    dx_hbm,
    dmod_all,
    sum_all,
    extra_all,
    select,
    gu_hbm,
    down_hbm,
    qkv_hbm,
    out_hbm,
    z_out,
    dx_out,
    mod_hbm,
    class_hbm,
    q_gain_out,
    k_gain_out,
    stats_out,
    flat,
    gate_up,
    down,
    qkv,
    out,
    mod,
    classes,
    z_rows,
    dx_rows,
    load_sems,
    store_sems,
):
    width, hidden = gate_up.shape[1], gate_up.shape[2]
    part, blocks, hidden_blocks = out.shape[0], width // LANES, hidden // LANES
    _, _, pieces = flat_plan(width, hidden, part)
    groups = (
        [(0, b) for b in range(hidden_blocks)],
        [(0, hidden_blocks + b) for b in range(hidden_blocks)],
        [(1, b) for b in range(blocks)],
        [(2, b) for b in range(blocks)],
        [(3, b) for b in range(blocks)],
    )
    loads = []
    for group in groups:
        spans = []
        for segment, block in group:
            for at, _, size in pieces(segment, block):
                if spans and spans[-1][0] + spans[-1][1] == at:
                    spans[-1][1] += size
                else:
                    spans.append([at, size])
        copies = []
        for at, size in spans:
            rows = pl.ds(at, size)
            sem = load_sems.at[len(loads), len(copies)]
            copies.append(pltpu.make_async_copy(flat_hbm.at[rows], flat.at[rows], sem))
            copies[-1].start()
        loads.append(copies)
    inward = (
        pltpu.make_async_copy(z_hbm, z_rows, load_sems.at[0, 2]),
        pltpu.make_async_copy(dx_hbm, dx_rows, load_sems.at[1, 2]),
    )
    outward = (
        pltpu.make_async_copy(z_rows, z_out, store_sems.at[5]),
        pltpu.make_async_copy(dx_rows, dx_out, store_sems.at[6]),
    )
    for copy in inward:
        copy.start()

    dp, images = dmod_all.shape[0], dmod_all.shape[1] // 8
    me = lax.axis_index("tensor")
    silu = jnp.concatenate([sum_all[p].astype(F32)[8:16] for p in range(dp)], axis=0).astype(BF)
    grad_cond = jnp.concatenate([sum_all[p].astype(F32)[0:8] for p in range(dp)], axis=0).astype(BF)
    dmods = [dmod_all[p].astype(F32) for p in range(dp)]
    mod_stores = []
    for j in range(6):
        grads = jnp.concatenate([dmods[p][j * images : (j + 1) * images] for p in range(dp)], axis=0).astype(BF)
        mod[j] = dot_tn(grads, silu)
        mine = pl.ds(pl.multiple_of(me * (part - 2 * LANES), 8), part)
        mod_stores.append(pltpu.make_async_copy(mod.at[j, mine], mod_hbm.at[j], store_sems.at[8 + j]))
        mod_stores[-1].start()
    labels = jnp.concatenate([extra_all[p, 8:16, LANES : LANES + 1] for p in range(dp)], axis=0)
    lanes = lax.broadcasted_iota(jnp.int32, (dp * images, classes.shape[0]), 1)
    one_hot = jnp.where(lanes == labels.astype(jnp.int32), 1.0, 0.0).astype(BF)
    for at, size in chunks_of(width, 384):
        classes[:, at : at + size] = dot_tn(one_hot, grad_cond[:, at : at + size])
    class_store = pltpu.make_async_copy(classes.at[pl.ds(0, class_hbm.shape[0])], class_hbm, store_sems.at[7])
    class_store.start()

    for i in range(2):
        inward[i].wait()
        outward[i].start()

    gain_sum, squares = extra_all[0, 0:8, :], extra_all[0, 8:16, 0:LANES]
    for p in range(1, dp):
        gain_sum += extra_all[p, 0:8, :]
        squares += extra_all[p, 8:16, 0:LANES]
    gain_sum = lax.dot_general(
        gain_sum,
        select[...].astype(F32),
        (((1,), (1,)), ((), ())),
        precision=lax.Precision.HIGHEST,
        preferred_element_type=F32,
    )
    q_gain_out[...] = gain_sum[0:1]
    k_gain_out[...] = gain_sum[1:2]
    for i in range(3):
        stats_out[0:1, i : i + 1] = jnp.sqrt(jnp.sum(squares[i : i + 1], axis=1, keepdims=True) * (1.0 / count))

    stores = (
        pltpu.make_async_copy(gate_up.at[0], gu_hbm.at[0], store_sems.at[0]),
        pltpu.make_async_copy(gate_up.at[1], gu_hbm.at[1], store_sems.at[1]),
        pltpu.make_async_copy(down, down_hbm, store_sems.at[2]),
        pltpu.make_async_copy(qkv, qkv_hbm, store_sems.at[3]),
        pltpu.make_async_copy(out, out_hbm, store_sems.at[4]),
    )
    for i, group in enumerate(groups):
        for copy in loads[i]:
            copy.wait()
        for segment, block in group:
            for at, low, size in pieces(segment, block):
                value = flat[at : at + size, :].astype(F32)
                rows = slice(low, low + size)
                cols = slice(block * LANES, (block + 1) * LANES)
                if segment == 0:
                    local = block % hidden_blocks
                    gate_up[block // hidden_blocks, rows, local * LANES : (local + 1) * LANES] = value
                elif segment == 1:
                    down[rows, cols] = value
                elif segment == 2:
                    qkv[rows, cols] = value
                else:
                    out[rows, cols] = value
        stores[i].start()
    for copy in (*stores, *outward, *mod_stores, class_store):
        copy.wait()


def run_finish(count, class_count, hidden, flat, z_rows, dx_rows, dmod_all, sum_all, extra_all, select):
    part, width = select.shape[0], sum_all.shape[2]
    vmem = pl.BlockSpec(memory_space=pltpu.VMEM)
    anywhere = pl.BlockSpec(memory_space=pl.ANY)
    shapes = ((2, width, hidden), (hidden, width), (3 * part, width), (part, width))
    return pl.pallas_call(
        functools.partial(finish_kernel, count),
        out_shape=tuple(jax.ShapeDtypeStruct(shape, F32) for shape in shapes)
        + (
            jax.ShapeDtypeStruct(z_rows.shape, BF),
            jax.ShapeDtypeStruct(dx_rows.shape, F32),
            jax.ShapeDtypeStruct((6, part, width), F32),
            jax.ShapeDtypeStruct((class_count, width), F32),
            jax.ShapeDtypeStruct((1, part), F32),
            jax.ShapeDtypeStruct((1, part), F32),
            jax.ShapeDtypeStruct((1, 3), F32),
        ),
        in_specs=[anywhere] * 3 + [vmem] * 4,
        out_specs=[anywhere] * 8 + [vmem] * 3,
        scratch_shapes=[pltpu.VMEM(flat.shape, BF)]
        + [pltpu.VMEM(shape, F32) for shape in shapes]
        + [
            pltpu.VMEM((6, 3 * LANES, width), F32),
            pltpu.VMEM((-(-class_count // LANES) * LANES, width), F32),
            pltpu.VMEM(z_rows.shape, BF),
            pltpu.VMEM(dx_rows.shape, F32),
            pltpu.SemaphoreType.DMA((5, 3)),
            pltpu.SemaphoreType.DMA((14,)),
        ],
        compiler_params=pltpu.CompilerParams(vmem_limit_bytes=60 * 2**20),
    )(flat, z_rows, dx_rows, dmod_all, sum_all, extra_all, select)


def time_embed(bin_row, feature_count):
    halfway = feature_count // 2
    frequency = jnp.exp(-math.log(10000.0) * jnp.arange(halfway, dtype=F32) / halfway)
    moment = (bin_row.astype(F32) + 0.5) * (1000.0 / NBINS)
    angles = moment[:, None] * frequency[None, :]
    return jnp.concatenate([jnp.cos(angles), jnp.sin(angles)], axis=-1)


def per_device(
    tokens,
    velocity_grad,
    bins,
    labels,
    places,
    class_table,
    mod_weight,
    qkv_weight,
    out_weight,
    gate_up_weight,
    down_weight,
    q_gain,
    k_gain,
):
    micro, per_micro, rows, width = tokens.shape
    images = micro * per_micro
    dp = lax.axis_size("dp")
    me = lax.axis_index("tensor")
    heads = q_gain.shape[1] // HEAD_DIM
    select = jnp.asarray(head_select(heads), BF)

    label_row = labels.reshape(images)
    one_hot = label_row[:, None] == jnp.arange(class_table.shape[0], dtype=jnp.int32)[None, :]
    picked = jnp.dot(one_hot.astype(BF), class_table, preferred_element_type=F32)
    cond = time_embed(bins.reshape(images), width) + picked
    silu_low = jax.nn.silu(cond).astype(BF)
    mod_w = mod_weight[0]
    part = width // 4
    columns = jnp.einsum("id,djf->ijf", silu_low, mod_w, preferred_element_type=F32)
    shift = me * (part - 2 * LANES)
    mod_cols = lax.dynamic_update_slice(jnp.zeros((images, 8, 3 * LANES), F32), columns, (0, 0, shift))

    order = jnp.stack([me, (me + 2) % 4, me + 1 - 2 * (me % 2), (me + 2) % 4 + 1 - 2 * (me % 2)])
    placed = jnp.take(places.reshape(images, 4, rows), order, axis=1).reshape(images * 4 * rows)
    spot = jnp.arange(6 * GRID, dtype=jnp.int32)[None, :] % (2 * GRID)
    marks = (jnp.where(spot < GRID, placed[:, None] // GRID, placed[:, None] % GRID + GRID) == spot).astype(BF)
    table, table_parts = angle_table(), []
    for _ in range(3):
        table_parts.append(table.astype(BF))
        table = table - table_parts[-1].astype(np.float32)
    turns = jnp.dot(marks, jnp.asarray(np.concatenate(table_parts)), preferred_element_type=F32)
    turns = turns.reshape(images, 4 * rows, 2 * LANES)

    results = run_main(
        tokens.reshape(images, rows, width),
        velocity_grad.reshape(images, rows, width),
        mod_cols,
        turns,
        jnp.transpose(qkv_weight[0], (0, 2, 1)),
        out_weight[0],
        gate_up_weight[0],
        down_weight[0],
        q_gain,
        k_gain,
        select,
    )
    z_rows, dx_rows, dmod_part, gain_sums, squares, a1, a2, d_ffn, d_attn, units, mixed, d_gu, d_qkv = results

    lanes_all = heads * LANES
    flat = images * 4 * rows
    flat_grads, dmod_all, sum_all, extra_all = run_tail(
        dp,
        a2.reshape(flat, width),
        d_gu.reshape(flat, d_gu.shape[2]),
        units.reshape(flat, units.shape[2]),
        d_ffn.reshape(flat, width),
        a1.reshape(flat, width),
        d_qkv.reshape(flat, d_qkv.shape[2]),
        mixed.reshape(flat, lanes_all),
        d_attn.reshape(flat, width),
        jnp.transpose(mod_w, (1, 2, 0)),
        select,
        cond,
        squares,
        silu_low,
        dmod_part.reshape(8 * images, 3 * LANES),
        gain_sums,
        label_row,
    )
    count = images * rows * width * dp * lax.axis_size("tensor")
    finished = run_finish(
        count,
        class_table.shape[0],
        units.shape[2],
        flat_grads,
        z_rows,
        dx_rows,
        dmod_all,
        sum_all,
        extra_all,
        select,
    )
    gate_up_grad, down_grad, qkv_grad, out_grad, z_out, dx_out, mod_grad, class_grad, q_grad, k_grad, stats = finished
    whole = (1, micro, per_micro, rows, width)
    return (
        z_out.reshape(whole),
        dx_out.reshape(whole),
        jnp.transpose(mod_grad, (2, 0, 1))[None],
        jnp.transpose(qkv_grad.reshape(3, part, width), (0, 2, 1))[None],
        out_grad[None],
        gate_up_grad[None],
        down_grad[None],
        q_grad,
        k_grad,
        class_grad,
        stats,
    )


def solution(mesh):
    return jax.shard_map(
        per_device,
        mesh=mesh,
        in_specs=(
            P(None, "dp", "tensor", None),
            P(None, "dp", "tensor", None),
            P(None, "dp"),
            P(None, "dp"),
            P(None, "dp", None),
            P(),
            P("section", None, None, "tensor"),
            P("section", None, None, "tensor"),
            P("section", "tensor", None),
            P("section", None, None, "tensor"),
            P("section", "tensor", None),
            P("section", "tensor"),
            P("section", "tensor"),
        ),
        out_specs=(
            P("section", None, "dp", "tensor", None),
            P("section", None, "dp", "tensor", None),
            P("section", None, None, "tensor"),
            P("section", None, None, "tensor"),
            P("section", "tensor", None),
            P("section", None, None, "tensor"),
            P("section", "tensor", None),
            P("section", "tensor"),
            P("section", "tensor"),
            P(),
            P("section", None),
        ),
        check_vma=False,
    )
```

```python
import functools
import math

import jax
import jax.numpy as jnp
import numpy as np
from jax import lax
from jax.experimental import pallas as pl
from jax.experimental.pallas import tpu as pltpu
from jax.sharding import PartitionSpec as P

MESH = pl.DeviceIdType.MESH
HEAD_DIM = 72
LANES = 128
NBINS = 1000
GRID = 16
EPS = 1e-06
BF = jnp.bfloat16
F32 = jnp.float32
SCALE = HEAD_DIM**-0.5
LOG2E = math.log2(math.e)

KEEP, SLOTS, PACK = 2, 4, 4
LENT = 4
ORDERS = (
    (
        0, 1, 8, 2, 3, 16, 9, 24, 10, 4, 17, 32, 11, 25, 18, 40, 26, 48, 33,
        56, 19, 34, 12, 41, 64, 49, 27, 57, 42, 144, 50, 35, 65, 58, 20, 43, 5, 145,
        66, 28, 51, 13, 146, 59, 36, 6, 21, 67, 44, 52, 60, 147, 14, 7, 29, 68, 22,
        15, 37, 148, 30, 23, 38, 31, 45, 53, 61, 39, 46, 54, 69, 62, 149, 70, 47, 72,
        55, 80, 63, 150, 88, 71, 151, 96, 104, 73, 81, 89, 112, 74, 97, 120, 82, 128, 105,
        90, 136, 98, 113, 75, 121, 83, 106, 91, 114, 129, 99, 122, 76, 130, 137, 107, 84, 92,
        77, 115, 100, 138, 123, 78, 85, 108, 93, 86, 79, 131, 94, 116, 101, 102, 124, 87, 109,
        132, 95, 139, 117, 103, 110, 125, 111, 140, 133, 118, 126, 119, 141, 134, 127, 135, 142, 143,
    ),
    (
        72, 73, 74, 80, 75, 81, 82, 76, 83, 77, 0, 8, 78, 16, 1, 24, 84, 9, 32,
        79, 17, 40, 85, 2, 25, 88, 10, 33, 48, 56, 18, 96, 41, 3, 86, 26, 89, 11,
        104, 97, 19, 4, 64, 112, 34, 27, 49, 120, 42, 105, 57, 90, 12, 113, 35, 98, 20,
        65, 128, 43, 121, 28, 50, 106, 136, 91, 5, 36, 13, 129, 114, 58, 99, 21, 122, 44,
        51, 66, 29, 59, 130, 6, 92, 14, 37, 107, 22, 7, 137, 67, 138, 30, 15, 87, 52,
        60, 45, 100, 115, 23, 38, 123, 31, 108, 93, 53, 131, 46, 68, 61, 39, 94, 116, 139,
        101, 102, 124, 47, 69, 109, 132, 95, 117, 144, 110, 103, 125, 140, 54, 133, 145, 118, 146,
        55, 111, 62, 126, 141, 119, 134, 63, 127, 147, 135, 142, 148, 70, 149, 71, 150, 143, 151,
    ),
)


def lane_of():
    quarter = HEAD_DIM // 4
    lanes = np.zeros((HEAD_DIM,), np.int64)
    for half in range(2):
        for part in range(2):
            for i in range(quarter):
                lanes[half * 2 * quarter + part * quarter + i] = part * 64 + half * quarter + i
    return lanes


def head_select(heads):
    select = np.zeros((heads * HEAD_DIM, heads * LANES), np.float32)
    lanes = lane_of()
    for h in range(heads):
        for f in range(HEAD_DIM):
            select[h * HEAD_DIM + f, h * LANES + lanes[f]] = 1.0
    return select


def angle_table():
    quarter = HEAD_DIM // 4
    frequency = (10000.0 ** (-np.arange(quarter, dtype=np.float32) / np.float32(quarter))).astype(np.float32)
    lanes = lane_of().reshape(2, 2, quarter)
    table = np.zeros((2 * GRID, 2 * LANES), np.float32)
    for place in range(GRID):
        angle = np.float32(place) * frequency
        for half in range(2):
            for part in range(2):
                sign = -1.0 if part == 0 else 1.0
                table[half * GRID + place, lanes[half, part]] = np.cos(angle)
                table[half * GRID + place, LANES + lanes[half, part]] = sign * np.sin(angle)
    return table


def dot(a, b):
    return lax.dot_general(a, b, (((1,), (0,)), ((), ())), preferred_element_type=F32)


def dot_nt(a, b):
    return lax.dot_general(a, b, (((1,), (1,)), ((), ())), preferred_element_type=F32)


def dot_tn(a, b):
    return lax.dot_general(a, b, (((0,), (0,)), ((), ())), preferred_element_type=F32)


def order_words(order, base):
    words = []
    for at in range(0, len(order), PACK):
        words.append(sum(entry * base**i for i, entry in enumerate(order[at : at + PACK])))
    while len(words) & (len(words) - 1):
        words.append(0)
    return words


def chunks_of(size, width):
    return [(at, min(width, size - at)) for at in range(0, size, width)]


def main_kernel(
    images,
    heads,
    tok,
    vel,
    mod_cols,
    places,
    angles,
    qkv_hbm,
    out_hbm,
    wgu_hbm,
    wdn_hbm,
    q_gain,
    k_gain,
    select,
    zout,
    dxout,
    dmod_part,
    gacc,
    sacc,
    a1_hbm,
    a2_hbm,
    dffn_hbm,
    dattn_hbm,
    hid_hbm,
    mix_hbm,
    dgu_hbm,
    dqkv_hbm,
    turns,
    wqkv,
    wout,
    wgu,
    wdn,
    gains,
    xin,
    din,
    a1f,
    a2f,
    dffn,
    dattn,
    x1s,
    attns,
    ffns,
    keep,
    send_a,
    recv_a,
    send_y,
    recv_y,
    mix_st,
    hid_st,
    dgu_st,
    dqkv_st,
    mod,
    mod_recv,
    dmod,
    mod_sems,
    dmod_sems,
    ag_sems,
    rs_sems,
    zx_sems,
    out_sems,
    in_sems,
):
    rows = tok.shape[1]
    width = tok.shape[2]
    hidden = wdn.shape[0]
    wide = chunks_of(width, 512)
    section = lax.axis_index("section")
    me = lax.axis_index("tensor")
    sib = me + 1 - 2 * lax.rem(me, 2)
    across = lax.rem(me + 2, 4)
    diag = lax.rem(sib + 2, 4)
    peers = (sib, across, diag)
    other = 1 - section
    enc = section == 0
    dec = section == 1

    load_x = pltpu.make_async_copy(tok, xin, in_sems.at[0])
    load_d = pltpu.make_async_copy(vel, din, in_sems.at[1])
    tokens, part = dattn.shape[1], out_hbm.shape[0]
    groups = [qkv_hbm.at[j] for j in range(3)] + [out_hbm]
    load_w = [
        pltpu.make_async_copy(wgu_hbm, wgu, in_sems.at[2]),
        pltpu.make_async_copy(wdn_hbm, wdn, in_sems.at[3]),
    ]
    load_raw = []
    for j, group in enumerate(groups):
        for i, (at, size) in enumerate(((0, tokens), (tokens, part - tokens))):
            src, dst = group.at[pl.ds(at, size)], dattn.at[2 * j + i, pl.ds(0, size)]
            load_raw.append(pltpu.make_async_copy(src, dst, in_sems.at[4 + 2 * j + i]))
    for copy in load_raw:
        copy.start()

    @pl.when(enc)
    def _():
        load_x.start()

    @pl.when(dec)
    def _():
        load_d.start()

    barrier = pltpu.get_barrier_semaphore()
    pl.semaphore_signal(barrier, inc=1, device_id={"tensor": sib}, device_id_type=MESH)
    pl.semaphore_signal(barrier, inc=1, device_id={"tensor": across}, device_id_type=MESH)
    pl.semaphore_signal(barrier, inc=1, device_id={"tensor": diag}, device_id_type=MESH)
    pl.semaphore_signal(barrier, inc=1, device_id={"section": other}, device_id_type=MESH)

    mod[...] = jnp.zeros_like(mod)
    gacc[...] = jnp.zeros_like(gacc)
    sacc[...] = jnp.zeros_like(sacc)
    dmod[...] = jnp.zeros_like(dmod)

    pl.semaphore_wait(barrier, 4)

    def remote(src, dst, send_sem, recv_sem, where):
        return pltpu.make_async_remote_copy(
            src_ref=src, dst_ref=dst, send_sem=send_sem, recv_sem=recv_sem, device_id=where, device_id_type=MESH
        )

    def gather(which, buf, n, kind):
        src, dst, where = ((0, rows, across), (0, 2 * rows, sib), (rows, 3 * rows, sib))[kind]
        return remote(
            buf.at[n, pl.ds(src, rows)],
            buf.at[n, pl.ds(dst, rows)],
            ag_sems.at[which, 2 * kind, n],
            ag_sems.at[which, 2 * kind + 1, n],
            {"tensor": where},
        )

    def its_tiles(device):
        return pl.ds(pl.multiple_of(device * (2 * LANES), LANES), 3 * LANES)

    def mod_copy(k):
        return remote(mod_cols, mod_recv.at[k], mod_sems.at[0, k], mod_sems.at[1, k], {"tensor": peers[k]})

    def dmod_copy(k, n):
        return remote(
            dmod.at[n, :, its_tiles(peers[k])],
            mod_recv.at[k, n],
            dmod_sems.at[0, k, n],
            dmod_sems.at[1, k, n],
            {"tensor": peers[k]},
        )

    for k in (1, 2, 0):
        mod_copy(k).start()

    @pl.when(enc)
    def _():
        load_x.wait()
        a1f[0, 0:rows, :] = xin[0]
        gather(0, a1f, 0, 0).start()
        gather(0, a1f, 0, 1).start()

    @pl.when(dec)
    def _():
        load_d.wait()

    for copy in load_w:
        copy.start()
    mod[:, :, its_tiles(me)] = mod_cols[...]

    gains[0:1, :] = dot(q_gain[...], select[...])
    gains[1:2, :] = dot(k_gain[...], select[...])
    for j in range(4):
        load_raw[2 * j].wait()
        load_raw[2 * j + 1].wait()
        ref = wqkv.at[j] if j < 3 else wout
        for at, size in wide:
            span = pl.ds(at, size)
            value = dot_tn(select[0:tokens, :], dattn[2 * j, :, span])
            value += dot_tn(select[tokens:part, :], dattn[2 * j + 1, 0 : part - tokens, span])
            ref[:, span] = value.astype(BF)

    spots = jnp.concatenate([places[i] for i in range(places.shape[0])], axis=0).astype(F32).T
    lane = lax.broadcasted_iota(jnp.int32, (rows, LANES), 1)
    spot = lax.rem(lane, 2 * GRID)
    by_row, used = spot < GRID, lane < 6 * GRID
    spot = jnp.where(by_row, spot, spot - GRID).astype(F32)
    for block in range(4):
        high, low, my_high, my_low = block // 2, block % 2, lax.div(me, 2), lax.rem(me, 2)
        at = high + my_high - 2 * high * my_high + 2 * (low + my_low - 2 * low * my_low)
        here = pl.ds(pl.multiple_of(at * rows, rows), rows)
        mine = slice(block * rows, (block + 1) * rows)
        for n in range(images):
            row = jnp.floor(spots[mine, n : n + 1] * (1.0 / GRID))
            marks = jnp.where(by_row, row, spots[mine, n : n + 1] - GRID * row) == spot
            turns[n, here, :] = dot(jnp.where(marks & used, 1.0, 0.0).astype(BF), angles[...])

    for k in range(3):
        mod_copy(k).wait()
        mod[:, :, its_tiles(peers[k])] += mod_recv[k]

    def gather_start(which, buf, n):
        gather(which, buf, n, 0).start()
        gather(which, buf, n, 1).start()

    def gather_relay(which, buf, n):
        gather(which, buf, n, 0).wait_recv()
        gather(which, buf, n, 2).start()

    def attn_relay(n):
        @pl.when(enc)
        def _():
            gather(0, a1f, n, 0).wait_recv()

        @pl.when(dec)
        def _():
            zy_pass(n).wait_recv()
            values = a1f[n, rows : 2 * rows, :].astype(F32)
            a1f[n, rows : 2 * rows, :] = modulated(values, mod_row(n, 0), mod_row(n, 1)).astype(BF)

        gather(0, a1f, n, 2).start()

    def gather_wait(which, buf, n):
        gather(which, buf, n, 1).wait_recv()
        gather(which, buf, n, 2).wait_recv()

    def gather_drain(which, buf, n):
        for kind in range(3):
            gather(which, buf, n, kind).wait_send()

    def to_sibling(which, n):
        return remote(
            send_a.at[which, lax.rem(n, KEEP)],
            recv_a.at[which, lax.rem(n, SLOTS)],
            rs_sems.at[which, 0, n],
            rs_sems.at[which, 1, n],
            {"tensor": sib},
        )

    def over_y(which, n):
        return remote(
            send_y.at[which, lax.rem(n, KEEP)],
            recv_y.at[which, lax.rem(n, SLOTS)],
            rs_sems.at[which, 2, n],
            rs_sems.at[which, 3, n],
            {"tensor": across},
        )

    def scatter_put(which, n, at, size, values):
        kind, own = which, lax.rem(n, KEEP)
        keep[kind, own, :, pl.ds(at, size)] = values[0 : 2 * rows]
        send_a[kind, own, :, pl.ds(at, size)] = values[2 * rows : 4 * rows].astype(BF)

    def scatter_start(which, n):
        to_sibling(which, n).start()

    def scatter_middle(which, n):
        kind, own, slot = which, lax.rem(n, KEEP), lax.rem(n, SLOTS)
        to_sibling(which, n).wait()
        theirs = recv_a[kind, slot, rows : 2 * rows].astype(F32)
        send_y[kind, own] = (keep[kind, own, rows : 2 * rows] + theirs).astype(BF)
        over_y(which, n).start()

    def scatter_end(which, n):
        kind, own, slot = which, lax.rem(n, KEEP), lax.rem(n, SLOTS)
        over_y(which, n).wait()
        mine = keep[kind, own, 0:rows] + recv_a[kind, slot, 0:rows].astype(F32)
        return mine + recv_y[kind, slot].astype(F32)

    def z_copy(n):
        return remote(zout.at[n], xin.at[n], zx_sems.at[0, n], zx_sems.at[1, n], {"section": other})

    def zy_copy(n):
        return remote(
            zout.at[n], dattn.at[n, pl.ds(rows, rows)], zx_sems.at[4, n], zx_sems.at[5, n], {"tensor": across}
        )

    def zy_pass(n):
        return remote(
            dattn.at[n, pl.ds(rows, rows)],
            a1f.at[n, pl.ds(rows, rows)],
            zx_sems.at[6, n],
            zx_sems.at[7, n],
            {"section": other},
        )

    def dz_copy(n):
        return remote(xin.at[n], din.at[n], zx_sems.at[2, n], zx_sems.at[3, n], {"section": other})

    def mod_row(n, row):
        return mod[n, pl.ds(row, 1), :]

    def inverse_rms(values):
        return lax.rsqrt(jnp.mean(values * values, axis=-1, keepdims=True) + EPS)

    def column_sum(values):
        return jnp.sum(values, axis=0, keepdims=True)

    def modulated(values, shift, scale):
        return (values * inverse_rms(values)) * (1.0 + scale) + shift

    def norm_back(values, grad, scale):
        inv = inverse_rms(values)
        normed = values * inv
        d_normed = grad * (1.0 + scale)
        d_values = inv * (d_normed - normed * jnp.mean(d_normed * normed, axis=-1, keepdims=True))
        return d_values, column_sum(grad), column_sum(grad * normed)

    def head_norm(raw):
        inv = lax.rsqrt(jnp.sum(raw * raw, axis=-1, keepdims=True) * (1.0 / HEAD_DIM) + EPS)
        return inv, raw * inv

    def turn(values, c, s):
        return values * c + pltpu.roll(values, 64, 1) * s

    def turn_back(values, c, s):
        return values * c - pltpu.roll(values, 64, 1) * s

    def softmax_parts(scaled, k):
        powered = jnp.exp2(dot_nt(scaled, k))
        return powered, 1.0 / jnp.sum(powered, axis=-1, keepdims=True)

    def out_copy(which, n):
        src = (a1f, a2f, dffn, dattn, hid_st, mix_st, dgu_st, dqkv_st)[which]
        dst = (a1_hbm, a2_hbm, dffn_hbm, dattn_hbm, hid_hbm, mix_hbm, dgu_hbm, dqkv_hbm)[which]
        return pltpu.make_async_copy(src.at[n] if which < 4 else src, dst.at[n], out_sems.at[which, n])

    def staged_ready(which, n):
        @pl.when(n > 0)
        def _():
            out_copy(which, n - 1).wait()

    def attn_in(n):
        @pl.when(dec)
        def _():
            z_copy(n).wait_recv()

        values = xin[n].astype(F32)
        sacc[0:1, :] += column_sum(values * values)

        @pl.when(dec | (n > 0))
        def _():
            a1f[n, 0:rows, :] = modulated(values, mod_row(n, 0), mod_row(n, 1)).astype(BF)

            @pl.when(enc)
            def _():
                gather(0, a1f, n, 0).start()

            gather(0, a1f, n, 1).start()

    def attn_drain(n):
        gather(0, a1f, n, 1).wait_send()
        gather(0, a1f, n, 2).wait_send()

        @pl.when(enc)
        def _():
            gather(0, a1f, n, 0).wait_send()

    def attn_compute(n):
        gather_wait(0, a1f, n)

        @pl.when(enc & (n == 0))
        def _():
            attn_drain(n)
            for at in range(0, 4 * rows, rows):
                values = a1f[0, at : at + rows, :].astype(F32)
                a1f[0, at : at + rows, :] = modulated(values, mod_row(0, 0), mod_row(0, 1)).astype(BF)

        staged_ready(5, n)
        a1 = a1f[n]
        c, s = turns[n, :, 0:LANES], turns[n, :, LANES : 2 * LANES]
        for pair in range(heads // 2):
            span = pl.ds(pair * 2 * LANES, 2 * LANES)
            q2 = dot_nt(a1, wqkv[0, span, :])
            k2 = dot_nt(a1, wqkv[1, span, :])
            v2 = dot_nt(a1, wqkv[2, span, :]).astype(BF)
            for half in range(2):
                at = (pair * 2 + half) * LANES
                cut = slice(half * LANES, (half + 1) * LANES)
                q_gain = gains[0:1, at : at + LANES] * (SCALE * LOG2E)
                q = turn(head_norm(q2[:, cut])[1] * q_gain, c, s).astype(BF)
                k = turn(head_norm(k2[:, cut])[1] * gains[1:2, at : at + LANES], c, s).astype(BF)
                powered, inverse = softmax_parts(q, k)
                mix_st[:, at : at + LANES] = (dot(powered.astype(BF), v2[:, cut]) * inverse).astype(BF)
        mixed = mix_st[...]
        for at, size in wide:
            scatter_put(0, n, at, size, dot(mixed, wout[:, pl.ds(at, size)]))
        scatter_start(0, n)
        out_copy(5, n).start()
        out_copy(0, n).start()

        @pl.when(dec | (n > 0))
        def _():
            attn_drain(n)

    def ffn_in(n):
        attended = scatter_end(0, n)
        attns[n] = attended.astype(BF)
        values = xin[n].astype(F32) + mod_row(n, 2) * attended
        x1s[n] = values
        sacc[1:2, :] += column_sum(values * values)
        a2f[n, 0:rows, :] = modulated(values, mod_row(n, 3), mod_row(n, 4)).astype(BF)
        gather_start(1, a2f, n)

    def ffn_down(n, units):
        for at, size in wide:
            scatter_put(1, n, at, size, dot(units, wdn[:, pl.ds(at, size)]))
        scatter_start(1, n)
        out_copy(1, n).start()
        gather_drain(1, a2f, n)

    def first_ffn(n):
        gather_wait(1, a2f, n)

        @pl.when(n == 0)
        def _():
            load_w[0].wait()
            load_w[1].wait()

    def ffn_compute(n):
        @pl.when(enc)
        def _():
            first_ffn(n)
            a2 = a2f[n]
            for at, size in chunks_of(hidden, 256):
                span = pl.ds(at, size)
                gate_val = dot(a2, wgu[0, :, span])
                up_val = dot(a2, wgu[1, :, span])
                hid_st[:, span] = (gate_val * jax.nn.sigmoid(gate_val) * up_val).astype(BF)
            ffn_down(n, hid_st[...])

    def block_out(n):
        feedfwd = scatter_end(1, n)
        ffns[n] = feedfwd.astype(BF)
        values = x1s[n] + mod_row(n, 5) * feedfwd
        sacc[2:3, :] += column_sum(values * values)
        zout[n] = values.astype(BF)

        @pl.when(enc)
        def _():
            z_copy(n).start()
            zy_copy(n).start()

        @pl.when(dec)
        def _():
            dmod[n, 5:6, :] = column_sum(din[n].astype(F32) * feedfwd)

    def pass_on(n):
        @pl.when(enc)
        def _():
            zy_copy(n).wait_recv()
            zy_pass(n).start()

        @pl.when(dec)
        def _():
            send_dmod(n)

    def send_dmod(n):
        for k in range(3):
            dmod_copy(k, n).start()

    def ffn_grad_in(n):
        @pl.when(enc)
        def _():
            zy_copy(n).wait_send()
            zy_pass(n).wait_send()
            dz_copy(n).wait_recv()

        grad = din[n].astype(F32)
        dffn[n, 0:rows, :] = (mod_row(n, 5) * grad).astype(BF)
        gather_start(2, dffn, n)

        @pl.when(enc)
        def _():
            dmod[n, 5:6, :] = column_sum(grad * ffns[n].astype(F32))

    def ffn_grad_compute(n):
        @pl.when(dec)
        def _():
            first_ffn(n)

        gather_wait(2, dffn, n)
        staged_ready(4, n)
        staged_ready(6, n)
        grad = dffn[n]
        a2 = a2f[n]
        for at, size in chunks_of(hidden, 256):
            span = pl.ds(at, size)
            gate_val = dot(a2, wgu[0, :, span])
            up_val = dot(a2, wgu[1, :, span])
            d_hidden = dot_nt(grad, wdn[span, :])
            sig = jax.nn.sigmoid(gate_val)
            act = gate_val * sig
            hid_st[:, span] = (act * up_val).astype(BF)
            dgu_st[:, span] = (d_hidden * up_val * (sig + act * (1.0 - sig))).astype(BF)
            dgu_st[:, pl.ds(hidden + at, size)] = (d_hidden * act).astype(BF)
        d_gate = dgu_st[:, 0:hidden]
        d_up = dgu_st[:, hidden : 2 * hidden]
        for at, size in wide:
            span = pl.ds(at, size)
            scatter_put(2, n, at, size, dot_nt(d_gate, wgu[0, span, :]) + dot_nt(d_up, wgu[1, span, :]))
        scatter_start(2, n)

        @pl.when(dec)
        def _():
            ffn_down(n, hid_st[...])

        out_copy(4, n).start()
        out_copy(6, n).start()
        out_copy(2, n).start()
        gather_drain(2, dffn, n)

    def attn_grad_in(n):
        d_a2 = scatter_end(2, n)
        grad, d_shift, d_scale = norm_back(x1s[n], d_a2, mod_row(n, 4))
        grad = grad + din[n].astype(F32)
        dxout[n] = grad
        dattn[n, 0:rows, :] = (mod_row(n, 2) * grad).astype(BF)
        gather_start(3, dattn, n)
        dmod[n, 2:3, :] = column_sum(grad * attns[n].astype(F32))
        dmod[n, 3:4, :] = d_shift
        dmod[n, 4:5, :] = d_scale

    def attn_grad_compute(n):
        gather_wait(3, dattn, n)
        staged_ready(7, n)
        grad = dattn[n]
        a1 = a1f[n]
        c, s = turns[n, :, 0:LANES], turns[n, :, LANES : 2 * LANES]
        lanes_all = heads * LANES
        for pair in range(heads // 2):
            span = pl.ds(pair * 2 * LANES, 2 * LANES)
            q2 = dot_nt(a1, wqkv[0, span, :])
            k2 = dot_nt(a1, wqkv[1, span, :])
            v2 = dot_nt(a1, wqkv[2, span, :]).astype(BF)
            d_mix2 = dot_nt(grad, wout[span, :])
            for half in range(2):
                at = (pair * 2 + half) * LANES
                cut = slice(half * LANES, (half + 1) * LANES)
                q_gain, k_gain = gains[0:1, at : at + LANES], gains[1:2, at : at + LANES]
                q_inv, q_norm = head_norm(q2[:, cut])
                k_inv, k_norm = head_norm(k2[:, cut])
                q = turn(q_norm * (q_gain * (SCALE * LOG2E)), c, s).astype(BF)
                k = turn(k_norm * k_gain, c, s).astype(BF)
                v = v2[:, cut]
                powered, inverse = softmax_parts(q, k)
                low = powered.astype(BF)
                mixed = dot(low, v) * inverse
                d_mix = d_mix2[:, cut] * inverse
                d_mix = d_mix.astype(BF)
                taken = jnp.sum(d_mix.astype(F32) * mixed, axis=-1, keepdims=True)
                d_v = dot_tn(low, d_mix)
                d_scores = (powered * (dot_nt(d_mix, v) - taken)).astype(BF)
                d_q = turn_back(dot(d_scores, k) * SCALE, c, s)
                d_k = turn_back(dot_tn(d_scores, q) * (1.0 / LOG2E), c, s)
                gacc[0:1, at : at + LANES] += column_sum(d_q * q_norm)
                gacc[1:2, at : at + LANES] += column_sum(d_k * k_norm)
                d_q = d_q * q_gain
                d_k = d_k * k_gain
                d_q = q_inv * (d_q - q_norm * (jnp.sum(d_q * q_norm, axis=-1, keepdims=True) * (1.0 / HEAD_DIM)))
                d_k = k_inv * (d_k - k_norm * (jnp.sum(d_k * k_norm, axis=-1, keepdims=True) * (1.0 / HEAD_DIM)))
                dqkv_st[:, at : at + LANES] = d_q.astype(BF)
                dqkv_st[:, lanes_all + at : lanes_all + at + LANES] = d_k.astype(BF)
                dqkv_st[:, 2 * lanes_all + at : 2 * lanes_all + at + LANES] = d_v.astype(BF)
        for at, size in wide:
            span = pl.ds(at, size)
            total = dot(dqkv_st[:, 0:lanes_all], wqkv[0, :, span])
            total += dot(dqkv_st[:, lanes_all : 2 * lanes_all], wqkv[1, :, span])
            total += dot(dqkv_st[:, 2 * lanes_all : 3 * lanes_all], wqkv[2, :, span])
            scatter_put(3, n, at, size, total)
        scatter_start(3, n)
        out_copy(7, n).start()
        out_copy(3, n).start()
        gather_drain(3, dattn, n)

    def block_grad_out(n):
        d_a1 = scatter_end(3, n)
        grad, d_shift, d_scale = norm_back(xin[n].astype(F32), d_a1, mod_row(n, 1))
        grad = grad + dxout[n]
        dxout[n] = grad
        dmod[n, 0:1, :] = d_shift
        dmod[n, 1:2, :] = d_scale

        @pl.when(dec)
        def _():
            xin[n] = grad.astype(BF)
            dz_copy(n).start()

        @pl.when(enc)
        def _():
            send_dmod(n)

    works = (
        attn_in,
        attn_relay,
        attn_compute,
        lambda n: scatter_middle(0, n),
        ffn_in,
        lambda n: gather_relay(1, a2f, n),
        ffn_compute,
        lambda n: scatter_middle(1, n),
        block_out,
        ffn_grad_in,
        lambda n: gather_relay(2, dffn, n),
        ffn_grad_compute,
        lambda n: scatter_middle(2, n),
        attn_grad_in,
        lambda n: gather_relay(3, dattn, n),
        attn_grad_compute,
        lambda n: scatter_middle(3, n),
        block_grad_out,
        pass_on,
    )

    def run_work(work, n, low, high):
        if high - low == 1:
            works[low](n)
            return
        middle = (low + high) // 2

        @pl.when(work < middle)
        def _():
            run_work(work, n, low, middle)

        @pl.when(work >= middle)
        def _():
            run_work(work, n, middle, high)

    base = len(works) * images
    tables = [order_words(order, base) for order in ORDERS]

    def entry_of(i):
        rest, values = i, [low + section * (high - low) for low, high in zip(*tables)]
        while len(values) > 1:
            bit, rest = lax.rem(rest, 2), lax.div(rest, 2)
            values = [low + bit * (high - low) for low, high in zip(values[0::2], values[1::2])]
        return values[0]

    def word_step(i, carry):
        def work_step(_, word):
            entry, word = lax.rem(word, base), lax.div(word, base)
            work, n = lax.div(entry, images), lax.rem(entry, images)
            run_work(work, n, 0, len(works))
            return word

        lax.fori_loop(0, PACK, work_step, entry_of(i))
        return carry

    lax.fori_loop(0, base // PACK, word_step, 0)

    for which in (4, 5, 6, 7):
        out_copy(which, images - 1).wait()

    def drain(n, carry):
        for which in (0, 1, 2, 3):
            out_copy(which, n).wait()
        part = dmod[n, :, its_tiles(me)]
        for k in range(3):
            dmod_copy(k, n).wait()
            part += mod_recv[k, n]
        for j in range(8):
            mod[j, pl.ds(n, 1), 0 : 3 * LANES] = part[j : j + 1]

        @pl.when(enc)
        def _():
            z_copy(n).wait_send()

        @pl.when(dec)
        def _():
            dz_copy(n).wait_send()

        return carry

    lax.fori_loop(0, images, drain, 0)
    dmod_part[...] = mod[:, :, 0 : 3 * LANES].astype(BF)


def run_main(tok, vel, mod_cols, places, angles, qkv, out, wgu, wdn, q_gain, k_gain, select):
    images, rows, width = tok.shape
    tokens = 4 * rows
    lanes_all = select.shape[1]
    heads = lanes_all // LANES
    hidden = wdn.shape[0]
    vmem = pl.BlockSpec(memory_space=pltpu.VMEM)
    anywhere = pl.BlockSpec(memory_space=pl.ANY)

    def hbm(last):
        return jax.ShapeDtypeStruct((images, tokens, last), BF)

    out_shape = (
        jax.ShapeDtypeStruct((images, rows, width), BF),
        jax.ShapeDtypeStruct((images, rows, width), F32),
        jax.ShapeDtypeStruct((8, images, 3 * LANES), BF),
        jax.ShapeDtypeStruct((8, lanes_all), F32),
        jax.ShapeDtypeStruct((8, width), F32),
        hbm(width),
        hbm(width),
        hbm(width),
        hbm(width),
        hbm(hidden),
        hbm(lanes_all),
        hbm(2 * hidden),
        hbm(3 * lanes_all),
    )
    scratch = [
        pltpu.VMEM((images, tokens, 2 * LANES), F32),
        pltpu.VMEM((3, lanes_all, width), BF),
        pltpu.VMEM((lanes_all, width), BF),
        pltpu.VMEM(wgu.shape, BF),
        pltpu.VMEM(wdn.shape, BF),
        pltpu.VMEM((8, lanes_all), F32),
        pltpu.VMEM((images, rows, width), BF),
        pltpu.VMEM((images, rows, width), BF),
        pltpu.VMEM((images, tokens, width), BF),
        pltpu.VMEM((images, tokens, width), BF),
        pltpu.VMEM((images, tokens, width), BF),
        pltpu.VMEM((images, tokens, width), BF),
        pltpu.VMEM((images, rows, width), F32),
        pltpu.VMEM((images, rows, width), BF),
        pltpu.VMEM((images, rows, width), BF),
        pltpu.VMEM((4, KEEP, 2 * rows, width), F32),
        pltpu.VMEM((4, KEEP, 2 * rows, width), BF),
        pltpu.VMEM((4, SLOTS, 2 * rows, width), BF),
        pltpu.VMEM((4, KEEP, rows, width), BF),
        pltpu.VMEM((4, SLOTS, rows, width), BF),
        pltpu.VMEM((tokens, lanes_all), BF),
        pltpu.VMEM((tokens, hidden), BF),
        pltpu.VMEM((tokens, 2 * hidden), BF),
        pltpu.VMEM((tokens, 3 * lanes_all), BF),
        pltpu.VMEM((images, 8, width), F32),
        pltpu.VMEM((3, images, 8, 3 * LANES), F32),
        pltpu.VMEM((images, 8, width), F32),
        pltpu.SemaphoreType.DMA((2, 3)),
        pltpu.SemaphoreType.DMA((2, 3, images)),
        pltpu.SemaphoreType.DMA((4, 6, images)),
        pltpu.SemaphoreType.DMA((4, 4, images)),
        pltpu.SemaphoreType.DMA((8, images)),
        pltpu.SemaphoreType.DMA((8, images)),
        pltpu.SemaphoreType.DMA((12,)),
    ]
    return pl.pallas_call(
        functools.partial(main_kernel, images, heads),
        out_shape=out_shape,
        in_specs=[anywhere, anywhere] + [vmem] * 3 + [anywhere] * 4 + [vmem] * 3,
        out_specs=[vmem] * 5 + [anywhere] * 8,
        scratch_shapes=scratch,
        compiler_params=pltpu.CompilerParams(
            collective_id=0, has_side_effects=True, vmem_limit_bytes=63 * 2**20
        ),
    )(tok, vel, mod_cols, places, angles, qkv, out, wgu, wdn, q_gain, k_gain, select)


def flat_plan(width, hidden, part):
    blocks = width // LANES
    segments = ((2 * hidden // LANES, width), (blocks, hidden), (blocks, 3 * part), (blocks, part))
    halves = [count * rows // 2 for count, rows in segments]
    half, chunk = sum(halves), width // 2
    assert half % chunk == 0

    def pieces(segment, block):
        rows, cut, at = segments[segment][1], halves[segment], sum(halves[:segment])
        low, high = block * rows, (block + 1) * rows
        if high <= cut:
            return [(at + low, 0, rows)]
        if low >= cut:
            return [(half + at + low - cut, 0, rows)]
        return [(at + low, 0, cut - low), (half + at, cut - low, high - cut)]

    return half, chunk, pieces


def tail_kernel(
    dp,
    a2_hbm,
    dgu_hbm,
    hid_hbm,
    dffn_hbm,
    a1_hbm,
    dqkv_hbm,
    mix_hbm,
    dattn_hbm,
    mod_hbm,
    pick,
    cond,
    squares,
    silu,
    dmod_low,
    gain_sums,
    labels,
    totals,
    dmod_all,
    sum_all,
    extra_all,
    left_a,
    right_a,
    left_b,
    right_b,
    turned,
    own,
    arrived,
    mod_w,
    summand,
    sum_st,
    sum_recv,
    load_sems,
    part_sems,
    total_sems,
    sum_sems,
    all_sems,
    x_part_sems,
    x_total_sems,
    here,
):
    section = lax.axis_index("section")
    place = lax.axis_index("dp")
    me = lax.axis_index("tensor")
    sib = me + 1 - 2 * lax.rem(me, 2)
    across = lax.rem(me + 2, 4)
    enc, dec = section == 0, section == 1
    width, hidden = left_a.shape[1], left_b.shape[1]
    part, lanes_all = pick.shape
    half, chunk, pieces = flat_plan(width, hidden, part)
    whole = half // chunk
    count = jnp.where(enc, whole - LENT, whole + LENT)

    tokens, ahead = left_a.shape[0], 2 * LANES
    quarter = tokens // 4

    def some_rows(i):
        rows = pl.ds(i * quarter, quarter)
        return a2_hbm.at[rows], left_a.at[rows]

    def some_columns(at, size):
        cols = pl.ds(at, size)
        return dgu_hbm.at[:, cols], right_a.at[:, cols]

    loads = [
        pltpu.make_async_copy(src, dst, load_sems.at[i])
        for i, (src, dst) in enumerate(
            (
                some_rows(0),
                some_rows(1),
                some_rows(2),
                some_rows(3),
                some_columns(0, ahead),
                some_columns(hidden, ahead),
                some_columns(ahead, hidden - ahead),
                some_columns(hidden + ahead, hidden - ahead),
                (hid_hbm, left_b),
                (dffn_hbm, right_b),
                (mix_hbm, left_b.at[:, pl.ds(0, lanes_all)]),
                (a1_hbm, left_a),
                (dqkv_hbm, right_a),
                (dattn_hbm, right_b),
            )
        )
    ]
    for i in range(10):
        loads[i].start()

    mod_w[...] = jnp.zeros_like(mod_w)
    mine = pl.ds(pl.multiple_of(me * (part - 2 * LANES), 16), part)
    mod_loads = [pltpu.make_async_copy(mod_hbm.at[j], mod_w.at[j, mine], load_sems.at[14 + j]) for j in range(6)]
    for copy in mod_loads:
        copy.start()

    barrier = pltpu.get_barrier_semaphore()
    for where in ({"tensor": sib}, {"tensor": across}):
        pl.semaphore_signal(barrier, inc=1, device_id=where, device_id_type=MESH)

    @pl.when(dec)
    def _():
        pl.semaphore_signal(barrier, inc=1, device_id={"section": 0}, device_id_type=MESH)

    for k in range(1, dp):
        pl.semaphore_signal(barrier, inc=1, device_id={"dp": lax.rem(place + k, dp)}, device_id_type=MESH)

    def put(segment, block, first, value):
        for at, low, size in pieces(segment, block):
            begin, end = max(low, first), min(low + size, first + value.shape[0])
            if begin < end:
                own[at + begin - low : at + end - low, :] = value[begin - first : end - first].astype(BF)

    def put_wide(segment, block, first, value):
        for i in range(value.shape[1] // LANES):
            put(segment, block + i, first, value[:, i * LANES : (i + 1) * LANES])

    def turn_left(ref, first, last):
        cols = ref.shape[1]
        for at in range(first, last, 256):
            turned[0:cols, at : at + 256] = ref[at : at + 256, :].T

    def gate_up_blocks(*blocks):
        for block in blocks:
            value = dot(turned[...], right_a[:, block * LANES : (block + 2) * LANES])
            put_wide(0, block, 0, value)

    def qkv_heads(*pairs):
        kept = 2 * HEAD_DIM
        for pair in pairs:
            value = dot_tn(right_a[:, pair * 2 * LANES : (pair + 1) * 2 * LANES], left_a[...]).astype(BF)
            put_wide(2, 0, pair * kept, dot(pick[0:kept, 0 : 2 * LANES], value))

    def portion(i):
        tiles, gu_half = width // LANES, hidden // LANES
        pairs = 3 * lanes_all // (2 * LANES)
        if i == 0:
            for k in range(4):
                loads[k].wait()
                turn_left(left_a, k * quarter, (k + 1) * quarter)
            loads[11].start()
            loads[4].wait()
            gate_up_blocks(0)
            loads[5].wait()
            gate_up_blocks(gu_half)
        elif i == 1:
            loads[6].wait()
            loads[7].wait()
            gate_up_blocks(2, gu_half + 2)
        elif i == 2:
            gate_up_blocks(*range(4, gu_half, 2), *range(gu_half + 4, 2 * gu_half, 2))
            loads[12].start()
        elif i == 3:
            loads[8].wait()
            turn_left(left_b, 0, tokens)
            loads[10].start()
            loads[9].wait()
            for block in range(0, tiles, 2):
                cut = slice(block * LANES, min(width, (block + 2) * LANES))
                put_wide(1, block, 0, dot(turned[0:hidden, :], right_b[:, cut]))
            loads[13].start()
        elif i == 4:
            loads[11].wait()
            loads[12].wait()
            qkv_heads(*range(0, pairs // 2))
        elif i == 5:
            qkv_heads(*range(pairs // 2, pairs))
        elif i == 6:
            loads[10].wait()
            loads[13].wait()
            value = dot(pick[...], dot_tn(left_b[:, 0:lanes_all], right_b[...]).astype(BF))
            put_wide(3, 0, 0, value)

    def along(direction, onward):
        step = 1 if (direction == 0) == onward else dp - 1
        return {"dp": lax.rem(place + step, dp)}

    def behind(direction):
        return place if direction == 0 else dp - 1 - place

    def rows_of(direction, c):
        lent = 2 * half + (direction * LENT + c - whole) * chunk
        return pl.ds(pl.multiple_of(jnp.where(c < whole, direction * half + c * chunk, lent), chunk), chunk)

    def lent_copy(ref, sems, direction, i, to_decoder):
        mine = rows_of(direction, whole - LENT + i)
        theirs = rows_of(direction, whole + i)
        return pltpu.make_async_remote_copy(
            src_ref=ref.at[mine if to_decoder else theirs],
            dst_ref=ref.at[theirs if to_decoder else mine],
            send_sem=sems.at[direction, 0, i],
            recv_sem=sems.at[direction, 1, i],
            device_id={"section": 1 if to_decoder else 0},
            device_id_type=MESH,
        )

    def lent_part(direction, i):
        return lent_copy(own, x_part_sems, direction, i, True)

    def lent_total(direction, i):
        return lent_copy(totals, x_total_sems, direction, i, False)

    def part_copy(direction, c):
        return pltpu.make_async_remote_copy(
            src_ref=own.at[rows_of(direction, c)],
            dst_ref=arrived.at[rows_of(direction, c)],
            send_sem=part_sems.at[direction, 0, c],
            recv_sem=part_sems.at[direction, 1, c],
            device_id=along(direction, True),
            device_id_type=MESH,
        )

    def total_copy(direction, c):
        return pltpu.make_async_remote_copy(
            src_ref=totals.at[rows_of(direction, c)],
            dst_ref=totals.at[rows_of(direction, c)],
            send_sem=total_sems.at[direction, 0, c],
            recv_sem=total_sems.at[direction, 1, c],
            device_id=along(direction, False),
            device_id_type=MESH,
        )

    def add_part(direction, c):
        begins, ends = behind(direction) == 0, behind(direction) == dp - 1
        rows = rows_of(direction, c)

        @pl.when(c >= whole)
        def _():
            lent_part(direction, c - whole).wait_recv()

        @pl.when(begins)
        def _():
            part_copy(direction, c).start()

        @pl.when(jnp.logical_not(begins))
        def _():
            part_copy(direction, c).wait_recv()
            value = (own[rows, :].astype(F32) + arrived[rows, :].astype(F32)).astype(BF)

            @pl.when(ends)
            def _():
                totals[rows, :] = value
                total_copy(direction, c).start()

            @pl.when(jnp.logical_not(ends))
            def _():
                own[rows, :] = value
                part_copy(direction, c).start()

    def pass_total(direction, c):
        begins, ends = behind(direction) == 0, behind(direction) == dp - 1
        passes = jnp.logical_not(begins) & jnp.logical_not(ends)
        back = c >= whole

        @pl.when(passes | (back & jnp.logical_not(ends)))
        def _():
            total_copy(direction, c).wait_recv()

        @pl.when(passes)
        def _():
            total_copy(direction, c).start()

        @pl.when(back)
        def _():
            lent_total(direction, c - whole).start()

    skew = 2

    def chunk_step(step):
        for direction in range(2):
            c = step - skew * behind(direction)

            @pl.when((c >= 0) & (c < count))
            def _():
                add_part(direction, c)

        for direction in range(2):
            u = step - skew * (2 * (dp - 1) - behind(direction))

            @pl.when((u >= 0) & (u < count))
            def _():
                pass_total(direction, u)

        for i in range(4):

            @pl.when(step == jnp.where(enc, 12, 22) + i)
            def _():
                small(i)

    def sum_copy(which):
        where = ({"section": 1 - section}, {"tensor": sib}, {"tensor": across})[which]
        height = (8, 16, 16)[which]
        src = summand if which == 0 else sum_st.at[which - 1]
        return pltpu.make_async_remote_copy(
            src_ref=src.at[pl.ds(0, height)],
            dst_ref=sum_recv.at[which, pl.ds(0, height)],
            send_sem=sum_sems.at[which, 0],
            recv_sem=sum_sems.at[which, 1],
            device_id=where,
            device_id_type=MESH,
        )

    def all_copy(which, k, outgoing):
        ref = (dmod_all, sum_all, extra_all)[which]
        peer = lax.rem(place + k, dp)
        slot = place if outgoing else peer
        return pltpu.make_async_remote_copy(
            src_ref=ref.at[slot],
            dst_ref=ref.at[slot],
            send_sem=all_sems.at[which, 0, k],
            recv_sem=all_sems.at[which, 1, slot],
            device_id={"dp": peer},
            device_id_type=MESH,
        )

    def small(step):
        if step == 0:
            dmod_all[place] = dmod_low[...]
            for k in range(1, dp):
                all_copy(0, k, True).start()

            for copy in mod_loads:
                copy.wait()
            images = cond.shape[0]
            grads = dmod_low[...].astype(F32)
            d_silu = dot(grads[0:images].astype(BF), mod_w[0])
            for j in range(1, 6):
                d_silu += dot(grads[j * images : (j + 1) * images].astype(BF), mod_w[j])
            sig = jax.nn.sigmoid(cond[...])
            summand[0:8, :] = d_silu * (sig + cond[...] * sig * (1.0 - sig))
            summand[8:16, :] = squares[...]

            @pl.when(dec)
            def _():
                pl.semaphore_wait(here, 1)

            sum_copy(0).start()
        elif step == 1:
            sum_copy(0).wait()
            sum_st[0] = summand[...]
            sum_st[0, 0:8, :] += sum_recv[0, 0:8, :]
            sum_copy(1).start()
        elif step == 2:
            sum_copy(1).wait()
            sum_st[1] = sum_st[0] + sum_recv[1]
            sum_copy(2).start()
        elif step == 3:
            sum_copy(2).wait()
            total = sum_st[1] + sum_recv[2]
            sum_all[place, 0:8, :] = total[0:8].astype(BF)
            sum_all[place, 8:16, :] = silu[...]
            square = total[8:16, 0:LANES]
            for i in range(1, width // LANES):
                square += total[8:16, i * LANES : (i + 1) * LANES]
            extra_all[place, 0:8, :] = gain_sums[...]
            extra_all[place, 8:16, :] = jnp.zeros_like(gain_sums)
            extra_all[place, 8:16, 0:LANES] = square
            for i in range(8):
                extra_all[place, 8 + i : 9 + i, LANES : 2 * LANES] = jnp.full((1, LANES), labels[i].astype(F32))
            for k in range(1, dp):
                all_copy(1, k, True).start()
                all_copy(2, k, True).start()

    portion(0)
    pl.semaphore_wait(barrier, jnp.where(enc, dp + 2, dp + 1))

    @pl.when(enc)
    def _():
        pl.semaphore_signal(here, inc=1, device_id={"section": 1}, device_id_type=MESH)

    for step in range(6):
        chunk_step(step)
        portion(step + 1)

    def lend(i, carry):
        for direction in range(2):
            lent_part(direction, i).start()
        return carry

    @pl.when(enc)
    def _():
        lax.fori_loop(0, LENT, lend, 0)

    def later_step(step, carry):
        chunk_step(step)
        return carry

    lax.fori_loop(6, whole + LENT + 2 * skew * (dp - 1), later_step, 0)

    def lent_back(i, carry):
        for direction in range(2):

            @pl.when(enc)
            def _():
                lent_part(direction, i).wait_send()
                lent_total(direction, i).wait_recv()

            @pl.when(dec)
            def _():
                lent_total(direction, i).wait_send()

        return carry

    lax.fori_loop(0, LENT, lent_back, 0)

    for which in range(3):
        for k in range(1, dp):
            all_copy(which, k, True).wait_send()
            all_copy(which, k, False).wait_recv()

    def drain(c, carry):
        for direction in range(2):

            @pl.when(behind(direction) != dp - 1)
            def _():
                part_copy(direction, c).wait_send()

            @pl.when(behind(direction) != 0)
            def _():
                total_copy(direction, c).wait_send()

            @pl.when((behind(direction) == 0) & (c < whole))
            def _():
                total_copy(direction, c).wait_recv()

        return carry

    lax.fori_loop(0, count, drain, 0)


def run_tail(dp, a2, dgu, hid, dffn, a1, dqkv, mix, dattn, mod_w, pick, cond, squares, silu, dmod_low, gain_sums, labels):
    tokens, width = a2.shape
    hidden = hid.shape[1]
    vmem = pl.BlockSpec(memory_space=pltpu.VMEM)
    anywhere = pl.BlockSpec(memory_space=pl.ANY)
    half, chunk, _ = flat_plan(width, hidden, pick.shape[0])
    flat_rows, chunks = 2 * (half + LENT * chunk), half // chunk + LENT
    return pl.pallas_call(
        functools.partial(tail_kernel, dp),
        out_shape=(
            jax.ShapeDtypeStruct((flat_rows, LANES), BF),
            jax.ShapeDtypeStruct((dp,) + dmod_low.shape, BF),
            jax.ShapeDtypeStruct((dp, 16, width), BF),
            jax.ShapeDtypeStruct((dp, 16, gain_sums.shape[1]), F32),
        ),
        in_specs=[anywhere] * 9 + [vmem] * 6 + [pl.BlockSpec(memory_space=pltpu.SMEM)],
        out_specs=[vmem] * 4,
        scratch_shapes=[
            pltpu.VMEM((tokens, width), BF),
            pltpu.VMEM((tokens, dgu.shape[1]), BF),
            pltpu.VMEM((tokens, hidden), BF),
            pltpu.VMEM((tokens, width), BF),
            pltpu.VMEM((width, tokens), BF),
            pltpu.VMEM((flat_rows, LANES), BF),
            pltpu.VMEM((flat_rows, LANES), BF),
            pltpu.VMEM((6, 3 * LANES, width), BF),
            pltpu.VMEM((16, width), F32),
            pltpu.VMEM((2, 16, width), F32),
            pltpu.VMEM((3, 16, width), F32),
            pltpu.SemaphoreType.DMA((20,)),
            pltpu.SemaphoreType.DMA((2, 2, chunks)),
            pltpu.SemaphoreType.DMA((2, 2, chunks)),
            pltpu.SemaphoreType.DMA((3, 2)),
            pltpu.SemaphoreType.DMA((3, 2, dp)),
            pltpu.SemaphoreType.DMA((2, 2, LENT)),
            pltpu.SemaphoreType.DMA((2, 2, LENT)),
            pltpu.SemaphoreType.REGULAR,
        ],
        compiler_params=pltpu.CompilerParams(
            collective_id=1, has_side_effects=True, vmem_limit_bytes=62 * 2**20
        ),
    )(a2, dgu, hid, dffn, a1, dqkv, mix, dattn, mod_w, pick, cond, squares, silu, dmod_low, gain_sums, labels)


def finish_kernel(
    count,
    flat_hbm,
    z_hbm,
    dx_hbm,
    dmod_all,
    sum_all,
    extra_all,
    select,
    gu_hbm,
    down_hbm,
    qkv_hbm,
    out_hbm,
    z_out,
    dx_out,
    mod_hbm,
    class_hbm,
    q_gain_out,
    k_gain_out,
    stats_out,
    flat,
    gate_up,
    down,
    qkv,
    out,
    mod,
    classes,
    z_rows,
    dx_rows,
    load_sems,
    store_sems,
):
    width, hidden = gate_up.shape[1], gate_up.shape[2]
    part, blocks, hidden_blocks = out.shape[0], width // LANES, hidden // LANES
    _, _, pieces = flat_plan(width, hidden, part)
    groups = (
        [(0, b) for b in range(hidden_blocks)],
        [(0, hidden_blocks + b) for b in range(hidden_blocks)],
        [(1, b) for b in range(blocks)],
        [(2, b) for b in range(blocks)],
        [(3, b) for b in range(blocks)],
    )
    loads = []
    for group in groups:
        spans = []
        for segment, block in group:
            for at, _, size in pieces(segment, block):
                if spans and spans[-1][0] + spans[-1][1] == at:
                    spans[-1][1] += size
                else:
                    spans.append([at, size])
        copies = []
        for at, size in spans:
            rows = pl.ds(at, size)
            sem = load_sems.at[len(loads), len(copies)]
            copies.append(pltpu.make_async_copy(flat_hbm.at[rows], flat.at[rows], sem))
            copies[-1].start()
        loads.append(copies)
    inward = (
        pltpu.make_async_copy(z_hbm, z_rows, load_sems.at[0, 2]),
        pltpu.make_async_copy(dx_hbm, dx_rows, load_sems.at[1, 2]),
    )
    outward = (
        pltpu.make_async_copy(z_rows, z_out, store_sems.at[5]),
        pltpu.make_async_copy(dx_rows, dx_out, store_sems.at[6]),
    )
    for copy in inward:
        copy.start()

    dp, images = dmod_all.shape[0], dmod_all.shape[1] // 8
    me = lax.axis_index("tensor")
    silu = jnp.concatenate([sum_all[p].astype(F32)[8:16] for p in range(dp)], axis=0).astype(BF)
    grad_cond = jnp.concatenate([sum_all[p].astype(F32)[0:8] for p in range(dp)], axis=0).astype(BF)
    dmods = [dmod_all[p].astype(F32) for p in range(dp)]
    mod_stores = []
    for j in range(6):
        grads = jnp.concatenate([dmods[p][j * images : (j + 1) * images] for p in range(dp)], axis=0).astype(BF)
        mod[j] = dot_tn(grads, silu)
        mine = pl.ds(pl.multiple_of(me * (part - 2 * LANES), 8), part)
        mod_stores.append(pltpu.make_async_copy(mod.at[j, mine], mod_hbm.at[j], store_sems.at[8 + j]))
        mod_stores[-1].start()
    labels = jnp.concatenate([extra_all[p, 8:16, LANES : LANES + 1] for p in range(dp)], axis=0)
    lanes = lax.broadcasted_iota(jnp.int32, (dp * images, classes.shape[0]), 1)
    one_hot = jnp.where(lanes == labels.astype(jnp.int32), 1.0, 0.0).astype(BF)
    for at, size in chunks_of(width, 384):
        classes[:, at : at + size] = dot_tn(one_hot, grad_cond[:, at : at + size])
    class_store = pltpu.make_async_copy(classes.at[pl.ds(0, class_hbm.shape[0])], class_hbm, store_sems.at[7])
    class_store.start()

    for i in range(2):
        inward[i].wait()
        outward[i].start()

    gain_sum, squares = extra_all[0, 0:8, :], extra_all[0, 8:16, 0:LANES]
    for p in range(1, dp):
        gain_sum += extra_all[p, 0:8, :]
        squares += extra_all[p, 8:16, 0:LANES]
    gain_sum = lax.dot_general(
        gain_sum,
        select[...].astype(F32),
        (((1,), (1,)), ((), ())),
        precision=lax.Precision.HIGHEST,
        preferred_element_type=F32,
    )
    q_gain_out[...] = gain_sum[0:1]
    k_gain_out[...] = gain_sum[1:2]
    for i in range(3):
        stats_out[0:1, i : i + 1] = jnp.sqrt(jnp.sum(squares[i : i + 1], axis=1, keepdims=True) * (1.0 / count))

    stores = (
        pltpu.make_async_copy(gate_up.at[0], gu_hbm.at[0], store_sems.at[0]),
        pltpu.make_async_copy(gate_up.at[1], gu_hbm.at[1], store_sems.at[1]),
        pltpu.make_async_copy(down, down_hbm, store_sems.at[2]),
        pltpu.make_async_copy(qkv, qkv_hbm, store_sems.at[3]),
        pltpu.make_async_copy(out, out_hbm, store_sems.at[4]),
    )
    for i, group in enumerate(groups):
        for copy in loads[i]:
            copy.wait()
        for segment, block in group:
            for at, low, size in pieces(segment, block):
                value = flat[at : at + size, :].astype(F32)
                rows = slice(low, low + size)
                cols = slice(block * LANES, (block + 1) * LANES)
                if segment == 0:
                    local = block % hidden_blocks
                    gate_up[block // hidden_blocks, rows, local * LANES : (local + 1) * LANES] = value
                elif segment == 1:
                    down[rows, cols] = value
                elif segment == 2:
                    qkv[rows, cols] = value
                else:
                    out[rows, cols] = value
        stores[i].start()
    for copy in (*stores, *outward, *mod_stores, class_store):
        copy.wait()


def run_finish(count, class_count, hidden, flat, z_rows, dx_rows, dmod_all, sum_all, extra_all, select):
    part, width = select.shape[0], sum_all.shape[2]
    vmem = pl.BlockSpec(memory_space=pltpu.VMEM)
    anywhere = pl.BlockSpec(memory_space=pl.ANY)
    shapes = ((2, width, hidden), (hidden, width), (3 * part, width), (part, width))
    return pl.pallas_call(
        functools.partial(finish_kernel, count),
        out_shape=tuple(jax.ShapeDtypeStruct(shape, F32) for shape in shapes)
        + (
            jax.ShapeDtypeStruct(z_rows.shape, BF),
            jax.ShapeDtypeStruct(dx_rows.shape, F32),
            jax.ShapeDtypeStruct((6, part, width), F32),
            jax.ShapeDtypeStruct((class_count, width), F32),
            jax.ShapeDtypeStruct((1, part), F32),
            jax.ShapeDtypeStruct((1, part), F32),
            jax.ShapeDtypeStruct((1, 3), F32),
        ),
        in_specs=[anywhere] * 3 + [vmem] * 4,
        out_specs=[anywhere] * 8 + [vmem] * 3,
        scratch_shapes=[pltpu.VMEM(flat.shape, BF)]
        + [pltpu.VMEM(shape, F32) for shape in shapes]
        + [
            pltpu.VMEM((6, 3 * LANES, width), F32),
            pltpu.VMEM((-(-class_count // LANES) * LANES, width), F32),
            pltpu.VMEM(z_rows.shape, BF),
            pltpu.VMEM(dx_rows.shape, F32),
            pltpu.SemaphoreType.DMA((5, 3)),
            pltpu.SemaphoreType.DMA((14,)),
        ],
        compiler_params=pltpu.CompilerParams(vmem_limit_bytes=60 * 2**20),
    )(flat, z_rows, dx_rows, dmod_all, sum_all, extra_all, select)


def time_embed(bin_row, feature_count):
    halfway = feature_count // 2
    frequency = jnp.exp(-math.log(10000.0) * jnp.arange(halfway, dtype=F32) / halfway)
    moment = (bin_row.astype(F32) + 0.5) * (1000.0 / NBINS)
    angles = moment[:, None] * frequency[None, :]
    return jnp.concatenate([jnp.cos(angles), jnp.sin(angles)], axis=-1)


def per_device(
    tokens,
    velocity_grad,
    bins,
    labels,
    places,
    class_table,
    mod_weight,
    qkv_weight,
    out_weight,
    gate_up_weight,
    down_weight,
    q_gain,
    k_gain,
):
    micro, per_micro, rows, width = tokens.shape
    images = micro * per_micro
    dp = lax.axis_size("dp")
    me = lax.axis_index("tensor")
    heads = q_gain.shape[1] // HEAD_DIM
    select = jnp.asarray(head_select(heads), BF)

    label_row = labels.reshape(images)
    one_hot = label_row[:, None] == jnp.arange(class_table.shape[0], dtype=jnp.int32)[None, :]
    picked = jnp.dot(one_hot.astype(BF), class_table, preferred_element_type=F32)
    cond = time_embed(bins.reshape(images), width) + picked
    silu_low = jax.nn.silu(cond).astype(BF)
    mod_w = mod_weight[0]
    part = width // 4
    columns = jnp.einsum("id,djf->ijf", silu_low, mod_w, preferred_element_type=F32)
    shift = me * (part - 2 * LANES)
    mod_cols = lax.dynamic_update_slice(jnp.zeros((images, 8, 3 * LANES), F32), columns, (0, 0, shift))

    table, table_parts = angle_table(), []
    for _ in range(3):
        table_parts.append(table.astype(BF))
        table = table - table_parts[-1].astype(np.float32)
    table_parts.append(np.zeros((LANES - 6 * GRID, 2 * LANES), BF))

    results = run_main(
        tokens.reshape(images, rows, width),
        velocity_grad.reshape(images, rows, width),
        mod_cols,
        places,
        jnp.asarray(np.concatenate(table_parts)),
        jnp.transpose(qkv_weight[0], (0, 2, 1)),
        out_weight[0],
        gate_up_weight[0],
        down_weight[0],
        q_gain,
        k_gain,
        select,
    )
    z_rows, dx_rows, dmod_part, gain_sums, squares, a1, a2, d_ffn, d_attn, units, mixed, d_gu, d_qkv = results

    lanes_all = heads * LANES
    flat = images * 4 * rows
    flat_grads, dmod_all, sum_all, extra_all = run_tail(
        dp,
        a2.reshape(flat, width),
        d_gu.reshape(flat, d_gu.shape[2]),
        units.reshape(flat, units.shape[2]),
        d_ffn.reshape(flat, width),
        a1.reshape(flat, width),
        d_qkv.reshape(flat, d_qkv.shape[2]),
        mixed.reshape(flat, lanes_all),
        d_attn.reshape(flat, width),
        jnp.transpose(mod_w, (1, 2, 0)),
        select,
        cond,
        squares,
        silu_low,
        dmod_part.reshape(8 * images, 3 * LANES),
        gain_sums,
        label_row,
    )
    count = images * rows * width * dp * lax.axis_size("tensor")
    finished = run_finish(
        count,
        class_table.shape[0],
        units.shape[2],
        flat_grads,
        z_rows,
        dx_rows,
        dmod_all,
        sum_all,
        extra_all,
        select,
    )
    gate_up_grad, down_grad, qkv_grad, out_grad, z_out, dx_out, mod_grad, class_grad, q_grad, k_grad, stats = finished
    whole = (1, micro, per_micro, rows, width)
    return (
        z_out.reshape(whole),
        dx_out.reshape(whole),
        jnp.transpose(mod_grad, (2, 0, 1))[None],
        jnp.transpose(qkv_grad.reshape(3, part, width), (0, 2, 1))[None],
        out_grad[None],
        gate_up_grad[None],
        down_grad[None],
        q_grad,
        k_grad,
        class_grad,
        stats,
    )


def solution(mesh):
    return jax.shard_map(
        per_device,
        mesh=mesh,
        in_specs=(
            P(None, "dp", "tensor", None),
            P(None, "dp", "tensor", None),
            P(None, "dp"),
            P(None, "dp"),
            P(None, "dp", None),
            P(),
            P("section", None, None, "tensor"),
            P("section", None, None, "tensor"),
            P("section", "tensor", None),
            P("section", None, None, "tensor"),
            P("section", "tensor", None),
            P("section", "tensor"),
            P("section", "tensor"),
        ),
        out_specs=(
            P("section", None, "dp", "tensor", None),
            P("section", None, "dp", "tensor", None),
            P("section", None, None, "tensor"),
            P("section", None, None, "tensor"),
            P("section", "tensor", None),
            P("section", None, None, "tensor"),
            P("section", "tensor", None),
            P("section", "tensor"),
            P("section", "tensor"),
            P(),
            P("section", None),
        ),
        check_vma=False,
    )
```

```python
import functools
import math

import jax
import jax.numpy as jnp
import numpy as np
from jax import lax
from jax.experimental import pallas as pl
from jax.experimental.pallas import tpu as pltpu
from jax.sharding import PartitionSpec as P

MESH = pl.DeviceIdType.MESH
HEAD_DIM = 72
LANES = 128
NBINS = 1000
GRID = 16
EPS = 1e-06
BF = jnp.bfloat16
F32 = jnp.float32
SCALE = HEAD_DIM**-0.5
LOG2E = math.log2(math.e)

KEEP, SLOTS, PACK = 2, 4, 4
LENT = 4
ORDERS = (
    (
        0, 1, 8, 2, 3, 16, 9, 24, 10, 4, 17, 32, 11, 25, 18, 40, 26, 48, 33,
        56, 19, 34, 12, 41, 64, 49, 27, 57, 42, 144, 50, 35, 65, 58, 20, 43, 5, 145,
        66, 28, 51, 13, 146, 59, 36, 6, 21, 67, 44, 52, 60, 147, 14, 7, 29, 68, 22,
        15, 37, 148, 30, 23, 38, 31, 45, 53, 61, 39, 46, 54, 69, 62, 149, 70, 47, 72,
        55, 80, 63, 150, 88, 71, 151, 96, 104, 73, 81, 89, 112, 74, 97, 120, 82, 128, 105,
        90, 136, 98, 113, 75, 121, 83, 106, 91, 114, 129, 99, 122, 76, 130, 137, 107, 84, 92,
        77, 115, 100, 138, 123, 78, 85, 108, 93, 86, 79, 131, 94, 116, 101, 102, 124, 87, 109,
        132, 95, 139, 117, 103, 110, 125, 111, 140, 133, 118, 126, 119, 141, 134, 127, 135, 142, 143,
    ),
    (
        72, 73, 74, 80, 75, 81, 82, 76, 83, 77, 0, 8, 78, 16, 1, 24, 84, 9, 32,
        79, 17, 40, 85, 2, 25, 88, 10, 33, 48, 56, 18, 96, 41, 3, 86, 26, 89, 11,
        104, 97, 19, 4, 64, 112, 34, 27, 49, 120, 42, 105, 57, 90, 12, 113, 35, 98, 20,
        65, 128, 43, 121, 28, 50, 106, 136, 91, 5, 36, 13, 129, 114, 58, 99, 21, 122, 44,
        51, 66, 29, 59, 130, 6, 92, 14, 37, 107, 22, 7, 137, 67, 138, 30, 15, 87, 52,
        60, 45, 100, 115, 23, 38, 123, 31, 108, 93, 53, 131, 46, 68, 61, 39, 94, 116, 139,
        101, 102, 124, 47, 69, 109, 132, 95, 117, 144, 110, 103, 125, 140, 54, 133, 145, 118, 146,
        55, 111, 62, 126, 141, 119, 134, 63, 127, 147, 135, 142, 148, 70, 149, 71, 150, 143, 151,
    ),
)


def lane_of():
    quarter = HEAD_DIM // 4
    lanes = np.zeros((HEAD_DIM,), np.int64)
    for half in range(2):
        for part in range(2):
            for i in range(quarter):
                lanes[half * 2 * quarter + part * quarter + i] = part * 64 + half * quarter + i
    return lanes


def head_select(heads):
    select = np.zeros((heads * HEAD_DIM, heads * LANES), np.float32)
    lanes = lane_of()
    for h in range(heads):
        for f in range(HEAD_DIM):
            select[h * HEAD_DIM + f, h * LANES + lanes[f]] = 1.0
    return select


def angle_table():
    quarter = HEAD_DIM // 4
    frequency = (10000.0 ** (-np.arange(quarter, dtype=np.float32) / np.float32(quarter))).astype(np.float32)
    lanes = lane_of().reshape(2, 2, quarter)
    table = np.zeros((2 * GRID, 2 * LANES), np.float32)
    for place in range(GRID):
        angle = np.float32(place) * frequency
        for half in range(2):
            for part in range(2):
                sign = -1.0 if part == 0 else 1.0
                table[half * GRID + place, lanes[half, part]] = np.cos(angle)
                table[half * GRID + place, LANES + lanes[half, part]] = sign * np.sin(angle)
    return table


def dot(a, b):
    return lax.dot_general(a, b, (((1,), (0,)), ((), ())), preferred_element_type=F32)


def dot_nt(a, b):
    return lax.dot_general(a, b, (((1,), (1,)), ((), ())), preferred_element_type=F32)


def dot_tn(a, b):
    return lax.dot_general(a, b, (((0,), (0,)), ((), ())), preferred_element_type=F32)


def order_words(order, base):
    words = []
    for at in range(0, len(order), PACK):
        words.append(sum(entry * base**i for i, entry in enumerate(order[at : at + PACK])))
    while len(words) & (len(words) - 1):
        words.append(0)
    return words


def chunks_of(size, width):
    return [(at, min(width, size - at)) for at in range(0, size, width)]


def main_kernel(
    images,
    heads,
    tok,
    vel,
    mod_cols,
    places,
    angles,
    qkv_hbm,
    out_hbm,
    wgu_hbm,
    wdn_hbm,
    q_gain,
    k_gain,
    select,
    zout,
    dxout,
    dmod_part,
    gacc,
    sacc,
    a1_hbm,
    a2_hbm,
    dffn_hbm,
    dattn_hbm,
    hid_hbm,
    mix_hbm,
    dgu_hbm,
    dqkv_hbm,
    turns,
    wqkv,
    wout,
    wgu,
    wdn,
    gains,
    xin,
    din,
    a1f,
    a2f,
    dffn,
    dattn,
    x1s,
    attns,
    ffns,
    keep,
    send_a,
    recv_a,
    send_y,
    recv_y,
    mix_st,
    hid_st,
    dgu_st,
    dqkv_st,
    mod,
    mod_recv,
    dmod,
    mod_sems,
    dmod_sems,
    ag_sems,
    rs_sems,
    zx_sems,
    out_sems,
    in_sems,
):
    rows = tok.shape[1]
    width = tok.shape[2]
    hidden = wdn.shape[0]
    wide = chunks_of(width, 512)
    section = lax.axis_index("section")
    me = lax.axis_index("tensor")
    sib = me + 1 - 2 * lax.rem(me, 2)
    across = lax.rem(me + 2, 4)
    diag = lax.rem(sib + 2, 4)
    peers = (sib, across, diag)
    other = 1 - section
    enc = section == 0
    dec = section == 1

    load_x = pltpu.make_async_copy(tok, xin, in_sems.at[0])
    load_d = pltpu.make_async_copy(vel, din, in_sems.at[1])
    tokens, part = dattn.shape[1], out_hbm.shape[0]
    groups = [qkv_hbm.at[j] for j in range(3)] + [out_hbm]
    load_w = [
        pltpu.make_async_copy(wgu_hbm, wgu, in_sems.at[2]),
        pltpu.make_async_copy(wdn_hbm, wdn, in_sems.at[3]),
    ]
    load_raw = []
    for j, group in enumerate(groups):
        for i, (at, size) in enumerate(((0, tokens), (tokens, part - tokens))):
            src, dst = group.at[pl.ds(at, size)], dattn.at[2 * j + i, pl.ds(0, size)]
            load_raw.append(pltpu.make_async_copy(src, dst, in_sems.at[4 + 2 * j + i]))
    for copy in load_raw:
        copy.start()

    @pl.when(enc)
    def _():
        load_x.start()

    @pl.when(dec)
    def _():
        load_d.start()

    barrier = pltpu.get_barrier_semaphore()
    pl.semaphore_signal(barrier, inc=1, device_id={"tensor": sib}, device_id_type=MESH)
    pl.semaphore_signal(barrier, inc=1, device_id={"tensor": across}, device_id_type=MESH)
    pl.semaphore_signal(barrier, inc=1, device_id={"tensor": diag}, device_id_type=MESH)
    pl.semaphore_signal(barrier, inc=1, device_id={"section": other}, device_id_type=MESH)

    mod[...] = jnp.zeros_like(mod)
    gacc[...] = jnp.zeros_like(gacc)
    sacc[...] = jnp.zeros_like(sacc)
    dmod[...] = jnp.zeros_like(dmod)

    pl.semaphore_wait(barrier, 4)

    def remote(src, dst, send_sem, recv_sem, where):
        return pltpu.make_async_remote_copy(
            src_ref=src, dst_ref=dst, send_sem=send_sem, recv_sem=recv_sem, device_id=where, device_id_type=MESH
        )

    def gather(which, buf, n, kind):
        src, dst, where = ((0, rows, across), (0, 2 * rows, sib), (rows, 3 * rows, sib))[kind]
        return remote(
            buf.at[n, pl.ds(src, rows)],
            buf.at[n, pl.ds(dst, rows)],
            ag_sems.at[which, 2 * kind, n],
            ag_sems.at[which, 2 * kind + 1, n],
            {"tensor": where},
        )

    def its_tiles(device):
        return pl.ds(pl.multiple_of(device * (2 * LANES), LANES), 3 * LANES)

    def mod_copy(k):
        return remote(mod_cols, mod_recv.at[k], mod_sems.at[0, k], mod_sems.at[1, k], {"tensor": peers[k]})

    def dmod_copy(k, n):
        return remote(
            dmod.at[n, :, its_tiles(peers[k])],
            mod_recv.at[k, n],
            dmod_sems.at[0, k, n],
            dmod_sems.at[1, k, n],
            {"tensor": peers[k]},
        )

    for k in (1, 2, 0):
        mod_copy(k).start()

    @pl.when(enc)
    def _():
        load_x.wait()
        a1f[0, 0:rows, :] = xin[0]
        gather(0, a1f, 0, 0).start()
        gather(0, a1f, 0, 1).start()

    @pl.when(dec)
    def _():
        load_d.wait()

    for copy in load_w:
        copy.start()
    mod[:, :, its_tiles(me)] = mod_cols[...]

    gains[0:1, :] = dot(q_gain[...], select[...])
    gains[1:2, :] = dot(k_gain[...], select[...])
    for j in range(4):
        load_raw[2 * j].wait()
        load_raw[2 * j + 1].wait()
        ref = wqkv.at[j] if j < 3 else wout
        for at, size in wide:
            span = pl.ds(at, size)
            value = dot_tn(select[0:tokens, :], dattn[2 * j, :, span])
            value += dot_tn(select[tokens:part, :], dattn[2 * j + 1, 0 : part - tokens, span])
            ref[:, span] = value.astype(BF)

    spots = jnp.concatenate([places[i] for i in range(places.shape[0])], axis=0).astype(F32).T
    lane = lax.broadcasted_iota(jnp.int32, (rows, LANES), 1)
    spot = lax.rem(lane, 2 * GRID)
    by_row, used = spot < GRID, lane < 6 * GRID
    spot = jnp.where(by_row, spot, spot - GRID).astype(F32)
    for block in range(4):
        high, low, my_high, my_low = block // 2, block % 2, lax.div(me, 2), lax.rem(me, 2)
        at = high + my_high - 2 * high * my_high + 2 * (low + my_low - 2 * low * my_low)
        here = pl.ds(pl.multiple_of(at * rows, rows), rows)
        mine = slice(block * rows, (block + 1) * rows)
        for n in range(images):
            row = jnp.floor(spots[mine, n : n + 1] * (1.0 / GRID))
            marks = jnp.where(by_row, row, spots[mine, n : n + 1] - GRID * row) == spot
            turns[n, here, :] = dot(jnp.where(marks & used, 1.0, 0.0).astype(BF), angles[...])

    for k in range(3):
        mod_copy(k).wait()
        mod[:, :, its_tiles(peers[k])] += mod_recv[k]

    def gather_start(which, buf, n):
        gather(which, buf, n, 0).start()
        gather(which, buf, n, 1).start()

    def gather_relay(which, buf, n):
        gather(which, buf, n, 0).wait_recv()
        gather(which, buf, n, 2).start()

    def attn_relay(n):
        @pl.when(enc)
        def _():
            gather(0, a1f, n, 0).wait_recv()

        @pl.when(dec)
        def _():
            zy_pass(n).wait_recv()
            values = a1f[n, rows : 2 * rows, :].astype(F32)
            a1f[n, rows : 2 * rows, :] = modulated(values, mod_row(n, 0), mod_row(n, 1)).astype(BF)

        gather(0, a1f, n, 2).start()

    def gather_wait(which, buf, n):
        gather(which, buf, n, 1).wait_recv()
        gather(which, buf, n, 2).wait_recv()

    def gather_drain(which, buf, n):
        for kind in range(3):
            gather(which, buf, n, kind).wait_send()

    def to_sibling(which, n):
        return remote(
            send_a.at[which, lax.rem(n, KEEP)],
            recv_a.at[which, lax.rem(n, SLOTS)],
            rs_sems.at[which, 0, n],
            rs_sems.at[which, 1, n],
            {"tensor": sib},
        )

    def over_y(which, n):
        return remote(
            send_y.at[which, lax.rem(n, KEEP)],
            recv_y.at[which, lax.rem(n, SLOTS)],
            rs_sems.at[which, 2, n],
            rs_sems.at[which, 3, n],
            {"tensor": across},
        )

    def scatter_put(which, n, at, size, values):
        kind, own = which, lax.rem(n, KEEP)
        keep[kind, own, :, pl.ds(at, size)] = values[0 : 2 * rows]
        send_a[kind, own, :, pl.ds(at, size)] = values[2 * rows : 4 * rows].astype(BF)

    def scatter_start(which, n):
        to_sibling(which, n).start()

    def scatter_middle(which, n):
        kind, own, slot = which, lax.rem(n, KEEP), lax.rem(n, SLOTS)
        to_sibling(which, n).wait()
        theirs = recv_a[kind, slot, rows : 2 * rows].astype(F32)
        send_y[kind, own] = (keep[kind, own, rows : 2 * rows] + theirs).astype(BF)
        over_y(which, n).start()

    def scatter_end(which, n):
        kind, own, slot = which, lax.rem(n, KEEP), lax.rem(n, SLOTS)
        over_y(which, n).wait()
        mine = keep[kind, own, 0:rows] + recv_a[kind, slot, 0:rows].astype(F32)
        return mine + recv_y[kind, slot].astype(F32)

    def z_copy(n):
        return remote(zout.at[n], xin.at[n], zx_sems.at[0, n], zx_sems.at[1, n], {"section": other})

    def zy_copy(n):
        return remote(
            zout.at[n], dattn.at[n, pl.ds(rows, rows)], zx_sems.at[4, n], zx_sems.at[5, n], {"tensor": across}
        )

    def zy_pass(n):
        return remote(
            dattn.at[n, pl.ds(rows, rows)],
            a1f.at[n, pl.ds(rows, rows)],
            zx_sems.at[6, n],
            zx_sems.at[7, n],
            {"section": other},
        )

    def dz_copy(n):
        return remote(xin.at[n], din.at[n], zx_sems.at[2, n], zx_sems.at[3, n], {"section": other})

    def mod_row(n, row):
        return mod[n, pl.ds(row, 1), :]

    def inverse_rms(values):
        return lax.rsqrt(jnp.mean(values * values, axis=-1, keepdims=True) + EPS)

    def column_sum(values):
        return jnp.sum(values, axis=0, keepdims=True)

    def modulated(values, shift, scale):
        return (values * inverse_rms(values)) * (1.0 + scale) + shift

    def norm_back(values, grad, scale):
        inv = inverse_rms(values)
        normed = values * inv
        d_normed = grad * (1.0 + scale)
        d_values = inv * (d_normed - normed * jnp.mean(d_normed * normed, axis=-1, keepdims=True))
        return d_values, column_sum(grad), column_sum(grad * normed)

    def head_norm(raw):
        inv = lax.rsqrt(jnp.sum(raw * raw, axis=-1, keepdims=True) * (1.0 / HEAD_DIM) + EPS)
        return inv, raw * inv

    def turn(values, c, s):
        return values * c + pltpu.roll(values, 64, 1) * s

    def turn_back(values, c, s):
        return values * c - pltpu.roll(values, 64, 1) * s

    def softmax_parts(scaled, k):
        powered = jnp.exp2(dot_nt(scaled, k))
        return powered, 1.0 / jnp.sum(powered, axis=-1, keepdims=True)

    def out_copy(which, n):
        src = (a1f, a2f, dffn, dattn, hid_st, mix_st, dgu_st, dqkv_st)[which]
        dst = (a1_hbm, a2_hbm, dffn_hbm, dattn_hbm, hid_hbm, mix_hbm, dgu_hbm, dqkv_hbm)[which]
        return pltpu.make_async_copy(src.at[n] if which < 4 else src, dst.at[n], out_sems.at[which, n])

    def staged_ready(which, n):
        @pl.when(n > 0)
        def _():
            out_copy(which, n - 1).wait()

    def attn_in(n):
        @pl.when(dec)
        def _():
            z_copy(n).wait_recv()

        values = xin[n].astype(F32)
        sacc[0:1, :] += column_sum(values * values)

        @pl.when(dec | (n > 0))
        def _():
            a1f[n, 0:rows, :] = modulated(values, mod_row(n, 0), mod_row(n, 1)).astype(BF)

            @pl.when(enc)
            def _():
                gather(0, a1f, n, 0).start()

            gather(0, a1f, n, 1).start()

    def attn_drain(n):
        gather(0, a1f, n, 1).wait_send()
        gather(0, a1f, n, 2).wait_send()

        @pl.when(enc)
        def _():
            gather(0, a1f, n, 0).wait_send()

    def attn_compute(n):
        gather_wait(0, a1f, n)

        @pl.when(enc & (n == 0))
        def _():
            attn_drain(n)
            for at in range(0, 4 * rows, rows):
                values = a1f[0, at : at + rows, :].astype(F32)
                a1f[0, at : at + rows, :] = modulated(values, mod_row(0, 0), mod_row(0, 1)).astype(BF)

        staged_ready(5, n)
        a1 = a1f[n]
        c, s = turns[n, :, 0:LANES], turns[n, :, LANES : 2 * LANES]
        for pair in range(heads // 2):
            span = pl.ds(pair * 2 * LANES, 2 * LANES)
            q2 = dot_nt(a1, wqkv[0, span, :])
            k2 = dot_nt(a1, wqkv[1, span, :])
            v2 = dot_nt(a1, wqkv[2, span, :]).astype(BF)
            for half in range(2):
                at = (pair * 2 + half) * LANES
                cut = slice(half * LANES, (half + 1) * LANES)
                q_gain = gains[0:1, at : at + LANES] * (SCALE * LOG2E)
                q = turn(head_norm(q2[:, cut])[1] * q_gain, c, s).astype(BF)
                k = turn(head_norm(k2[:, cut])[1] * gains[1:2, at : at + LANES], c, s).astype(BF)
                powered, inverse = softmax_parts(q, k)
                mix_st[:, at : at + LANES] = (dot(powered.astype(BF), v2[:, cut]) * inverse).astype(BF)
        mixed = mix_st[...]
        for at, size in wide:
            scatter_put(0, n, at, size, dot(mixed, wout[:, pl.ds(at, size)]))
        scatter_start(0, n)
        out_copy(5, n).start()
        out_copy(0, n).start()

        @pl.when(dec | (n > 0))
        def _():
            attn_drain(n)

    def ffn_in(n):
        attended = scatter_end(0, n)
        attns[n] = attended.astype(BF)
        values = xin[n].astype(F32) + mod_row(n, 2) * attended
        x1s[n] = values
        sacc[1:2, :] += column_sum(values * values)
        a2f[n, 0:rows, :] = modulated(values, mod_row(n, 3), mod_row(n, 4)).astype(BF)
        gather_start(1, a2f, n)

    def ffn_down(n, units):
        for at, size in wide:
            scatter_put(1, n, at, size, dot(units, wdn[:, pl.ds(at, size)]))
        scatter_start(1, n)
        out_copy(1, n).start()
        gather_drain(1, a2f, n)

    def first_ffn(n):
        gather_wait(1, a2f, n)

        @pl.when(n == 0)
        def _():
            load_w[0].wait()
            load_w[1].wait()

    def ffn_compute(n):
        @pl.when(enc)
        def _():
            first_ffn(n)
            a2 = a2f[n]
            for at, size in chunks_of(hidden, 256):
                span = pl.ds(at, size)
                gate_val = dot(a2, wgu[0, :, span])
                up_val = dot(a2, wgu[1, :, span])
                hid_st[:, span] = (gate_val * jax.nn.sigmoid(gate_val) * up_val).astype(BF)
            ffn_down(n, hid_st[...])

    def block_out(n):
        feedfwd = scatter_end(1, n)
        ffns[n] = feedfwd.astype(BF)
        values = x1s[n] + mod_row(n, 5) * feedfwd
        sacc[2:3, :] += column_sum(values * values)
        zout[n] = values.astype(BF)

        @pl.when(enc)
        def _():
            z_copy(n).start()
            zy_copy(n).start()

        @pl.when(dec)
        def _():
            dmod[n, 5:6, :] = column_sum(din[n].astype(F32) * feedfwd)

    def pass_on(n):
        @pl.when(enc)
        def _():
            zy_copy(n).wait_recv()
            zy_pass(n).start()

        @pl.when(dec)
        def _():
            send_dmod(n)

    def send_dmod(n):
        for k in range(3):
            dmod_copy(k, n).start()

    def ffn_grad_in(n):
        @pl.when(enc)
        def _():
            zy_copy(n).wait_send()
            zy_pass(n).wait_send()
            dz_copy(n).wait_recv()

        grad = din[n].astype(F32)
        dffn[n, 0:rows, :] = (mod_row(n, 5) * grad).astype(BF)
        gather_start(2, dffn, n)

        @pl.when(enc)
        def _():
            dmod[n, 5:6, :] = column_sum(grad * ffns[n].astype(F32))

    def ffn_grad_compute(n):
        @pl.when(dec)
        def _():
            first_ffn(n)

        gather_wait(2, dffn, n)
        staged_ready(4, n)
        staged_ready(6, n)
        grad = dffn[n]
        a2 = a2f[n]
        for at, size in chunks_of(hidden, 256):
            span = pl.ds(at, size)
            gate_val = dot(a2, wgu[0, :, span])
            up_val = dot(a2, wgu[1, :, span])
            d_hidden = dot_nt(grad, wdn[span, :])
            sig = jax.nn.sigmoid(gate_val)
            act = gate_val * sig
            hid_st[:, span] = (act * up_val).astype(BF)
            dgu_st[:, span] = (d_hidden * up_val * (sig + act * (1.0 - sig))).astype(BF)
            dgu_st[:, pl.ds(hidden + at, size)] = (d_hidden * act).astype(BF)
        d_gate = dgu_st[:, 0:hidden]
        d_up = dgu_st[:, hidden : 2 * hidden]
        for at, size in wide:
            span = pl.ds(at, size)
            scatter_put(2, n, at, size, dot_nt(d_gate, wgu[0, span, :]) + dot_nt(d_up, wgu[1, span, :]))
        scatter_start(2, n)

        @pl.when(dec)
        def _():
            ffn_down(n, hid_st[...])

        out_copy(4, n).start()
        out_copy(6, n).start()
        out_copy(2, n).start()
        gather_drain(2, dffn, n)

    def attn_grad_in(n):
        d_a2 = scatter_end(2, n)
        grad, d_shift, d_scale = norm_back(x1s[n], d_a2, mod_row(n, 4))
        grad = grad + din[n].astype(F32)
        dxout[n] = grad
        dattn[n, 0:rows, :] = (mod_row(n, 2) * grad).astype(BF)
        gather_start(3, dattn, n)
        dmod[n, 2:3, :] = column_sum(grad * attns[n].astype(F32))
        dmod[n, 3:4, :] = d_shift
        dmod[n, 4:5, :] = d_scale

    def attn_grad_compute(n):
        gather_wait(3, dattn, n)
        staged_ready(7, n)
        grad = dattn[n]
        a1 = a1f[n]
        c, s = turns[n, :, 0:LANES], turns[n, :, LANES : 2 * LANES]
        lanes_all = heads * LANES
        for pair in range(heads // 2):
            span = pl.ds(pair * 2 * LANES, 2 * LANES)
            q2 = dot_nt(a1, wqkv[0, span, :])
            k2 = dot_nt(a1, wqkv[1, span, :])
            v2 = dot_nt(a1, wqkv[2, span, :]).astype(BF)
            d_mix2 = dot_nt(grad, wout[span, :])
            for half in range(2):
                at = (pair * 2 + half) * LANES
                cut = slice(half * LANES, (half + 1) * LANES)
                q_gain, k_gain = gains[0:1, at : at + LANES], gains[1:2, at : at + LANES]
                q_inv, q_norm = head_norm(q2[:, cut])
                k_inv, k_norm = head_norm(k2[:, cut])
                q = turn(q_norm * (q_gain * (SCALE * LOG2E)), c, s).astype(BF)
                k = turn(k_norm * k_gain, c, s).astype(BF)
                v = v2[:, cut]
                powered, inverse = softmax_parts(q, k)
                low = powered.astype(BF)
                mixed = dot(low, v) * inverse
                d_mix = d_mix2[:, cut] * inverse
                d_mix = d_mix.astype(BF)
                taken = jnp.sum(d_mix.astype(F32) * mixed, axis=-1, keepdims=True)
                d_v = dot_tn(low, d_mix)
                d_scores = (powered * (dot_nt(d_mix, v) - taken)).astype(BF)
                d_q = turn_back(dot(d_scores, k) * SCALE, c, s)
                d_k = turn_back(dot_tn(d_scores, q) * (1.0 / LOG2E), c, s)
                gacc[0:1, at : at + LANES] += column_sum(d_q * q_norm)
                gacc[1:2, at : at + LANES] += column_sum(d_k * k_norm)
                d_q = d_q * q_gain
                d_k = d_k * k_gain
                d_q = q_inv * (d_q - q_norm * (jnp.sum(d_q * q_norm, axis=-1, keepdims=True) * (1.0 / HEAD_DIM)))
                d_k = k_inv * (d_k - k_norm * (jnp.sum(d_k * k_norm, axis=-1, keepdims=True) * (1.0 / HEAD_DIM)))
                dqkv_st[:, at : at + LANES] = d_q.astype(BF)
                dqkv_st[:, lanes_all + at : lanes_all + at + LANES] = d_k.astype(BF)
                dqkv_st[:, 2 * lanes_all + at : 2 * lanes_all + at + LANES] = d_v.astype(BF)
        for at, size in wide:
            span = pl.ds(at, size)
            total = dot(dqkv_st[:, 0:lanes_all], wqkv[0, :, span])
            total += dot(dqkv_st[:, lanes_all : 2 * lanes_all], wqkv[1, :, span])
            total += dot(dqkv_st[:, 2 * lanes_all : 3 * lanes_all], wqkv[2, :, span])
            scatter_put(3, n, at, size, total)
        scatter_start(3, n)
        out_copy(7, n).start()
        out_copy(3, n).start()
        gather_drain(3, dattn, n)

    def block_grad_out(n):
        d_a1 = scatter_end(3, n)
        grad, d_shift, d_scale = norm_back(xin[n].astype(F32), d_a1, mod_row(n, 1))
        grad = grad + dxout[n]
        dxout[n] = grad
        dmod[n, 0:1, :] = d_shift
        dmod[n, 1:2, :] = d_scale

        @pl.when(dec)
        def _():
            xin[n] = grad.astype(BF)
            dz_copy(n).start()

        @pl.when(enc)
        def _():
            send_dmod(n)

    works = (
        attn_in,
        attn_relay,
        attn_compute,
        lambda n: scatter_middle(0, n),
        ffn_in,
        lambda n: gather_relay(1, a2f, n),
        ffn_compute,
        lambda n: scatter_middle(1, n),
        block_out,
        ffn_grad_in,
        lambda n: gather_relay(2, dffn, n),
        ffn_grad_compute,
        lambda n: scatter_middle(2, n),
        attn_grad_in,
        lambda n: gather_relay(3, dattn, n),
        attn_grad_compute,
        lambda n: scatter_middle(3, n),
        block_grad_out,
        pass_on,
    )

    def run_work(work, n, low, high):
        if high - low == 1:
            works[low](n)
            return
        middle = (low + high) // 2

        @pl.when(work < middle)
        def _():
            run_work(work, n, low, middle)

        @pl.when(work >= middle)
        def _():
            run_work(work, n, middle, high)

    base = len(works) * images
    tables = [order_words(order, base) for order in ORDERS]

    def entry_of(i):
        rest, values = i, [low + section * (high - low) for low, high in zip(*tables)]
        while len(values) > 1:
            bit, rest = lax.rem(rest, 2), lax.div(rest, 2)
            values = [low + bit * (high - low) for low, high in zip(values[0::2], values[1::2])]
        return values[0]

    def word_step(i, carry):
        def work_step(_, word):
            entry, word = lax.rem(word, base), lax.div(word, base)
            work, n = lax.div(entry, images), lax.rem(entry, images)
            run_work(work, n, 0, len(works))
            return word

        lax.fori_loop(0, PACK, work_step, entry_of(i))
        return carry

    lax.fori_loop(0, base // PACK, word_step, 0)

    for which in (4, 5, 6, 7):
        out_copy(which, images - 1).wait()

    def drain(n, carry):
        for which in (0, 1, 2, 3):
            out_copy(which, n).wait()
        part = dmod[n, :, its_tiles(me)]
        for k in range(3):
            dmod_copy(k, n).wait()
            part += mod_recv[k, n]
        for j in range(8):
            mod[j, pl.ds(n, 1), 0 : 3 * LANES] = part[j : j + 1]

        @pl.when(enc)
        def _():
            z_copy(n).wait_send()

        @pl.when(dec)
        def _():
            dz_copy(n).wait_send()

        return carry

    lax.fori_loop(0, images, drain, 0)
    dmod_part[...] = mod[:, :, 0 : 3 * LANES].astype(BF)


def run_main(tok, vel, mod_cols, places, angles, qkv, out, wgu, wdn, q_gain, k_gain, select):
    images, rows, width = tok.shape
    tokens = 4 * rows
    lanes_all = select.shape[1]
    heads = lanes_all // LANES
    hidden = wdn.shape[0]
    vmem = pl.BlockSpec(memory_space=pltpu.VMEM)
    anywhere = pl.BlockSpec(memory_space=pl.ANY)

    def hbm(last):
        return jax.ShapeDtypeStruct((images, tokens, last), BF)

    out_shape = (
        jax.ShapeDtypeStruct((images, rows, width), BF),
        jax.ShapeDtypeStruct((images, rows, width), F32),
        jax.ShapeDtypeStruct((8, images, 3 * LANES), BF),
        jax.ShapeDtypeStruct((8, lanes_all), F32),
        jax.ShapeDtypeStruct((8, width), F32),
        hbm(width),
        hbm(width),
        hbm(width),
        hbm(width),
        hbm(hidden),
        hbm(lanes_all),
        hbm(2 * hidden),
        hbm(3 * lanes_all),
    )
    scratch = [
        pltpu.VMEM((images, tokens, 2 * LANES), F32),
        pltpu.VMEM((3, lanes_all, width), BF),
        pltpu.VMEM((lanes_all, width), BF),
        pltpu.VMEM(wgu.shape, BF),
        pltpu.VMEM(wdn.shape, BF),
        pltpu.VMEM((8, lanes_all), F32),
        pltpu.VMEM((images, rows, width), BF),
        pltpu.VMEM((images, rows, width), BF),
        pltpu.VMEM((images, tokens, width), BF),
        pltpu.VMEM((images, tokens, width), BF),
        pltpu.VMEM((images, tokens, width), BF),
        pltpu.VMEM((images, tokens, width), BF),
        pltpu.VMEM((images, rows, width), F32),
        pltpu.VMEM((images, rows, width), BF),
        pltpu.VMEM((images, rows, width), BF),
        pltpu.VMEM((4, KEEP, 2 * rows, width), F32),
        pltpu.VMEM((4, KEEP, 2 * rows, width), BF),
        pltpu.VMEM((4, SLOTS, 2 * rows, width), BF),
        pltpu.VMEM((4, KEEP, rows, width), BF),
        pltpu.VMEM((4, SLOTS, rows, width), BF),
        pltpu.VMEM((tokens, lanes_all), BF),
        pltpu.VMEM((tokens, hidden), BF),
        pltpu.VMEM((tokens, 2 * hidden), BF),
        pltpu.VMEM((tokens, 3 * lanes_all), BF),
        pltpu.VMEM((images, 8, width), F32),
        pltpu.VMEM((3, images, 8, 3 * LANES), F32),
        pltpu.VMEM((images, 8, width), F32),
        pltpu.SemaphoreType.DMA((2, 3)),
        pltpu.SemaphoreType.DMA((2, 3, images)),
        pltpu.SemaphoreType.DMA((4, 6, images)),
        pltpu.SemaphoreType.DMA((4, 4, images)),
        pltpu.SemaphoreType.DMA((8, images)),
        pltpu.SemaphoreType.DMA((8, images)),
        pltpu.SemaphoreType.DMA((12,)),
    ]
    return pl.pallas_call(
        functools.partial(main_kernel, images, heads),
        out_shape=out_shape,
        in_specs=[anywhere, anywhere] + [vmem] * 3 + [anywhere] * 4 + [vmem] * 3,
        out_specs=[vmem] * 5 + [anywhere] * 8,
        scratch_shapes=scratch,
        compiler_params=pltpu.CompilerParams(
            collective_id=0, has_side_effects=True, vmem_limit_bytes=63 * 2**20
        ),
    )(tok, vel, mod_cols, places, angles, qkv, out, wgu, wdn, q_gain, k_gain, select)


def flat_plan(width, hidden, part):
    blocks = width // LANES
    segments = ((2 * hidden // LANES, width), (blocks, hidden), (blocks, 3 * part), (blocks, part))
    halves = [count * rows // 2 for count, rows in segments]
    half, chunk = sum(halves), width // 2
    assert half % chunk == 0

    def pieces(segment, block):
        rows, cut, at = segments[segment][1], halves[segment], sum(halves[:segment])
        low, high = block * rows, (block + 1) * rows
        if high <= cut:
            return [(at + low, 0, rows)]
        if low >= cut:
            return [(half + at + low - cut, 0, rows)]
        return [(at + low, 0, cut - low), (half + at, cut - low, high - cut)]

    return half, chunk, pieces


def tail_kernel(
    dp,
    a2_hbm,
    dgu_hbm,
    hid_hbm,
    dffn_hbm,
    a1_hbm,
    dqkv_hbm,
    mix_hbm,
    dattn_hbm,
    mod_hbm,
    pick,
    cond,
    squares,
    silu,
    dmod_low,
    gain_sums,
    labels,
    totals,
    dmod_all,
    sum_all,
    extra_all,
    left_a,
    right_a,
    left_b,
    right_b,
    turned,
    own,
    arrived,
    mod_w,
    summand,
    sum_st,
    sum_recv,
    load_sems,
    part_sems,
    total_sems,
    sum_sems,
    all_sems,
    x_part_sems,
    x_total_sems,
    here,
):
    section = lax.axis_index("section")
    place = lax.axis_index("dp")
    me = lax.axis_index("tensor")
    sib = me + 1 - 2 * lax.rem(me, 2)
    across = lax.rem(me + 2, 4)
    enc, dec = section == 0, section == 1
    width, hidden = left_a.shape[1], left_b.shape[1]
    part, lanes_all = pick.shape
    half, chunk, pieces = flat_plan(width, hidden, part)
    whole = half // chunk
    count = jnp.where(enc, whole - LENT, whole + LENT)

    tokens, ahead = left_a.shape[0], 2 * LANES
    quarter = tokens // 4

    def some_rows(i):
        rows = pl.ds(i * quarter, quarter)
        return a2_hbm.at[rows], left_a.at[rows]

    def some_columns(at, size):
        cols = pl.ds(at, size)
        return dgu_hbm.at[:, cols], right_a.at[:, cols]

    loads = [
        pltpu.make_async_copy(src, dst, load_sems.at[i])
        for i, (src, dst) in enumerate(
            (
                some_rows(0),
                some_rows(1),
                some_rows(2),
                some_rows(3),
                some_columns(0, ahead),
                some_columns(hidden, ahead),
                some_columns(ahead, hidden - ahead),
                some_columns(hidden + ahead, hidden - ahead),
                (hid_hbm, left_b),
                (dffn_hbm, right_b),
                (mix_hbm, left_b.at[:, pl.ds(0, lanes_all)]),
                (a1_hbm, left_a),
                (dqkv_hbm, right_a),
                (dattn_hbm, right_b),
            )
        )
    ]
    for i in range(10):
        loads[i].start()

    mod_w[...] = jnp.zeros_like(mod_w)
    mine = pl.ds(pl.multiple_of(me * (part - 2 * LANES), 16), part)
    mod_loads = [pltpu.make_async_copy(mod_hbm.at[j], mod_w.at[j, mine], load_sems.at[14 + j]) for j in range(6)]
    for copy in mod_loads:
        copy.start()

    barrier = pltpu.get_barrier_semaphore()
    for where in ({"tensor": sib}, {"tensor": across}):
        pl.semaphore_signal(barrier, inc=1, device_id=where, device_id_type=MESH)

    @pl.when(dec)
    def _():
        pl.semaphore_signal(barrier, inc=1, device_id={"section": 0}, device_id_type=MESH)

    for k in range(1, dp):
        pl.semaphore_signal(barrier, inc=1, device_id={"dp": lax.rem(place + k, dp)}, device_id_type=MESH)

    def put(segment, block, first, value):
        for at, low, size in pieces(segment, block):
            begin, end = max(low, first), min(low + size, first + value.shape[0])
            if begin < end:
                own[at + begin - low : at + end - low, :] = value[begin - first : end - first].astype(BF)

    def put_wide(segment, block, first, value):
        for i in range(value.shape[1] // LANES):
            put(segment, block + i, first, value[:, i * LANES : (i + 1) * LANES])

    def turn_left(ref, first, last):
        cols = ref.shape[1]
        for at in range(first, last, 256):
            turned[0:cols, at : at + 256] = ref[at : at + 256, :].T

    def gate_up_blocks(*blocks):
        for block in blocks:
            value = dot(turned[...], right_a[:, block * LANES : (block + 2) * LANES])
            put_wide(0, block, 0, value)

    def qkv_heads(*pairs):
        kept = 2 * HEAD_DIM
        for pair in pairs:
            value = dot_tn(right_a[:, pair * 2 * LANES : (pair + 1) * 2 * LANES], left_a[...]).astype(BF)
            put_wide(2, 0, pair * kept, dot(pick[0:kept, 0 : 2 * LANES], value))

    def portion(i):
        tiles, gu_half = width // LANES, hidden // LANES
        pairs = 3 * lanes_all // (2 * LANES)
        if i == 0:
            for k in range(4):
                loads[k].wait()
                turn_left(left_a, k * quarter, (k + 1) * quarter)
            loads[11].start()
            loads[4].wait()
            gate_up_blocks(0)
            loads[5].wait()
            gate_up_blocks(gu_half)
        elif i == 1:
            loads[6].wait()
            gate_up_blocks(2)
        elif i == 2:
            loads[7].wait()
            gate_up_blocks(gu_half + 2)
        elif i == 3:
            gate_up_blocks(*range(4, gu_half, 2))
        elif i == 4:
            gate_up_blocks(*range(gu_half + 4, 2 * gu_half, 2))
            loads[12].start()
        elif i in (5, 6):
            if i == 5:
                loads[8].wait()
                turn_left(left_b, 0, tokens)
                loads[10].start()
                loads[9].wait()
            split = tiles // 4 * 2
            for block in range(0, split, 2) if i == 5 else range(split, tiles, 2):
                cut = slice(block * LANES, min(width, (block + 2) * LANES))
                put_wide(1, block, 0, dot(turned[0:hidden, :], right_b[:, cut]))
            if i == 6:
                loads[13].start()
        elif i in (7, 8, 9):
            if i == 7:
                loads[11].wait()
                loads[12].wait()
            third = -(-pairs // 3)
            qkv_heads(*range((i - 7) * third, min(pairs, (i - 6) * third)))
        elif i == 10:
            loads[10].wait()
            loads[13].wait()
            value = dot(pick[...], dot_tn(left_b[:, 0:lanes_all], right_b[...]).astype(BF))
            put_wide(3, 0, 0, value)

    def along(direction, onward):
        step = 1 if (direction == 0) == onward else dp - 1
        return {"dp": lax.rem(place + step, dp)}

    def behind(direction):
        return place if direction == 0 else dp - 1 - place

    def rows_of(direction, c):
        lent = 2 * half + (direction * LENT + c - whole) * chunk
        return pl.ds(pl.multiple_of(jnp.where(c < whole, direction * half + c * chunk, lent), chunk), chunk)

    def lent_copy(ref, sems, direction, i, to_decoder):
        mine = rows_of(direction, whole - LENT + i)
        theirs = rows_of(direction, whole + i)
        return pltpu.make_async_remote_copy(
            src_ref=ref.at[mine if to_decoder else theirs],
            dst_ref=ref.at[theirs if to_decoder else mine],
            send_sem=sems.at[direction, 0, i],
            recv_sem=sems.at[direction, 1, i],
            device_id={"section": 1 if to_decoder else 0},
            device_id_type=MESH,
        )

    def lent_part(direction, i):
        return lent_copy(own, x_part_sems, direction, i, True)

    def lent_total(direction, i):
        return lent_copy(totals, x_total_sems, direction, i, False)

    def part_copy(direction, c):
        return pltpu.make_async_remote_copy(
            src_ref=own.at[rows_of(direction, c)],
            dst_ref=arrived.at[rows_of(direction, c)],
            send_sem=part_sems.at[direction, 0, c],
            recv_sem=part_sems.at[direction, 1, c],
            device_id=along(direction, True),
            device_id_type=MESH,
        )

    def total_copy(direction, c):
        return pltpu.make_async_remote_copy(
            src_ref=totals.at[rows_of(direction, c)],
            dst_ref=totals.at[rows_of(direction, c)],
            send_sem=total_sems.at[direction, 0, c],
            recv_sem=total_sems.at[direction, 1, c],
            device_id=along(direction, False),
            device_id_type=MESH,
        )

    def add_part(direction, c):
        begins, ends = behind(direction) == 0, behind(direction) == dp - 1
        rows = rows_of(direction, c)

        @pl.when(c >= whole)
        def _():
            lent_part(direction, c - whole).wait_recv()

        @pl.when(begins)
        def _():
            part_copy(direction, c).start()

        @pl.when(jnp.logical_not(begins))
        def _():
            part_copy(direction, c).wait_recv()
            value = (own[rows, :].astype(F32) + arrived[rows, :].astype(F32)).astype(BF)

            @pl.when(ends)
            def _():
                totals[rows, :] = value
                total_copy(direction, c).start()

            @pl.when(jnp.logical_not(ends))
            def _():
                own[rows, :] = value
                part_copy(direction, c).start()

    def pass_total(direction, c):
        begins, ends = behind(direction) == 0, behind(direction) == dp - 1
        passes = jnp.logical_not(begins) & jnp.logical_not(ends)
        back = c >= whole

        @pl.when(passes | (back & jnp.logical_not(ends)))
        def _():
            total_copy(direction, c).wait_recv()

        @pl.when(passes)
        def _():
            total_copy(direction, c).start()

        @pl.when(back)
        def _():
            lent_total(direction, c - whole).start()

    skew = 2

    def chunk_step(step):
        for direction in range(2):
            c = step - skew * behind(direction)

            @pl.when((c >= 0) & (c < count))
            def _():
                add_part(direction, c)

        for direction in range(2):
            u = step - skew * (2 * (dp - 1) - behind(direction))

            @pl.when((u >= 0) & (u < count))
            def _():
                pass_total(direction, u)

        for i in range(4):

            @pl.when(step == jnp.where(enc, 12, 22) + i)
            def _():
                small(i)

    def sum_copy(which):
        where = ({"section": 1 - section}, {"tensor": sib}, {"tensor": across})[which]
        height = (8, 16, 16)[which]
        src = summand if which == 0 else sum_st.at[which - 1]
        return pltpu.make_async_remote_copy(
            src_ref=src.at[pl.ds(0, height)],
            dst_ref=sum_recv.at[which, pl.ds(0, height)],
            send_sem=sum_sems.at[which, 0],
            recv_sem=sum_sems.at[which, 1],
            device_id=where,
            device_id_type=MESH,
        )

    def all_copy(which, k, outgoing):
        ref = (dmod_all, sum_all, extra_all)[which]
        peer = lax.rem(place + k, dp)
        slot = place if outgoing else peer
        return pltpu.make_async_remote_copy(
            src_ref=ref.at[slot],
            dst_ref=ref.at[slot],
            send_sem=all_sems.at[which, 0, k],
            recv_sem=all_sems.at[which, 1, slot],
            device_id={"dp": peer},
            device_id_type=MESH,
        )

    def small(step):
        if step == 0:
            dmod_all[place] = dmod_low[...]
            for k in range(1, dp):
                all_copy(0, k, True).start()

            for copy in mod_loads:
                copy.wait()
            images = cond.shape[0]
            grads = dmod_low[...].astype(F32)
            d_silu = dot(grads[0:images].astype(BF), mod_w[0])
            for j in range(1, 6):
                d_silu += dot(grads[j * images : (j + 1) * images].astype(BF), mod_w[j])
            sig = jax.nn.sigmoid(cond[...])
            summand[0:8, :] = d_silu * (sig + cond[...] * sig * (1.0 - sig))
            summand[8:16, :] = squares[...]

            @pl.when(dec)
            def _():
                pl.semaphore_wait(here, 1)

            sum_copy(0).start()
        elif step == 1:
            sum_copy(0).wait()
            sum_st[0] = summand[...]
            sum_st[0, 0:8, :] += sum_recv[0, 0:8, :]
            sum_copy(1).start()
        elif step == 2:
            sum_copy(1).wait()
            sum_st[1] = sum_st[0] + sum_recv[1]
            sum_copy(2).start()
        elif step == 3:
            sum_copy(2).wait()
            total = sum_st[1] + sum_recv[2]
            sum_all[place, 0:8, :] = total[0:8].astype(BF)
            sum_all[place, 8:16, :] = silu[...]
            square = total[8:16, 0:LANES]
            for i in range(1, width // LANES):
                square += total[8:16, i * LANES : (i + 1) * LANES]
            extra_all[place, 0:8, :] = gain_sums[...]
            extra_all[place, 8:16, :] = jnp.zeros_like(gain_sums)
            extra_all[place, 8:16, 0:LANES] = square
            for i in range(8):
                extra_all[place, 8 + i : 9 + i, LANES : 2 * LANES] = jnp.full((1, LANES), labels[i].astype(F32))
            for k in range(1, dp):
                all_copy(1, k, True).start()
                all_copy(2, k, True).start()

    portion(0)
    pl.semaphore_wait(barrier, jnp.where(enc, dp + 2, dp + 1))

    @pl.when(enc)
    def _():
        pl.semaphore_signal(here, inc=1, device_id={"section": 1}, device_id_type=MESH)

    for step in range(10):
        chunk_step(step)
        portion(step + 1)

    def lend(i, carry):
        for direction in range(2):
            lent_part(direction, i).start()
        return carry

    @pl.when(enc)
    def _():
        lax.fori_loop(0, LENT, lend, 0)

    def later_step(step, carry):
        chunk_step(step)
        return carry

    lax.fori_loop(10, whole + LENT + 2 * skew * (dp - 1), later_step, 0)

    def lent_back(i, carry):
        for direction in range(2):

            @pl.when(enc)
            def _():
                lent_part(direction, i).wait_send()
                lent_total(direction, i).wait_recv()

            @pl.when(dec)
            def _():
                lent_total(direction, i).wait_send()

        return carry

    lax.fori_loop(0, LENT, lent_back, 0)

    for which in range(3):
        for k in range(1, dp):
            all_copy(which, k, True).wait_send()
            all_copy(which, k, False).wait_recv()

    def drain(c, carry):
        for direction in range(2):

            @pl.when(behind(direction) != dp - 1)
            def _():
                part_copy(direction, c).wait_send()

            @pl.when(behind(direction) != 0)
            def _():
                total_copy(direction, c).wait_send()

            @pl.when((behind(direction) == 0) & (c < whole))
            def _():
                total_copy(direction, c).wait_recv()

        return carry

    lax.fori_loop(0, count, drain, 0)


def run_tail(dp, a2, dgu, hid, dffn, a1, dqkv, mix, dattn, mod_w, pick, cond, squares, silu, dmod_low, gain_sums, labels):
    tokens, width = a2.shape
    hidden = hid.shape[1]
    vmem = pl.BlockSpec(memory_space=pltpu.VMEM)
    anywhere = pl.BlockSpec(memory_space=pl.ANY)
    half, chunk, _ = flat_plan(width, hidden, pick.shape[0])
    flat_rows, chunks = 2 * (half + LENT * chunk), half // chunk + LENT
    return pl.pallas_call(
        functools.partial(tail_kernel, dp),
        out_shape=(
            jax.ShapeDtypeStruct((flat_rows, LANES), BF),
            jax.ShapeDtypeStruct((dp,) + dmod_low.shape, BF),
            jax.ShapeDtypeStruct((dp, 16, width), BF),
            jax.ShapeDtypeStruct((dp, 16, gain_sums.shape[1]), F32),
        ),
        in_specs=[anywhere] * 9 + [vmem] * 6 + [pl.BlockSpec(memory_space=pltpu.SMEM)],
        out_specs=[vmem] * 4,
        scratch_shapes=[
            pltpu.VMEM((tokens, width), BF),
            pltpu.VMEM((tokens, dgu.shape[1]), BF),
            pltpu.VMEM((tokens, hidden), BF),
            pltpu.VMEM((tokens, width), BF),
            pltpu.VMEM((width, tokens), BF),
            pltpu.VMEM((flat_rows, LANES), BF),
            pltpu.VMEM((flat_rows, LANES), BF),
            pltpu.VMEM((6, 3 * LANES, width), BF),
            pltpu.VMEM((16, width), F32),
            pltpu.VMEM((2, 16, width), F32),
            pltpu.VMEM((3, 16, width), F32),
            pltpu.SemaphoreType.DMA((20,)),
            pltpu.SemaphoreType.DMA((2, 2, chunks)),
            pltpu.SemaphoreType.DMA((2, 2, chunks)),
            pltpu.SemaphoreType.DMA((3, 2)),
            pltpu.SemaphoreType.DMA((3, 2, dp)),
            pltpu.SemaphoreType.DMA((2, 2, LENT)),
            pltpu.SemaphoreType.DMA((2, 2, LENT)),
            pltpu.SemaphoreType.REGULAR,
        ],
        compiler_params=pltpu.CompilerParams(
            collective_id=1, has_side_effects=True, vmem_limit_bytes=62 * 2**20
        ),
    )(a2, dgu, hid, dffn, a1, dqkv, mix, dattn, mod_w, pick, cond, squares, silu, dmod_low, gain_sums, labels)


def finish_kernel(
    count,
    flat_hbm,
    z_hbm,
    dx_hbm,
    dmod_all,
    sum_all,
    extra_all,
    select,
    gu_hbm,
    down_hbm,
    qkv_hbm,
    out_hbm,
    z_out,
    dx_out,
    mod_hbm,
    class_hbm,
    q_gain_out,
    k_gain_out,
    stats_out,
    flat,
    gate_up,
    down,
    qkv,
    out,
    mod,
    classes,
    z_rows,
    dx_rows,
    load_sems,
    store_sems,
):
    width, hidden = gate_up.shape[1], gate_up.shape[2]
    part, blocks, hidden_blocks = out.shape[0], width // LANES, hidden // LANES
    _, _, pieces = flat_plan(width, hidden, part)
    groups = (
        [(0, b) for b in range(hidden_blocks)],
        [(0, hidden_blocks + b) for b in range(hidden_blocks)],
        [(1, b) for b in range(blocks)],
        [(2, b) for b in range(blocks)],
        [(3, b) for b in range(blocks)],
    )
    loads = []
    for group in groups:
        spans = []
        for segment, block in group:
            for at, _, size in pieces(segment, block):
                if spans and spans[-1][0] + spans[-1][1] == at:
                    spans[-1][1] += size
                else:
                    spans.append([at, size])
        copies = []
        for at, size in spans:
            rows = pl.ds(at, size)
            sem = load_sems.at[len(loads), len(copies)]
            copies.append(pltpu.make_async_copy(flat_hbm.at[rows], flat.at[rows], sem))
            copies[-1].start()
        loads.append(copies)
    inward = (
        pltpu.make_async_copy(z_hbm, z_rows, load_sems.at[0, 2]),
        pltpu.make_async_copy(dx_hbm, dx_rows, load_sems.at[1, 2]),
    )
    outward = (
        pltpu.make_async_copy(z_rows, z_out, store_sems.at[5]),
        pltpu.make_async_copy(dx_rows, dx_out, store_sems.at[6]),
    )
    for copy in inward:
        copy.start()

    dp, images = dmod_all.shape[0], dmod_all.shape[1] // 8
    me = lax.axis_index("tensor")
    silu = jnp.concatenate([sum_all[p].astype(F32)[8:16] for p in range(dp)], axis=0).astype(BF)
    grad_cond = jnp.concatenate([sum_all[p].astype(F32)[0:8] for p in range(dp)], axis=0).astype(BF)
    dmods = [dmod_all[p].astype(F32) for p in range(dp)]
    mod_stores = []
    for j in range(6):
        grads = jnp.concatenate([dmods[p][j * images : (j + 1) * images] for p in range(dp)], axis=0).astype(BF)
        mod[j] = dot_tn(grads, silu)
        mine = pl.ds(pl.multiple_of(me * (part - 2 * LANES), 8), part)
        mod_stores.append(pltpu.make_async_copy(mod.at[j, mine], mod_hbm.at[j], store_sems.at[8 + j]))
        mod_stores[-1].start()
    labels = jnp.concatenate([extra_all[p, 8:16, LANES : LANES + 1] for p in range(dp)], axis=0)
    lanes = lax.broadcasted_iota(jnp.int32, (dp * images, classes.shape[0]), 1)
    one_hot = jnp.where(lanes == labels.astype(jnp.int32), 1.0, 0.0).astype(BF)
    for at, size in chunks_of(width, 384):
        classes[:, at : at + size] = dot_tn(one_hot, grad_cond[:, at : at + size])
    class_store = pltpu.make_async_copy(classes.at[pl.ds(0, class_hbm.shape[0])], class_hbm, store_sems.at[7])
    class_store.start()

    for i in range(2):
        inward[i].wait()
        outward[i].start()

    gain_sum, squares = extra_all[0, 0:8, :], extra_all[0, 8:16, 0:LANES]
    for p in range(1, dp):
        gain_sum += extra_all[p, 0:8, :]
        squares += extra_all[p, 8:16, 0:LANES]
    gain_sum = lax.dot_general(
        gain_sum,
        select[...].astype(F32),
        (((1,), (1,)), ((), ())),
        precision=lax.Precision.HIGHEST,
        preferred_element_type=F32,
    )
    q_gain_out[...] = gain_sum[0:1]
    k_gain_out[...] = gain_sum[1:2]
    for i in range(3):
        stats_out[0:1, i : i + 1] = jnp.sqrt(jnp.sum(squares[i : i + 1], axis=1, keepdims=True) * (1.0 / count))

    stores = (
        pltpu.make_async_copy(gate_up.at[0], gu_hbm.at[0], store_sems.at[0]),
        pltpu.make_async_copy(gate_up.at[1], gu_hbm.at[1], store_sems.at[1]),
        pltpu.make_async_copy(down, down_hbm, store_sems.at[2]),
        pltpu.make_async_copy(qkv, qkv_hbm, store_sems.at[3]),
        pltpu.make_async_copy(out, out_hbm, store_sems.at[4]),
    )
    for i, group in enumerate(groups):
        for copy in loads[i]:
            copy.wait()
        for segment, block in group:
            for at, low, size in pieces(segment, block):
                value = flat[at : at + size, :].astype(F32)
                rows = slice(low, low + size)
                cols = slice(block * LANES, (block + 1) * LANES)
                if segment == 0:
                    local = block % hidden_blocks
                    gate_up[block // hidden_blocks, rows, local * LANES : (local + 1) * LANES] = value
                elif segment == 1:
                    down[rows, cols] = value
                elif segment == 2:
                    qkv[rows, cols] = value
                else:
                    out[rows, cols] = value
        stores[i].start()
    for copy in (*stores, *outward, *mod_stores, class_store):
        copy.wait()


def run_finish(count, class_count, hidden, flat, z_rows, dx_rows, dmod_all, sum_all, extra_all, select):
    part, width = select.shape[0], sum_all.shape[2]
    vmem = pl.BlockSpec(memory_space=pltpu.VMEM)
    anywhere = pl.BlockSpec(memory_space=pl.ANY)
    shapes = ((2, width, hidden), (hidden, width), (3 * part, width), (part, width))
    return pl.pallas_call(
        functools.partial(finish_kernel, count),
        out_shape=tuple(jax.ShapeDtypeStruct(shape, F32) for shape in shapes)
        + (
            jax.ShapeDtypeStruct(z_rows.shape, BF),
            jax.ShapeDtypeStruct(dx_rows.shape, F32),
            jax.ShapeDtypeStruct((6, part, width), F32),
            jax.ShapeDtypeStruct((class_count, width), F32),
            jax.ShapeDtypeStruct((1, part), F32),
            jax.ShapeDtypeStruct((1, part), F32),
            jax.ShapeDtypeStruct((1, 3), F32),
        ),
        in_specs=[anywhere] * 3 + [vmem] * 4,
        out_specs=[anywhere] * 8 + [vmem] * 3,
        scratch_shapes=[pltpu.VMEM(flat.shape, BF)]
        + [pltpu.VMEM(shape, F32) for shape in shapes]
        + [
            pltpu.VMEM((6, 3 * LANES, width), F32),
            pltpu.VMEM((-(-class_count // LANES) * LANES, width), F32),
            pltpu.VMEM(z_rows.shape, BF),
            pltpu.VMEM(dx_rows.shape, F32),
            pltpu.SemaphoreType.DMA((5, 3)),
            pltpu.SemaphoreType.DMA((14,)),
        ],
        compiler_params=pltpu.CompilerParams(vmem_limit_bytes=60 * 2**20),
    )(flat, z_rows, dx_rows, dmod_all, sum_all, extra_all, select)


def time_embed(bin_row, feature_count):
    halfway = feature_count // 2
    frequency = jnp.exp(-math.log(10000.0) * jnp.arange(halfway, dtype=F32) / halfway)
    moment = (bin_row.astype(F32) + 0.5) * (1000.0 / NBINS)
    angles = moment[:, None] * frequency[None, :]
    return jnp.concatenate([jnp.cos(angles), jnp.sin(angles)], axis=-1)


def per_device(
    tokens,
    velocity_grad,
    bins,
    labels,
    places,
    class_table,
    mod_weight,
    qkv_weight,
    out_weight,
    gate_up_weight,
    down_weight,
    q_gain,
    k_gain,
):
    micro, per_micro, rows, width = tokens.shape
    images = micro * per_micro
    dp = lax.axis_size("dp")
    me = lax.axis_index("tensor")
    heads = q_gain.shape[1] // HEAD_DIM
    select = jnp.asarray(head_select(heads), BF)

    label_row = labels.reshape(images)
    one_hot = label_row[:, None] == jnp.arange(class_table.shape[0], dtype=jnp.int32)[None, :]
    picked = jnp.dot(one_hot.astype(BF), class_table, preferred_element_type=F32)
    cond = time_embed(bins.reshape(images), width) + picked
    silu_low = jax.nn.silu(cond).astype(BF)
    mod_w = mod_weight[0]
    part = width // 4
    columns = jnp.einsum("id,djf->ijf", silu_low, mod_w, preferred_element_type=F32)
    shift = me * (part - 2 * LANES)
    mod_cols = lax.dynamic_update_slice(jnp.zeros((images, 8, 3 * LANES), F32), columns, (0, 0, shift))

    table, table_parts = angle_table(), []
    for _ in range(3):
        table_parts.append(table.astype(BF))
        table = table - table_parts[-1].astype(np.float32)
    table_parts.append(np.zeros((LANES - 6 * GRID, 2 * LANES), BF))

    results = run_main(
        tokens.reshape(images, rows, width),
        velocity_grad.reshape(images, rows, width),
        mod_cols,
        places,
        jnp.asarray(np.concatenate(table_parts)),
        jnp.transpose(qkv_weight[0], (0, 2, 1)),
        out_weight[0],
        gate_up_weight[0],
        down_weight[0],
        q_gain,
        k_gain,
        select,
    )
    z_rows, dx_rows, dmod_part, gain_sums, squares, a1, a2, d_ffn, d_attn, units, mixed, d_gu, d_qkv = results

    lanes_all = heads * LANES
    flat = images * 4 * rows
    flat_grads, dmod_all, sum_all, extra_all = run_tail(
        dp,
        a2.reshape(flat, width),
        d_gu.reshape(flat, d_gu.shape[2]),
        units.reshape(flat, units.shape[2]),
        d_ffn.reshape(flat, width),
        a1.reshape(flat, width),
        d_qkv.reshape(flat, d_qkv.shape[2]),
        mixed.reshape(flat, lanes_all),
        d_attn.reshape(flat, width),
        jnp.transpose(mod_w, (1, 2, 0)),
        select,
        cond,
        squares,
        silu_low,
        dmod_part.reshape(8 * images, 3 * LANES),
        gain_sums,
        label_row,
    )
    count = images * rows * width * dp * lax.axis_size("tensor")
    finished = run_finish(
        count,
        class_table.shape[0],
        units.shape[2],
        flat_grads,
        z_rows,
        dx_rows,
        dmod_all,
        sum_all,
        extra_all,
        select,
    )
    gate_up_grad, down_grad, qkv_grad, out_grad, z_out, dx_out, mod_grad, class_grad, q_grad, k_grad, stats = finished
    whole = (1, micro, per_micro, rows, width)
    return (
        z_out.reshape(whole),
        dx_out.reshape(whole),
        jnp.transpose(mod_grad, (2, 0, 1))[None],
        jnp.transpose(qkv_grad.reshape(3, part, width), (0, 2, 1))[None],
        out_grad[None],
        gate_up_grad[None],
        down_grad[None],
        q_grad,
        k_grad,
        class_grad,
        stats,
    )


def solution(mesh):
    return jax.shard_map(
        per_device,
        mesh=mesh,
        in_specs=(
            P(None, "dp", "tensor", None),
            P(None, "dp", "tensor", None),
            P(None, "dp"),
            P(None, "dp"),
            P(None, "dp", None),
            P(),
            P("section", None, None, "tensor"),
            P("section", None, None, "tensor"),
            P("section", "tensor", None),
            P("section", None, None, "tensor"),
            P("section", "tensor", None),
            P("section", "tensor"),
            P("section", "tensor"),
        ),
        out_specs=(
            P("section", None, "dp", "tensor", None),
            P("section", None, "dp", "tensor", None),
            P("section", None, None, "tensor"),
            P("section", None, None, "tensor"),
            P("section", "tensor", None),
            P("section", None, None, "tensor"),
            P("section", "tensor", None),
            P("section", "tensor"),
            P("section", "tensor"),
            P(),
            P("section", None),
        ),
        check_vma=False,
    )
```

```python
import functools
import math

import jax
import jax.numpy as jnp
import numpy as np
from jax import lax
from jax.experimental import pallas as pl
from jax.experimental.pallas import tpu as pltpu
from jax.sharding import PartitionSpec as P

MESH = pl.DeviceIdType.MESH
HEAD_DIM = 72
LANES = 128
NBINS = 1000
GRID = 16
EPS = 1e-06
BF = jnp.bfloat16
F32 = jnp.float32
SCALE = HEAD_DIM**-0.5
LOG2E = math.log2(math.e)

KEEP, SLOTS, PACK = 2, 4, 4
LENT = 4
ORDERS = (
    (
        0, 1, 8, 2, 3, 16, 9, 24, 10, 4, 17, 32, 11, 25, 18, 40, 26, 48, 33,
        56, 19, 34, 12, 41, 64, 49, 27, 57, 42, 144, 50, 35, 65, 58, 20, 43, 5, 145,
        66, 28, 51, 13, 146, 59, 36, 6, 21, 67, 44, 52, 60, 147, 14, 7, 29, 68, 22,
        15, 37, 148, 30, 23, 38, 31, 45, 53, 61, 39, 46, 54, 69, 62, 149, 70, 47, 72,
        55, 80, 63, 150, 88, 71, 151, 96, 104, 73, 81, 89, 112, 74, 97, 120, 82, 128, 105,
        90, 136, 98, 113, 75, 121, 83, 106, 91, 114, 129, 99, 122, 76, 130, 137, 107, 84, 92,
        77, 115, 100, 138, 123, 78, 85, 108, 93, 86, 79, 131, 94, 116, 101, 102, 124, 87, 109,
        132, 95, 139, 117, 103, 110, 125, 111, 140, 133, 118, 126, 119, 141, 134, 127, 135, 142, 143,
    ),
    (
        72, 73, 74, 80, 75, 81, 82, 76, 83, 77, 0, 8, 78, 16, 1, 24, 84, 9, 32,
        79, 17, 40, 85, 2, 25, 88, 10, 33, 48, 56, 18, 96, 41, 3, 86, 26, 89, 11,
        104, 97, 19, 4, 64, 112, 34, 27, 49, 120, 42, 105, 57, 90, 12, 113, 35, 98, 20,
        65, 128, 43, 121, 28, 50, 106, 136, 91, 5, 36, 13, 129, 114, 58, 99, 21, 122, 44,
        51, 66, 29, 59, 130, 6, 92, 14, 37, 107, 22, 7, 137, 67, 138, 30, 15, 87, 52,
        60, 45, 100, 115, 23, 38, 123, 31, 108, 93, 53, 131, 46, 68, 61, 39, 94, 116, 139,
        101, 102, 124, 47, 69, 109, 132, 95, 117, 144, 110, 103, 125, 140, 54, 133, 145, 118, 146,
        55, 111, 62, 126, 141, 119, 134, 63, 127, 147, 135, 142, 148, 70, 149, 71, 150, 143, 151,
    ),
)


def lane_of():
    quarter = HEAD_DIM // 4
    lanes = np.zeros((HEAD_DIM,), np.int64)
    for half in range(2):
        for part in range(2):
            for i in range(quarter):
                lanes[half * 2 * quarter + part * quarter + i] = part * 64 + half * quarter + i
    return lanes


def head_select(heads):
    select = np.zeros((heads * HEAD_DIM, heads * LANES), np.float32)
    lanes = lane_of()
    for h in range(heads):
        for f in range(HEAD_DIM):
            select[h * HEAD_DIM + f, h * LANES + lanes[f]] = 1.0
    return select


def angle_table():
    quarter = HEAD_DIM // 4
    frequency = (10000.0 ** (-np.arange(quarter, dtype=np.float32) / np.float32(quarter))).astype(np.float32)
    lanes = lane_of().reshape(2, 2, quarter)
    table = np.zeros((2 * GRID, 2 * LANES), np.float32)
    for place in range(GRID):
        angle = np.float32(place) * frequency
        for half in range(2):
            for part in range(2):
                sign = -1.0 if part == 0 else 1.0
                table[half * GRID + place, lanes[half, part]] = np.cos(angle)
                table[half * GRID + place, LANES + lanes[half, part]] = sign * np.sin(angle)
    return table


def dot(a, b):
    return lax.dot_general(a, b, (((1,), (0,)), ((), ())), preferred_element_type=F32)


def dot_nt(a, b):
    return lax.dot_general(a, b, (((1,), (1,)), ((), ())), preferred_element_type=F32)


def dot_tn(a, b):
    return lax.dot_general(a, b, (((0,), (0,)), ((), ())), preferred_element_type=F32)


def order_words(order, base):
    words = []
    for at in range(0, len(order), PACK):
        words.append(sum(entry * base**i for i, entry in enumerate(order[at : at + PACK])))
    while len(words) & (len(words) - 1):
        words.append(0)
    return words


def chunks_of(size, width):
    return [(at, min(width, size - at)) for at in range(0, size, width)]


def main_kernel(
    images,
    heads,
    tok,
    vel,
    mod_cols,
    places,
    angles,
    qkv_hbm,
    out_hbm,
    wgu_hbm,
    wdn_hbm,
    q_gain,
    k_gain,
    select,
    zout,
    dxout,
    dmod_part,
    gacc,
    sacc,
    a1_hbm,
    a2_hbm,
    dffn_hbm,
    dattn_hbm,
    hid_hbm,
    mix_hbm,
    dgu_hbm,
    dqkv_hbm,
    turns,
    wqkv,
    wout,
    wgu,
    wdn,
    gains,
    xin,
    din,
    a1f,
    a2f,
    dffn,
    dattn,
    x1s,
    attns,
    ffns,
    keep,
    send_a,
    recv_a,
    send_y,
    recv_y,
    mix_st,
    hid_st,
    dgu_st,
    dqkv_st,
    mod,
    mod_recv,
    dmod,
    mod_sems,
    dmod_sems,
    ag_sems,
    rs_sems,
    zx_sems,
    out_sems,
    in_sems,
):
    rows = tok.shape[1]
    width = tok.shape[2]
    hidden = wdn.shape[0]
    wide = chunks_of(width, 512)
    section = lax.axis_index("section")
    me = lax.axis_index("tensor")
    sib = me + 1 - 2 * lax.rem(me, 2)
    across = lax.rem(me + 2, 4)
    diag = lax.rem(sib + 2, 4)
    peers = (sib, across, diag)
    other = 1 - section
    enc = section == 0
    dec = section == 1

    load_x = pltpu.make_async_copy(tok, xin, in_sems.at[0])
    load_d = pltpu.make_async_copy(vel, din, in_sems.at[1])
    tokens, part = dattn.shape[1], out_hbm.shape[0]
    groups = [qkv_hbm.at[j] for j in range(3)] + [out_hbm]
    load_w = [
        pltpu.make_async_copy(wgu_hbm, wgu, in_sems.at[2]),
        pltpu.make_async_copy(wdn_hbm, wdn, in_sems.at[3]),
    ]
    load_raw = []
    for j, group in enumerate(groups):
        for i, (at, size) in enumerate(((0, tokens), (tokens, part - tokens))):
            src, dst = group.at[pl.ds(at, size)], dattn.at[2 * j + i, pl.ds(0, size)]
            load_raw.append(pltpu.make_async_copy(src, dst, in_sems.at[4 + 2 * j + i]))
    for copy in load_raw:
        copy.start()

    @pl.when(enc)
    def _():
        load_x.start()

    @pl.when(dec)
    def _():
        load_d.start()

    barrier = pltpu.get_barrier_semaphore()
    pl.semaphore_signal(barrier, inc=1, device_id={"tensor": sib}, device_id_type=MESH)
    pl.semaphore_signal(barrier, inc=1, device_id={"tensor": across}, device_id_type=MESH)
    pl.semaphore_signal(barrier, inc=1, device_id={"tensor": diag}, device_id_type=MESH)
    pl.semaphore_signal(barrier, inc=1, device_id={"section": other}, device_id_type=MESH)

    mod[...] = jnp.zeros_like(mod)
    gacc[...] = jnp.zeros_like(gacc)
    sacc[...] = jnp.zeros_like(sacc)
    dmod[...] = jnp.zeros_like(dmod)

    pl.semaphore_wait(barrier, 4)

    def remote(src, dst, send_sem, recv_sem, where):
        return pltpu.make_async_remote_copy(
            src_ref=src, dst_ref=dst, send_sem=send_sem, recv_sem=recv_sem, device_id=where, device_id_type=MESH
        )

    def gather(which, buf, n, kind):
        src, dst, where = ((0, rows, across), (0, 2 * rows, sib), (rows, 3 * rows, sib))[kind]
        return remote(
            buf.at[n, pl.ds(src, rows)],
            buf.at[n, pl.ds(dst, rows)],
            ag_sems.at[which, 2 * kind, n],
            ag_sems.at[which, 2 * kind + 1, n],
            {"tensor": where},
        )

    def its_tiles(device):
        return pl.ds(pl.multiple_of(device * (2 * LANES), LANES), 3 * LANES)

    def mod_copy(k):
        return remote(mod_cols, mod_recv.at[k], mod_sems.at[0, k], mod_sems.at[1, k], {"tensor": peers[k]})

    def dmod_copy(k, n):
        return remote(
            dmod.at[n, :, its_tiles(peers[k])],
            mod_recv.at[k, n],
            dmod_sems.at[0, k, n],
            dmod_sems.at[1, k, n],
            {"tensor": peers[k]},
        )

    for k in (1, 2, 0):
        mod_copy(k).start()

    @pl.when(enc)
    def _():
        load_x.wait()
        a1f[0, 0:rows, :] = xin[0]
        gather(0, a1f, 0, 0).start()
        gather(0, a1f, 0, 1).start()

    @pl.when(dec)
    def _():
        load_d.wait()

    for copy in load_w:
        copy.start()
    mod[:, :, its_tiles(me)] = mod_cols[...]

    gains[0:1, :] = dot(q_gain[...], select[...])
    gains[1:2, :] = dot(k_gain[...], select[...])
    for j in range(4):
        load_raw[2 * j].wait()
        load_raw[2 * j + 1].wait()
        ref = wqkv.at[j] if j < 3 else wout
        for at, size in wide:
            span = pl.ds(at, size)
            value = dot_tn(select[0:tokens, :], dattn[2 * j, :, span])
            value += dot_tn(select[tokens:part, :], dattn[2 * j + 1, 0 : part - tokens, span])
            ref[:, span] = value.astype(BF)

    spots = jnp.concatenate([places[i] for i in range(places.shape[0])], axis=0).astype(F32).T
    lane = lax.broadcasted_iota(jnp.int32, (rows, LANES), 1)
    spot = lax.rem(lane, 2 * GRID)
    by_row, used = spot < GRID, lane < 6 * GRID
    spot = jnp.where(by_row, spot, spot - GRID).astype(F32)
    for block in range(4):
        high, low, my_high, my_low = block // 2, block % 2, lax.div(me, 2), lax.rem(me, 2)
        at = high + my_high - 2 * high * my_high + 2 * (low + my_low - 2 * low * my_low)
        here = pl.ds(pl.multiple_of(at * rows, rows), rows)
        mine = slice(block * rows, (block + 1) * rows)
        for n in range(images):
            row = jnp.floor(spots[mine, n : n + 1] * (1.0 / GRID))
            marks = jnp.where(by_row, row, spots[mine, n : n + 1] - GRID * row) == spot
            turns[n, here, :] = dot(jnp.where(marks & used, 1.0, 0.0).astype(BF), angles[...])

    for k in range(3):
        mod_copy(k).wait()
        mod[:, :, its_tiles(peers[k])] += mod_recv[k]

    def gather_start(which, buf, n):
        gather(which, buf, n, 0).start()
        gather(which, buf, n, 1).start()

    def gather_relay(which, buf, n):
        gather(which, buf, n, 0).wait_recv()
        gather(which, buf, n, 2).start()

    def attn_relay(n):
        @pl.when(enc)
        def _():
            gather(0, a1f, n, 0).wait_recv()

        @pl.when(dec)
        def _():
            zy_pass(n).wait_recv()
            values = a1f[n, rows : 2 * rows, :].astype(F32)
            a1f[n, rows : 2 * rows, :] = modulated(values, mod_row(n, 0), mod_row(n, 1)).astype(BF)

        gather(0, a1f, n, 2).start()

    def gather_wait(which, buf, n):
        gather(which, buf, n, 1).wait_recv()
        gather(which, buf, n, 2).wait_recv()

    def gather_drain(which, buf, n):
        for kind in range(3):
            gather(which, buf, n, kind).wait_send()

    def to_sibling(which, n):
        return remote(
            send_a.at[which, lax.rem(n, KEEP)],
            recv_a.at[which, lax.rem(n, SLOTS)],
            rs_sems.at[which, 0, n],
            rs_sems.at[which, 1, n],
            {"tensor": sib},
        )

    def over_y(which, n):
        return remote(
            send_y.at[which, lax.rem(n, KEEP)],
            recv_y.at[which, lax.rem(n, SLOTS)],
            rs_sems.at[which, 2, n],
            rs_sems.at[which, 3, n],
            {"tensor": across},
        )

    def scatter_put(which, n, at, size, values):
        kind, own = which, lax.rem(n, KEEP)
        keep[kind, own, :, pl.ds(at, size)] = values[0 : 2 * rows]
        send_a[kind, own, :, pl.ds(at, size)] = values[2 * rows : 4 * rows].astype(BF)

    def scatter_start(which, n):
        to_sibling(which, n).start()

    def scatter_middle(which, n):
        kind, own, slot = which, lax.rem(n, KEEP), lax.rem(n, SLOTS)
        to_sibling(which, n).wait()
        theirs = recv_a[kind, slot, rows : 2 * rows].astype(F32)
        send_y[kind, own] = (keep[kind, own, rows : 2 * rows] + theirs).astype(BF)
        over_y(which, n).start()

    def scatter_end(which, n):
        kind, own, slot = which, lax.rem(n, KEEP), lax.rem(n, SLOTS)
        over_y(which, n).wait()
        mine = keep[kind, own, 0:rows] + recv_a[kind, slot, 0:rows].astype(F32)
        return mine + recv_y[kind, slot].astype(F32)

    def z_copy(n):
        return remote(zout.at[n], xin.at[n], zx_sems.at[0, n], zx_sems.at[1, n], {"section": other})

    def zy_copy(n):
        return remote(
            zout.at[n], dattn.at[n, pl.ds(rows, rows)], zx_sems.at[4, n], zx_sems.at[5, n], {"tensor": across}
        )

    def zy_pass(n):
        return remote(
            dattn.at[n, pl.ds(rows, rows)],
            a1f.at[n, pl.ds(rows, rows)],
            zx_sems.at[6, n],
            zx_sems.at[7, n],
            {"section": other},
        )

    def dz_copy(n):
        return remote(xin.at[n], din.at[n], zx_sems.at[2, n], zx_sems.at[3, n], {"section": other})

    def mod_row(n, row):
        return mod[n, pl.ds(row, 1), :]

    def inverse_rms(values):
        return lax.rsqrt(jnp.mean(values * values, axis=-1, keepdims=True) + EPS)

    def column_sum(values):
        return jnp.sum(values, axis=0, keepdims=True)

    def modulated(values, shift, scale):
        return (values * inverse_rms(values)) * (1.0 + scale) + shift

    def norm_back(values, grad, scale):
        inv = inverse_rms(values)
        normed = values * inv
        d_normed = grad * (1.0 + scale)
        d_values = inv * (d_normed - normed * jnp.mean(d_normed * normed, axis=-1, keepdims=True))
        return d_values, column_sum(grad), column_sum(grad * normed)

    def head_norm(raw):
        inv = lax.rsqrt(jnp.sum(raw * raw, axis=-1, keepdims=True) * (1.0 / HEAD_DIM) + EPS)
        return inv, raw * inv

    def turn(values, c, s):
        return values * c + pltpu.roll(values, 64, 1) * s

    def turn_back(values, c, s):
        return values * c - pltpu.roll(values, 64, 1) * s

    def softmax_parts(scaled, k):
        powered = jnp.exp2(dot_nt(scaled, k))
        return powered, 1.0 / jnp.sum(powered, axis=-1, keepdims=True)

    def out_copy(which, n):
        src = (a1f, a2f, dffn, dattn, hid_st, mix_st, dgu_st, dqkv_st)[which]
        dst = (a1_hbm, a2_hbm, dffn_hbm, dattn_hbm, hid_hbm, mix_hbm, dgu_hbm, dqkv_hbm)[which]
        return pltpu.make_async_copy(src.at[n] if which < 4 else src, dst.at[n], out_sems.at[which, n])

    def staged_ready(which, n):
        @pl.when(n > 0)
        def _():
            out_copy(which, n - 1).wait()

    def attn_in(n):
        @pl.when(dec)
        def _():
            z_copy(n).wait_recv()

        values = xin[n].astype(F32)
        sacc[0:1, :] += column_sum(values * values)

        @pl.when(dec | (n > 0))
        def _():
            a1f[n, 0:rows, :] = modulated(values, mod_row(n, 0), mod_row(n, 1)).astype(BF)

            @pl.when(enc)
            def _():
                gather(0, a1f, n, 0).start()

            gather(0, a1f, n, 1).start()

    def attn_drain(n):
        gather(0, a1f, n, 1).wait_send()
        gather(0, a1f, n, 2).wait_send()

        @pl.when(enc)
        def _():
            gather(0, a1f, n, 0).wait_send()

    def attn_compute(n):
        gather_wait(0, a1f, n)

        @pl.when(enc & (n == 0))
        def _():
            attn_drain(n)
            for at in range(0, 4 * rows, rows):
                values = a1f[0, at : at + rows, :].astype(F32)
                a1f[0, at : at + rows, :] = modulated(values, mod_row(0, 0), mod_row(0, 1)).astype(BF)

        staged_ready(5, n)
        a1 = a1f[n]
        c, s = turns[n, :, 0:LANES], turns[n, :, LANES : 2 * LANES]
        for pair in range(heads // 2):
            span = pl.ds(pair * 2 * LANES, 2 * LANES)
            q2 = dot_nt(a1, wqkv[0, span, :])
            k2 = dot_nt(a1, wqkv[1, span, :])
            v2 = dot_nt(a1, wqkv[2, span, :]).astype(BF)
            for half in range(2):
                at = (pair * 2 + half) * LANES
                cut = slice(half * LANES, (half + 1) * LANES)
                q_gain = gains[0:1, at : at + LANES] * (SCALE * LOG2E)
                q = turn(head_norm(q2[:, cut])[1] * q_gain, c, s).astype(BF)
                k = turn(head_norm(k2[:, cut])[1] * gains[1:2, at : at + LANES], c, s).astype(BF)
                powered, inverse = softmax_parts(q, k)
                mix_st[:, at : at + LANES] = (dot(powered.astype(BF), v2[:, cut]) * inverse).astype(BF)
        mixed = mix_st[...]
        for at, size in wide:
            scatter_put(0, n, at, size, dot(mixed, wout[:, pl.ds(at, size)]))
        scatter_start(0, n)
        out_copy(5, n).start()
        out_copy(0, n).start()

        @pl.when(dec | (n > 0))
        def _():
            attn_drain(n)

    def ffn_in(n):
        attended = scatter_end(0, n)
        attns[n] = attended.astype(BF)
        values = xin[n].astype(F32) + mod_row(n, 2) * attended
        x1s[n] = values
        sacc[1:2, :] += column_sum(values * values)
        a2f[n, 0:rows, :] = modulated(values, mod_row(n, 3), mod_row(n, 4)).astype(BF)
        gather_start(1, a2f, n)

    def ffn_down(n, units):
        for at, size in wide:
            scatter_put(1, n, at, size, dot(units, wdn[:, pl.ds(at, size)]))
        scatter_start(1, n)
        out_copy(1, n).start()
        gather_drain(1, a2f, n)

    def first_ffn(n):
        gather_wait(1, a2f, n)

        @pl.when(n == 0)
        def _():
            load_w[0].wait()
            load_w[1].wait()

    def ffn_compute(n):
        @pl.when(enc)
        def _():
            first_ffn(n)
            a2 = a2f[n]
            for at, size in chunks_of(hidden, 256):
                span = pl.ds(at, size)
                gate_val = dot(a2, wgu[0, :, span])
                up_val = dot(a2, wgu[1, :, span])
                hid_st[:, span] = (gate_val * jax.nn.sigmoid(gate_val) * up_val).astype(BF)
            ffn_down(n, hid_st[...])

    def block_out(n):
        feedfwd = scatter_end(1, n)
        ffns[n] = feedfwd.astype(BF)
        values = x1s[n] + mod_row(n, 5) * feedfwd
        sacc[2:3, :] += column_sum(values * values)
        zout[n] = values.astype(BF)

        @pl.when(enc)
        def _():
            z_copy(n).start()
            zy_copy(n).start()

        @pl.when(dec)
        def _():
            dmod[n, 5:6, :] = column_sum(din[n].astype(F32) * feedfwd)

    def pass_on(n):
        @pl.when(enc)
        def _():
            zy_copy(n).wait_recv()
            zy_pass(n).start()

        @pl.when(dec)
        def _():
            send_dmod(n)

    def send_dmod(n):
        for k in range(3):
            dmod_copy(k, n).start()

    def ffn_grad_in(n):
        @pl.when(enc)
        def _():
            zy_copy(n).wait_send()
            zy_pass(n).wait_send()
            dz_copy(n).wait_recv()

        grad = din[n].astype(F32)
        dffn[n, 0:rows, :] = (mod_row(n, 5) * grad).astype(BF)
        gather_start(2, dffn, n)

        @pl.when(enc)
        def _():
            dmod[n, 5:6, :] = column_sum(grad * ffns[n].astype(F32))

    def ffn_grad_compute(n):
        @pl.when(dec)
        def _():
            first_ffn(n)

        gather_wait(2, dffn, n)
        staged_ready(4, n)
        staged_ready(6, n)
        grad = dffn[n]
        a2 = a2f[n]
        for at, size in chunks_of(hidden, 256):
            span = pl.ds(at, size)
            gate_val = dot(a2, wgu[0, :, span])
            up_val = dot(a2, wgu[1, :, span])
            d_hidden = dot_nt(grad, wdn[span, :])
            sig = jax.nn.sigmoid(gate_val)
            act = gate_val * sig
            hid_st[:, span] = (act * up_val).astype(BF)
            dgu_st[:, span] = (d_hidden * up_val * (sig + act * (1.0 - sig))).astype(BF)
            dgu_st[:, pl.ds(hidden + at, size)] = (d_hidden * act).astype(BF)
        d_gate = dgu_st[:, 0:hidden]
        d_up = dgu_st[:, hidden : 2 * hidden]
        for at, size in wide:
            span = pl.ds(at, size)
            scatter_put(2, n, at, size, dot_nt(d_gate, wgu[0, span, :]) + dot_nt(d_up, wgu[1, span, :]))
        scatter_start(2, n)

        @pl.when(dec)
        def _():
            ffn_down(n, hid_st[...])

        out_copy(4, n).start()
        out_copy(6, n).start()
        out_copy(2, n).start()
        gather_drain(2, dffn, n)

    def attn_grad_in(n):
        d_a2 = scatter_end(2, n)
        grad, d_shift, d_scale = norm_back(x1s[n], d_a2, mod_row(n, 4))
        grad = grad + din[n].astype(F32)
        dxout[n] = grad
        dattn[n, 0:rows, :] = (mod_row(n, 2) * grad).astype(BF)
        gather_start(3, dattn, n)
        dmod[n, 2:3, :] = column_sum(grad * attns[n].astype(F32))
        dmod[n, 3:4, :] = d_shift
        dmod[n, 4:5, :] = d_scale

    def attn_grad_compute(n):
        gather_wait(3, dattn, n)
        staged_ready(7, n)
        grad = dattn[n]
        a1 = a1f[n]
        c, s = turns[n, :, 0:LANES], turns[n, :, LANES : 2 * LANES]
        lanes_all = heads * LANES
        for pair in range(heads // 2):
            span = pl.ds(pair * 2 * LANES, 2 * LANES)
            q2 = dot_nt(a1, wqkv[0, span, :])
            k2 = dot_nt(a1, wqkv[1, span, :])
            v2 = dot_nt(a1, wqkv[2, span, :]).astype(BF)
            d_mix2 = dot_nt(grad, wout[span, :])
            for half in range(2):
                at = (pair * 2 + half) * LANES
                cut = slice(half * LANES, (half + 1) * LANES)
                q_gain, k_gain = gains[0:1, at : at + LANES], gains[1:2, at : at + LANES]
                q_inv, q_norm = head_norm(q2[:, cut])
                k_inv, k_norm = head_norm(k2[:, cut])
                q = turn(q_norm * (q_gain * (SCALE * LOG2E)), c, s).astype(BF)
                k = turn(k_norm * k_gain, c, s).astype(BF)
                v = v2[:, cut]
                powered, inverse = softmax_parts(q, k)
                low = powered.astype(BF)
                mixed = dot(low, v) * inverse
                d_mix = d_mix2[:, cut] * inverse
                d_mix = d_mix.astype(BF)
                taken = jnp.sum(d_mix.astype(F32) * mixed, axis=-1, keepdims=True)
                d_v = dot_tn(low, d_mix)
                d_scores = (powered * (dot_nt(d_mix, v) - taken)).astype(BF)
                d_q = turn_back(dot(d_scores, k) * SCALE, c, s)
                d_k = turn_back(dot_tn(d_scores, q) * (1.0 / LOG2E), c, s)
                gacc[0:1, at : at + LANES] += column_sum(d_q * q_norm)
                gacc[1:2, at : at + LANES] += column_sum(d_k * k_norm)
                d_q = d_q * q_gain
                d_k = d_k * k_gain
                d_q = q_inv * (d_q - q_norm * (jnp.sum(d_q * q_norm, axis=-1, keepdims=True) * (1.0 / HEAD_DIM)))
                d_k = k_inv * (d_k - k_norm * (jnp.sum(d_k * k_norm, axis=-1, keepdims=True) * (1.0 / HEAD_DIM)))
                dqkv_st[:, at : at + LANES] = d_q.astype(BF)
                dqkv_st[:, lanes_all + at : lanes_all + at + LANES] = d_k.astype(BF)
                dqkv_st[:, 2 * lanes_all + at : 2 * lanes_all + at + LANES] = d_v.astype(BF)
        for at, size in wide:
            span = pl.ds(at, size)
            total = dot(dqkv_st[:, 0:lanes_all], wqkv[0, :, span])
            total += dot(dqkv_st[:, lanes_all : 2 * lanes_all], wqkv[1, :, span])
            total += dot(dqkv_st[:, 2 * lanes_all : 3 * lanes_all], wqkv[2, :, span])
            scatter_put(3, n, at, size, total)
        scatter_start(3, n)
        out_copy(7, n).start()
        out_copy(3, n).start()
        gather_drain(3, dattn, n)

    def block_grad_out(n):
        d_a1 = scatter_end(3, n)
        grad, d_shift, d_scale = norm_back(xin[n].astype(F32), d_a1, mod_row(n, 1))
        grad = grad + dxout[n]
        dxout[n] = grad
        dmod[n, 0:1, :] = d_shift
        dmod[n, 1:2, :] = d_scale

        @pl.when(dec)
        def _():
            xin[n] = grad.astype(BF)
            dz_copy(n).start()

        @pl.when(enc)
        def _():
            send_dmod(n)

    works = (
        attn_in,
        attn_relay,
        attn_compute,
        lambda n: scatter_middle(0, n),
        ffn_in,
        lambda n: gather_relay(1, a2f, n),
        ffn_compute,
        lambda n: scatter_middle(1, n),
        block_out,
        ffn_grad_in,
        lambda n: gather_relay(2, dffn, n),
        ffn_grad_compute,
        lambda n: scatter_middle(2, n),
        attn_grad_in,
        lambda n: gather_relay(3, dattn, n),
        attn_grad_compute,
        lambda n: scatter_middle(3, n),
        block_grad_out,
        pass_on,
    )

    def run_work(work, n, low, high):
        if high - low == 1:
            works[low](n)
            return
        middle = (low + high) // 2

        @pl.when(work < middle)
        def _():
            run_work(work, n, low, middle)

        @pl.when(work >= middle)
        def _():
            run_work(work, n, middle, high)

    base = len(works) * images
    tables = [order_words(order, base) for order in ORDERS]

    def entry_of(i):
        rest, values = i, [low + section * (high - low) for low, high in zip(*tables)]
        while len(values) > 1:
            bit, rest = lax.rem(rest, 2), lax.div(rest, 2)
            values = [low + bit * (high - low) for low, high in zip(values[0::2], values[1::2])]
        return values[0]

    def word_step(i, carry):
        def work_step(_, word):
            entry, word = lax.rem(word, base), lax.div(word, base)
            work, n = lax.div(entry, images), lax.rem(entry, images)
            run_work(work, n, 0, len(works))
            return word

        lax.fori_loop(0, PACK, work_step, entry_of(i))
        return carry

    lax.fori_loop(0, base // PACK, word_step, 0)

    for which in (4, 5, 6, 7):
        out_copy(which, images - 1).wait()

    def drain(n, carry):
        for which in (0, 1, 2, 3):
            out_copy(which, n).wait()
        part = dmod[n, :, its_tiles(me)]
        for k in range(3):
            dmod_copy(k, n).wait()
            part += mod_recv[k, n]
        for j in range(8):
            mod[j, pl.ds(n, 1), 0 : 3 * LANES] = part[j : j + 1]

        @pl.when(enc)
        def _():
            z_copy(n).wait_send()

        @pl.when(dec)
        def _():
            dz_copy(n).wait_send()

        return carry

    lax.fori_loop(0, images, drain, 0)
    dmod_part[...] = mod[0:6, :, 0 : 3 * LANES].astype(BF)


def run_main(tok, vel, mod_cols, places, angles, qkv, out, wgu, wdn, q_gain, k_gain, select):
    images, rows, width = tok.shape
    tokens = 4 * rows
    lanes_all = select.shape[1]
    heads = lanes_all // LANES
    hidden = wdn.shape[0]
    vmem = pl.BlockSpec(memory_space=pltpu.VMEM)
    anywhere = pl.BlockSpec(memory_space=pl.ANY)

    def hbm(last):
        return jax.ShapeDtypeStruct((images, tokens, last), BF)

    out_shape = (
        jax.ShapeDtypeStruct((images, rows, width), BF),
        jax.ShapeDtypeStruct((images, rows, width), F32),
        jax.ShapeDtypeStruct((6, images, 3 * LANES), BF),
        jax.ShapeDtypeStruct((8, lanes_all), F32),
        jax.ShapeDtypeStruct((8, width), F32),
        hbm(width),
        hbm(width),
        hbm(width),
        hbm(width),
        hbm(hidden),
        hbm(lanes_all),
        hbm(2 * hidden),
        hbm(3 * lanes_all),
    )
    scratch = [
        pltpu.VMEM((images, tokens, 2 * LANES), F32),
        pltpu.VMEM((3, lanes_all, width), BF),
        pltpu.VMEM((lanes_all, width), BF),
        pltpu.VMEM(wgu.shape, BF),
        pltpu.VMEM(wdn.shape, BF),
        pltpu.VMEM((8, lanes_all), F32),
        pltpu.VMEM((images, rows, width), BF),
        pltpu.VMEM((images, rows, width), BF),
        pltpu.VMEM((images, tokens, width), BF),
        pltpu.VMEM((images, tokens, width), BF),
        pltpu.VMEM((images, tokens, width), BF),
        pltpu.VMEM((images, tokens, width), BF),
        pltpu.VMEM((images, rows, width), F32),
        pltpu.VMEM((images, rows, width), BF),
        pltpu.VMEM((images, rows, width), BF),
        pltpu.VMEM((4, KEEP, 2 * rows, width), F32),
        pltpu.VMEM((4, KEEP, 2 * rows, width), BF),
        pltpu.VMEM((4, SLOTS, 2 * rows, width), BF),
        pltpu.VMEM((4, KEEP, rows, width), BF),
        pltpu.VMEM((4, SLOTS, rows, width), BF),
        pltpu.VMEM((tokens, lanes_all), BF),
        pltpu.VMEM((tokens, hidden), BF),
        pltpu.VMEM((tokens, 2 * hidden), BF),
        pltpu.VMEM((tokens, 3 * lanes_all), BF),
        pltpu.VMEM((images, 8, width), F32),
        pltpu.VMEM((3, images, 8, 3 * LANES), F32),
        pltpu.VMEM((images, 8, width), F32),
        pltpu.SemaphoreType.DMA((2, 3)),
        pltpu.SemaphoreType.DMA((2, 3, images)),
        pltpu.SemaphoreType.DMA((4, 6, images)),
        pltpu.SemaphoreType.DMA((4, 4, images)),
        pltpu.SemaphoreType.DMA((8, images)),
        pltpu.SemaphoreType.DMA((8, images)),
        pltpu.SemaphoreType.DMA((12,)),
    ]
    return pl.pallas_call(
        functools.partial(main_kernel, images, heads),
        out_shape=out_shape,
        in_specs=[anywhere, anywhere] + [vmem] * 3 + [anywhere] * 4 + [vmem] * 3,
        out_specs=[vmem] * 5 + [anywhere] * 8,
        scratch_shapes=scratch,
        compiler_params=pltpu.CompilerParams(
            collective_id=0, has_side_effects=True, vmem_limit_bytes=63 * 2**20
        ),
    )(tok, vel, mod_cols, places, angles, qkv, out, wgu, wdn, q_gain, k_gain, select)


def flat_plan(width, hidden, part):
    blocks = width // LANES
    segments = ((2 * hidden // LANES, width), (blocks, hidden), (blocks, 3 * part), (blocks, part))
    halves = [count * rows // 2 for count, rows in segments]
    half, chunk = sum(halves), width // 2
    assert half % chunk == 0

    def pieces(segment, block):
        rows, cut, at = segments[segment][1], halves[segment], sum(halves[:segment])
        low, high = block * rows, (block + 1) * rows
        if high <= cut:
            return [(at + low, 0, rows)]
        if low >= cut:
            return [(half + at + low - cut, 0, rows)]
        return [(at + low, 0, cut - low), (half + at, cut - low, high - cut)]

    return half, chunk, pieces


def tail_kernel(
    dp,
    a2_hbm,
    dgu_hbm,
    hid_hbm,
    dffn_hbm,
    a1_hbm,
    dqkv_hbm,
    mix_hbm,
    dattn_hbm,
    mod_hbm,
    pick,
    cond,
    squares,
    silu,
    dmod_low,
    gain_sums,
    labels,
    totals,
    dmod_all,
    sum_all,
    extra_all,
    left_a,
    right_a,
    left_b,
    right_b,
    turned,
    own,
    arrived,
    mod_w,
    summand,
    sum_st,
    sum_recv,
    load_sems,
    part_sems,
    total_sems,
    sum_sems,
    all_sems,
    x_part_sems,
    x_total_sems,
    here,
):
    section = lax.axis_index("section")
    place = lax.axis_index("dp")
    me = lax.axis_index("tensor")
    sib = me + 1 - 2 * lax.rem(me, 2)
    across = lax.rem(me + 2, 4)
    enc, dec = section == 0, section == 1
    width, hidden = left_a.shape[1], left_b.shape[1]
    part, lanes_all = pick.shape
    half, chunk, pieces = flat_plan(width, hidden, part)
    whole = half // chunk
    count = jnp.where(enc, whole - LENT, whole + LENT)

    tokens, ahead = left_a.shape[0], 2 * LANES
    quarter = tokens // 4

    def some_rows(i):
        rows = pl.ds(i * quarter, quarter)
        return a2_hbm.at[rows], left_a.at[rows]

    def some_columns(at, size):
        cols = pl.ds(at, size)
        return dgu_hbm.at[:, cols], right_a.at[:, cols]

    loads = [
        pltpu.make_async_copy(src, dst, load_sems.at[i])
        for i, (src, dst) in enumerate(
            (
                some_rows(0),
                some_rows(1),
                some_rows(2),
                some_rows(3),
                some_columns(0, ahead),
                some_columns(hidden, ahead),
                some_columns(ahead, hidden - ahead),
                some_columns(hidden + ahead, hidden - ahead),
                (hid_hbm, left_b),
                (dffn_hbm, right_b),
                (mix_hbm, left_b.at[:, pl.ds(0, lanes_all)]),
                (a1_hbm, left_a),
                (dqkv_hbm, right_a),
                (dattn_hbm, right_b),
            )
        )
    ]
    for i in range(10):
        loads[i].start()

    mine = pl.ds(pl.multiple_of(me * (part - 2 * LANES), 16), part)
    mod_loads = [pltpu.make_async_copy(mod_hbm.at[j], mod_w.at[j, mine], load_sems.at[14 + j]) for j in range(6)]
    barrier = pltpu.get_barrier_semaphore()
    for where in ({"tensor": sib}, {"tensor": across}):
        pl.semaphore_signal(barrier, inc=1, device_id=where, device_id_type=MESH)

    @pl.when(dec)
    def _():
        pl.semaphore_signal(barrier, inc=1, device_id={"section": 0}, device_id_type=MESH)

    for k in range(1, dp):
        pl.semaphore_signal(barrier, inc=1, device_id={"dp": lax.rem(place + k, dp)}, device_id_type=MESH)

    def put(segment, block, first, value):
        for at, low, size in pieces(segment, block):
            begin, end = max(low, first), min(low + size, first + value.shape[0])
            if begin < end:
                own[at + begin - low : at + end - low, :] = value[begin - first : end - first].astype(BF)

    def put_wide(segment, block, first, value):
        for i in range(value.shape[1] // LANES):
            put(segment, block + i, first, value[:, i * LANES : (i + 1) * LANES])

    def turn_left(ref, first, last):
        cols = ref.shape[1]
        for at in range(first, last, 256):
            turned[0:cols, at : at + 256] = ref[at : at + 256, :].T

    def gate_up_blocks(*blocks):
        for block in blocks:
            value = dot(turned[...], right_a[:, block * LANES : (block + 2) * LANES])
            put_wide(0, block, 0, value)

    def qkv_heads(*pairs):
        kept = 2 * HEAD_DIM
        for pair in pairs:
            value = dot_tn(right_a[:, pair * 2 * LANES : (pair + 1) * 2 * LANES], left_a[...]).astype(BF)
            put_wide(2, 0, pair * kept, dot(pick[0:kept, 0 : 2 * LANES], value))

    def portion(i):
        tiles, gu_half = width // LANES, hidden // LANES
        pairs = 3 * lanes_all // (2 * LANES)
        if i == 0:
            for k in range(4):
                loads[k].wait()
                turn_left(left_a, k * quarter, (k + 1) * quarter)
            loads[11].start()
            loads[4].wait()
            gate_up_blocks(0)
            loads[5].wait()
            gate_up_blocks(gu_half)
        elif i == 1:
            loads[6].wait()
            gate_up_blocks(2)
        elif i == 2:
            loads[7].wait()
            gate_up_blocks(gu_half + 2)
        elif i == 3:
            gate_up_blocks(*range(4, gu_half, 2))
        elif i == 4:
            gate_up_blocks(*range(gu_half + 4, 2 * gu_half, 2))
            loads[12].start()
            mod_w[...] = jnp.zeros_like(mod_w)
            for copy in mod_loads:
                copy.start()
        elif i in (5, 6):
            if i == 5:
                loads[8].wait()
                turn_left(left_b, 0, tokens)
                loads[10].start()
                loads[9].wait()
            split = tiles // 4 * 2
            for block in range(0, split, 2) if i == 5 else range(split, tiles, 2):
                cut = slice(block * LANES, min(width, (block + 2) * LANES))
                put_wide(1, block, 0, dot(turned[0:hidden, :], right_b[:, cut]))
            if i == 6:
                loads[13].start()
        elif i in (7, 8, 9):
            if i == 7:
                loads[11].wait()
                loads[12].wait()
            third = -(-pairs // 3)
            qkv_heads(*range((i - 7) * third, min(pairs, (i - 6) * third)))
        elif i == 10:
            loads[10].wait()
            loads[13].wait()
            value = dot(pick[...], dot_tn(left_b[:, 0:lanes_all], right_b[...]).astype(BF))
            put_wide(3, 0, 0, value)

    def along(direction, onward):
        step = 1 if (direction == 0) == onward else dp - 1
        return {"dp": lax.rem(place + step, dp)}

    def behind(direction):
        return place if direction == 0 else dp - 1 - place

    def rows_of(direction, c):
        lent = 2 * half + (direction * LENT + c - whole) * chunk
        return pl.ds(pl.multiple_of(jnp.where(c < whole, direction * half + c * chunk, lent), chunk), chunk)

    def lent_copy(ref, sems, direction, i, to_decoder):
        mine = rows_of(direction, whole - LENT + i)
        theirs = rows_of(direction, whole + i)
        return pltpu.make_async_remote_copy(
            src_ref=ref.at[mine if to_decoder else theirs],
            dst_ref=ref.at[theirs if to_decoder else mine],
            send_sem=sems.at[direction, 0, i],
            recv_sem=sems.at[direction, 1, i],
            device_id={"section": 1 if to_decoder else 0},
            device_id_type=MESH,
        )

    def lent_part(direction, i):
        return lent_copy(own, x_part_sems, direction, i, True)

    def lent_total(direction, i):
        return lent_copy(totals, x_total_sems, direction, i, False)

    def part_copy(direction, c):
        return pltpu.make_async_remote_copy(
            src_ref=own.at[rows_of(direction, c)],
            dst_ref=arrived.at[rows_of(direction, c)],
            send_sem=part_sems.at[direction, 0, c],
            recv_sem=part_sems.at[direction, 1, c],
            device_id=along(direction, True),
            device_id_type=MESH,
        )

    def total_copy(direction, c):
        return pltpu.make_async_remote_copy(
            src_ref=totals.at[rows_of(direction, c)],
            dst_ref=totals.at[rows_of(direction, c)],
            send_sem=total_sems.at[direction, 0, c],
            recv_sem=total_sems.at[direction, 1, c],
            device_id=along(direction, False),
            device_id_type=MESH,
        )

    def add_part(direction, c):
        begins, ends = behind(direction) == 0, behind(direction) == dp - 1
        rows = rows_of(direction, c)

        @pl.when(c >= whole)
        def _():
            lent_part(direction, c - whole).wait_recv()

        @pl.when(begins)
        def _():
            part_copy(direction, c).start()

        @pl.when(jnp.logical_not(begins))
        def _():
            part_copy(direction, c).wait_recv()
            value = (own[rows, :].astype(F32) + arrived[rows, :].astype(F32)).astype(BF)

            @pl.when(ends)
            def _():
                totals[rows, :] = value
                total_copy(direction, c).start()

            @pl.when(jnp.logical_not(ends))
            def _():
                own[rows, :] = value
                part_copy(direction, c).start()

    def pass_total(direction, c):
        begins, ends = behind(direction) == 0, behind(direction) == dp - 1
        passes = jnp.logical_not(begins) & jnp.logical_not(ends)
        back = c >= whole

        @pl.when(passes | (back & jnp.logical_not(ends)))
        def _():
            total_copy(direction, c).wait_recv()

        @pl.when(passes)
        def _():
            total_copy(direction, c).start()

        @pl.when(back)
        def _():
            lent_total(direction, c - whole).start()

    skew = 2

    def chunk_step(step):
        for direction in range(2):
            c = step - skew * behind(direction)

            @pl.when((c >= 0) & (c < count))
            def _():
                add_part(direction, c)

        for direction in range(2):
            u = step - skew * (2 * (dp - 1) - behind(direction))

            @pl.when((u >= 0) & (u < count))
            def _():
                pass_total(direction, u)

        for i in range(4):

            @pl.when(step == jnp.where(enc, 12, 22) + i)
            def _():
                small(i)

        for k in range(1, dp):

            @pl.when(step == jnp.where(enc, 15, 25) + 2 * k)
            def _():
                hop(k)

    def sum_copy(which):
        where = ({"section": 1 - section}, {"tensor": sib}, {"tensor": across})[which]
        height = (8, 16, 16)[which]
        src = summand if which == 0 else sum_st.at[which - 1]
        return pltpu.make_async_remote_copy(
            src_ref=src.at[pl.ds(0, height)],
            dst_ref=sum_recv.at[which, pl.ds(0, height)],
            send_sem=sum_sems.at[which, 0],
            recv_sem=sum_sems.at[which, 1],
            device_id=where,
            device_id_type=MESH,
        )

    def all_copy(which, direction, slot):
        ref = (dmod_all, sum_all, extra_all)[which]
        return pltpu.make_async_remote_copy(
            src_ref=ref.at[slot],
            dst_ref=ref.at[slot],
            send_sem=all_sems.at[which, direction, slot],
            recv_sem=all_sems.at[which, 2, slot],
            device_id=along(direction, True),
            device_id_type=MESH,
        )

    def hop(k):
        for direction in range(2):
            slot = place - k if direction == 0 else place + k
            there = (slot >= 0) & (slot < dp)

            @pl.when(there)
            def _():
                for which in range(3):
                    if k > 0:
                        all_copy(which, direction, slot).wait_recv()

            @pl.when(there & (behind(direction) < dp - 1))
            def _():
                for which in range(3):
                    all_copy(which, direction, slot).start()

    def small(step):
        if step == 0:
            dmod_all[place] = dmod_low[...]

            for copy in mod_loads:
                copy.wait()
            images = cond.shape[0]
            grads = dmod_low[...].astype(F32)
            d_silu = dot(grads[0:images].astype(BF), mod_w[0])
            for j in range(1, 6):
                d_silu += dot(grads[j * images : (j + 1) * images].astype(BF), mod_w[j])
            sig = jax.nn.sigmoid(cond[...])
            summand[0:8, :] = d_silu * (sig + cond[...] * sig * (1.0 - sig))
            summand[8:16, :] = squares[...]

            @pl.when(dec)
            def _():
                pl.semaphore_wait(here, 1)

            sum_copy(0).start()
        elif step == 1:
            sum_copy(0).wait()
            sum_st[0] = summand[...]
            sum_st[0, 0:8, :] += sum_recv[0, 0:8, :]
            sum_copy(1).start()
        elif step == 2:
            sum_copy(1).wait()
            sum_st[1] = sum_st[0] + sum_recv[1]
            sum_copy(2).start()
        elif step == 3:
            sum_copy(2).wait()
            total = sum_st[1] + sum_recv[2]
            sum_all[place, 0:8, :] = total[0:8].astype(BF)
            sum_all[place, 8:16, :] = silu[...]
            square = total[8:16, 0:LANES]
            for i in range(1, width // LANES):
                square += total[8:16, i * LANES : (i + 1) * LANES]
            extra_all[place, 0:8, :] = gain_sums[...]
            extra_all[place, 8:16, :] = jnp.zeros_like(gain_sums)
            extra_all[place, 8:16, 0:LANES] = square
            for i in range(8):
                extra_all[place, 8 + i : 9 + i, LANES : 2 * LANES] = jnp.full((1, LANES), labels[i].astype(F32))
            hop(0)

    portion(0)
    pl.semaphore_wait(barrier, jnp.where(enc, dp + 2, dp + 1))

    @pl.when(enc)
    def _():
        pl.semaphore_signal(here, inc=1, device_id={"section": 1}, device_id_type=MESH)

    for step in range(10):
        chunk_step(step)
        portion(step + 1)

    def lend(i, carry):
        for direction in range(2):
            lent_part(direction, i).start()
        return carry

    @pl.when(enc)
    def _():
        lax.fori_loop(0, LENT, lend, 0)

    def later_step(step, carry):
        chunk_step(step)
        return carry

    lax.fori_loop(10, whole + LENT + 2 * skew * (dp - 1), later_step, 0)

    def lent_back(i, carry):
        for direction in range(2):

            @pl.when(enc)
            def _():
                lent_part(direction, i).wait_send()
                lent_total(direction, i).wait_recv()

            @pl.when(dec)
            def _():
                lent_total(direction, i).wait_send()

        return carry

    lax.fori_loop(0, LENT, lent_back, 0)

    for k in range(dp):
        for direction in range(2):
            slot = place - k if direction == 0 else place + k

            @pl.when((slot >= 0) & (slot < dp) & (behind(direction) < dp - 1))
            def _():
                for which in range(3):
                    all_copy(which, direction, slot).wait_send()

    def drain(c, carry):
        for direction in range(2):

            @pl.when(behind(direction) != dp - 1)
            def _():
                part_copy(direction, c).wait_send()

            @pl.when(behind(direction) != 0)
            def _():
                total_copy(direction, c).wait_send()

            @pl.when((behind(direction) == 0) & (c < whole))
            def _():
                total_copy(direction, c).wait_recv()

        return carry

    lax.fori_loop(0, count, drain, 0)


def run_tail(dp, a2, dgu, hid, dffn, a1, dqkv, mix, dattn, mod_w, pick, cond, squares, silu, dmod_low, gain_sums, labels):
    tokens, width = a2.shape
    hidden = hid.shape[1]
    vmem = pl.BlockSpec(memory_space=pltpu.VMEM)
    anywhere = pl.BlockSpec(memory_space=pl.ANY)
    half, chunk, _ = flat_plan(width, hidden, pick.shape[0])
    flat_rows, chunks = 2 * (half + LENT * chunk), half // chunk + LENT
    return pl.pallas_call(
        functools.partial(tail_kernel, dp),
        out_shape=(
            jax.ShapeDtypeStruct((flat_rows, LANES), BF),
            jax.ShapeDtypeStruct((dp,) + dmod_low.shape, BF),
            jax.ShapeDtypeStruct((dp, 16, width), BF),
            jax.ShapeDtypeStruct((dp, 16, gain_sums.shape[1]), F32),
        ),
        in_specs=[anywhere] * 9 + [vmem] * 6 + [pl.BlockSpec(memory_space=pltpu.SMEM)],
        out_specs=[vmem] * 4,
        scratch_shapes=[
            pltpu.VMEM((tokens, width), BF),
            pltpu.VMEM((tokens, dgu.shape[1]), BF),
            pltpu.VMEM((tokens, hidden), BF),
            pltpu.VMEM((tokens, width), BF),
            pltpu.VMEM((width, tokens), BF),
            pltpu.VMEM((flat_rows, LANES), BF),
            pltpu.VMEM((flat_rows, LANES), BF),
            pltpu.VMEM((6, 3 * LANES, width), BF),
            pltpu.VMEM((16, width), F32),
            pltpu.VMEM((2, 16, width), F32),
            pltpu.VMEM((3, 16, width), F32),
            pltpu.SemaphoreType.DMA((20,)),
            pltpu.SemaphoreType.DMA((2, 2, chunks)),
            pltpu.SemaphoreType.DMA((2, 2, chunks)),
            pltpu.SemaphoreType.DMA((3, 2)),
            pltpu.SemaphoreType.DMA((3, 3, dp)),
            pltpu.SemaphoreType.DMA((2, 2, LENT)),
            pltpu.SemaphoreType.DMA((2, 2, LENT)),
            pltpu.SemaphoreType.REGULAR,
        ],
        compiler_params=pltpu.CompilerParams(
            collective_id=1, has_side_effects=True, vmem_limit_bytes=62 * 2**20
        ),
    )(a2, dgu, hid, dffn, a1, dqkv, mix, dattn, mod_w, pick, cond, squares, silu, dmod_low, gain_sums, labels)


def finish_kernel(
    count,
    flat_hbm,
    z_hbm,
    dx_hbm,
    dmod_all,
    sum_all,
    extra_all,
    select,
    gu_hbm,
    down_hbm,
    qkv_hbm,
    out_hbm,
    z_out,
    dx_out,
    mod_hbm,
    class_hbm,
    q_gain_out,
    k_gain_out,
    stats_out,
    flat,
    gate_up,
    down,
    qkv,
    out,
    mod,
    classes,
    z_rows,
    dx_rows,
    load_sems,
    store_sems,
):
    width, hidden = gate_up.shape[1], gate_up.shape[2]
    part, blocks, hidden_blocks = out.shape[0], width // LANES, hidden // LANES
    _, _, pieces = flat_plan(width, hidden, part)
    groups = (
        [(0, b) for b in range(hidden_blocks)],
        [(0, hidden_blocks + b) for b in range(hidden_blocks)],
        [(1, b) for b in range(blocks)],
        [(2, b) for b in range(blocks)],
        [(3, b) for b in range(blocks)],
    )
    loads = []
    for group in groups:
        spans = []
        for segment, block in group:
            for at, _, size in pieces(segment, block):
                if spans and spans[-1][0] + spans[-1][1] == at:
                    spans[-1][1] += size
                else:
                    spans.append([at, size])
        copies = []
        for at, size in spans:
            rows = pl.ds(at, size)
            sem = load_sems.at[len(loads), len(copies)]
            copies.append(pltpu.make_async_copy(flat_hbm.at[rows], flat.at[rows], sem))
            copies[-1].start()
        loads.append(copies)
    inward = (
        pltpu.make_async_copy(z_hbm, z_rows, load_sems.at[0, 2]),
        pltpu.make_async_copy(dx_hbm, dx_rows, load_sems.at[1, 2]),
    )
    outward = (
        pltpu.make_async_copy(z_rows, z_out, store_sems.at[5]),
        pltpu.make_async_copy(dx_rows, dx_out, store_sems.at[6]),
    )
    for copy in inward:
        copy.start()

    dp, images = dmod_all.shape[0], dmod_all.shape[1] // 6
    me = lax.axis_index("tensor")
    silu = jnp.concatenate([sum_all[p].astype(F32)[8:16] for p in range(dp)], axis=0).astype(BF)
    grad_cond = jnp.concatenate([sum_all[p].astype(F32)[0:8] for p in range(dp)], axis=0).astype(BF)
    dmods = [dmod_all[p].astype(F32) for p in range(dp)]
    mod_stores = []
    for j in range(6):
        grads = jnp.concatenate([dmods[p][j * images : (j + 1) * images] for p in range(dp)], axis=0).astype(BF)
        mod[j] = dot_tn(grads, silu)
        mine = pl.ds(pl.multiple_of(me * (part - 2 * LANES), 8), part)
        mod_stores.append(pltpu.make_async_copy(mod.at[j, mine], mod_hbm.at[j], store_sems.at[8 + j]))
        mod_stores[-1].start()
    labels = jnp.concatenate([extra_all[p, 8:16, LANES : LANES + 1] for p in range(dp)], axis=0)
    lanes = lax.broadcasted_iota(jnp.int32, (dp * images, classes.shape[0]), 1)
    one_hot = jnp.where(lanes == labels.astype(jnp.int32), 1.0, 0.0).astype(BF)
    for at, size in chunks_of(width, 384):
        classes[:, at : at + size] = dot_tn(one_hot, grad_cond[:, at : at + size])
    class_store = pltpu.make_async_copy(classes.at[pl.ds(0, class_hbm.shape[0])], class_hbm, store_sems.at[7])
    class_store.start()

    for i in range(2):
        inward[i].wait()
        outward[i].start()

    gain_sum, squares = extra_all[0, 0:8, :], extra_all[0, 8:16, 0:LANES]
    for p in range(1, dp):
        gain_sum += extra_all[p, 0:8, :]
        squares += extra_all[p, 8:16, 0:LANES]
    gain_sum = lax.dot_general(
        gain_sum,
        select[...].astype(F32),
        (((1,), (1,)), ((), ())),
        precision=lax.Precision.HIGHEST,
        preferred_element_type=F32,
    )
    q_gain_out[...] = gain_sum[0:1]
    k_gain_out[...] = gain_sum[1:2]
    for i in range(3):
        stats_out[0:1, i : i + 1] = jnp.sqrt(jnp.sum(squares[i : i + 1], axis=1, keepdims=True) * (1.0 / count))

    stores = (
        pltpu.make_async_copy(gate_up.at[0], gu_hbm.at[0], store_sems.at[0]),
        pltpu.make_async_copy(gate_up.at[1], gu_hbm.at[1], store_sems.at[1]),
        pltpu.make_async_copy(down, down_hbm, store_sems.at[2]),
        pltpu.make_async_copy(qkv, qkv_hbm, store_sems.at[3]),
        pltpu.make_async_copy(out, out_hbm, store_sems.at[4]),
    )
    for i, group in enumerate(groups):
        for copy in loads[i]:
            copy.wait()
        for segment, block in group:
            for at, low, size in pieces(segment, block):
                value = flat[at : at + size, :].astype(F32)
                rows = slice(low, low + size)
                cols = slice(block * LANES, (block + 1) * LANES)
                if segment == 0:
                    local = block % hidden_blocks
                    gate_up[block // hidden_blocks, rows, local * LANES : (local + 1) * LANES] = value
                elif segment == 1:
                    down[rows, cols] = value
                elif segment == 2:
                    qkv[rows, cols] = value
                else:
                    out[rows, cols] = value
        stores[i].start()
    for copy in (*stores, *outward, *mod_stores, class_store):
        copy.wait()


def run_finish(count, class_count, hidden, flat, z_rows, dx_rows, dmod_all, sum_all, extra_all, select):
    part, width = select.shape[0], sum_all.shape[2]
    vmem = pl.BlockSpec(memory_space=pltpu.VMEM)
    anywhere = pl.BlockSpec(memory_space=pl.ANY)
    shapes = ((2, width, hidden), (hidden, width), (3 * part, width), (part, width))
    return pl.pallas_call(
        functools.partial(finish_kernel, count),
        out_shape=tuple(jax.ShapeDtypeStruct(shape, F32) for shape in shapes)
        + (
            jax.ShapeDtypeStruct(z_rows.shape, BF),
            jax.ShapeDtypeStruct(dx_rows.shape, F32),
            jax.ShapeDtypeStruct((6, part, width), F32),
            jax.ShapeDtypeStruct((class_count, width), F32),
            jax.ShapeDtypeStruct((1, part), F32),
            jax.ShapeDtypeStruct((1, part), F32),
            jax.ShapeDtypeStruct((1, 3), F32),
        ),
        in_specs=[anywhere] * 3 + [vmem] * 4,
        out_specs=[anywhere] * 8 + [vmem] * 3,
        scratch_shapes=[pltpu.VMEM(flat.shape, BF)]
        + [pltpu.VMEM(shape, F32) for shape in shapes]
        + [
            pltpu.VMEM((6, 3 * LANES, width), F32),
            pltpu.VMEM((-(-class_count // LANES) * LANES, width), F32),
            pltpu.VMEM(z_rows.shape, BF),
            pltpu.VMEM(dx_rows.shape, F32),
            pltpu.SemaphoreType.DMA((5, 3)),
            pltpu.SemaphoreType.DMA((14,)),
        ],
        compiler_params=pltpu.CompilerParams(vmem_limit_bytes=60 * 2**20),
    )(flat, z_rows, dx_rows, dmod_all, sum_all, extra_all, select)


def time_embed(bin_row, feature_count):
    halfway = feature_count // 2
    frequency = jnp.exp(-math.log(10000.0) * jnp.arange(halfway, dtype=F32) / halfway)
    moment = (bin_row.astype(F32) + 0.5) * (1000.0 / NBINS)
    angles = moment[:, None] * frequency[None, :]
    return jnp.concatenate([jnp.cos(angles), jnp.sin(angles)], axis=-1)


def per_device(
    tokens,
    velocity_grad,
    bins,
    labels,
    places,
    class_table,
    mod_weight,
    qkv_weight,
    out_weight,
    gate_up_weight,
    down_weight,
    q_gain,
    k_gain,
):
    micro, per_micro, rows, width = tokens.shape
    images = micro * per_micro
    dp = lax.axis_size("dp")
    me = lax.axis_index("tensor")
    heads = q_gain.shape[1] // HEAD_DIM
    select = jnp.asarray(head_select(heads), BF)

    label_row = labels.reshape(images)
    one_hot = label_row[:, None] == jnp.arange(class_table.shape[0], dtype=jnp.int32)[None, :]
    picked = jnp.dot(one_hot.astype(BF), class_table, preferred_element_type=F32)
    cond = time_embed(bins.reshape(images), width) + picked
    silu_low = jax.nn.silu(cond).astype(BF)
    mod_w = mod_weight[0]
    part = width // 4
    columns = jnp.einsum("id,djf->ijf", silu_low, mod_w, preferred_element_type=F32)
    shift = me * (part - 2 * LANES)
    mod_cols = lax.dynamic_update_slice(jnp.zeros((images, 8, 3 * LANES), F32), columns, (0, 0, shift))

    table, table_parts = angle_table(), []
    for _ in range(3):
        table_parts.append(table.astype(BF))
        table = table - table_parts[-1].astype(np.float32)
    table_parts.append(np.zeros((LANES - 6 * GRID, 2 * LANES), BF))

    results = run_main(
        tokens.reshape(images, rows, width),
        velocity_grad.reshape(images, rows, width),
        mod_cols,
        places,
        jnp.asarray(np.concatenate(table_parts)),
        jnp.transpose(qkv_weight[0], (0, 2, 1)),
        out_weight[0],
        gate_up_weight[0],
        down_weight[0],
        q_gain,
        k_gain,
        select,
    )
    z_rows, dx_rows, dmod_part, gain_sums, squares, a1, a2, d_ffn, d_attn, units, mixed, d_gu, d_qkv = results

    lanes_all = heads * LANES
    flat = images * 4 * rows
    flat_grads, dmod_all, sum_all, extra_all = run_tail(
        dp,
        a2.reshape(flat, width),
        d_gu.reshape(flat, d_gu.shape[2]),
        units.reshape(flat, units.shape[2]),
        d_ffn.reshape(flat, width),
        a1.reshape(flat, width),
        d_qkv.reshape(flat, d_qkv.shape[2]),
        mixed.reshape(flat, lanes_all),
        d_attn.reshape(flat, width),
        jnp.transpose(mod_w, (1, 2, 0)),
        select,
        cond,
        squares,
        silu_low,
        dmod_part.reshape(6 * images, 3 * LANES),
        gain_sums,
        label_row,
    )
    count = images * rows * width * dp * lax.axis_size("tensor")
    finished = run_finish(
        count,
        class_table.shape[0],
        units.shape[2],
        flat_grads,
        z_rows,
        dx_rows,
        dmod_all,
        sum_all,
        extra_all,
        select,
    )
    gate_up_grad, down_grad, qkv_grad, out_grad, z_out, dx_out, mod_grad, class_grad, q_grad, k_grad, stats = finished
    whole = (1, micro, per_micro, rows, width)
    return (
        z_out.reshape(whole),
        dx_out.reshape(whole),
        jnp.transpose(mod_grad, (2, 0, 1))[None],
        jnp.transpose(qkv_grad.reshape(3, part, width), (0, 2, 1))[None],
        out_grad[None],
        gate_up_grad[None],
        down_grad[None],
        q_grad,
        k_grad,
        class_grad,
        stats,
    )


def solution(mesh):
    return jax.shard_map(
        per_device,
        mesh=mesh,
        in_specs=(
            P(None, "dp", "tensor", None),
            P(None, "dp", "tensor", None),
            P(None, "dp"),
            P(None, "dp"),
            P(None, "dp", None),
            P(),
            P("section", None, None, "tensor"),
            P("section", None, None, "tensor"),
            P("section", "tensor", None),
            P("section", None, None, "tensor"),
            P("section", "tensor", None),
            P("section", "tensor"),
            P("section", "tensor"),
        ),
        out_specs=(
            P("section", None, "dp", "tensor", None),
            P("section", None, "dp", "tensor", None),
            P("section", None, None, "tensor"),
            P("section", None, None, "tensor"),
            P("section", "tensor", None),
            P("section", None, None, "tensor"),
            P("section", "tensor", None),
            P("section", "tensor"),
            P("section", "tensor"),
            P(),
            P("section", None),
        ),
        check_vma=False,
    )
```
